32 devices in a mesh: groups: 2 (over y), row: 8 (over z, x), col: 2 (over core).
Axes of the slice: x: 2, y: 2, z: 4, core: 2. Of those that a mesh axis runs over, the one named last changes fastest.
Arguments:
- pair_rep: bfloat16 [576, 288, 128], P(('groups', 'row'), 'col'), parts along dimension 0, may hold values from -6 to 6
- slab_rep: bfloat16 [16, 288, 128], P(('groups', 'row')), parts along dimension 0, may hold values from -6 to 6
- length: int32 [2], P('groups'), parts along dimension 0, may hold values from 144 to 288
- weight_a: bfloat16 [128, 128], replicated, may hold values from -0.5 to 0.5
- gate_a: bfloat16 [128, 128], replicated, may hold values from -0.5 to 0.5
- weight_b: bfloat16 [128, 128], replicated, may hold values from -0.5 to 0.5
- gate_b: bfloat16 [128, 128], replicated, may hold values from -0.5 to 0.5
- weight_gate: bfloat16 [128, 128], replicated, may hold values from -0.5 to 0.5
- weight_out: bfloat16 [128, 128], replicated, may hold values from -0.5 to 0.5
Outputs:
- update: bfloat16 [16, 288, 128], P('groups', ('row', 'col')), parts along dimension 0
The draws below stay inside these ranges and needn't reach their ends.
There are 2 independent parts, one for each index of `groups`. The reference program is written for one: setup_inputs(seed, part) draws one part's arguments, and reference() takes and returns one part's arrays. A program takes and returns all parts, laid end to end along the dimension named above; an argument that names none is the same for every part. Nothing has to cross between parts.
Inputs may be any that keep to these rules, and one draw needn't show every extreme that they name: Positions at index length or beyond are padding.
All inputs are finite; a program needn't handle non-finite values.
Results may differ from the reference program's by a relative error of at most 0.0085.
Values may be sent and summed in bfloat16 or wider, within the bound.
No kernel may reach another device: no remote copies, remote signals or barrier semaphores. Data moves between devices by JAX's collectives and lax.ppermute only.
A program may use at most 64 MiB of HBM per device.

```python
import jax
import jax.numpy as jnp
from jax import lax

CZ = 128
CH = 128
ROWS_DEV = 36
N = 288
R = 8


def level_of(rng, extent, pieces, least, high):
    def one(dim, blocks):
        draws = jax.random.uniform(jax.random.fold_in(jax.random.fold_in(rng, 6), dim), (blocks,), jnp.float32, least / len(pieces), high / len(pieces))
        return jnp.repeat(jnp.exp(draws), extent[dim] // blocks).reshape((-1,) + (1,) * (len(extent) - dim - 1))

    level = one(*pieces[0])
    for cut in pieces[1:]:
        level = level * one(*cut)
    return level


def noise(own_key, shape, scale, reach, split=(), kind=jnp.bfloat16):
    drawn = jax.random.normal(own_key, shape, jnp.float32) * scale
    if len(split) > 0:
        drawn = level_of(own_key, shape, split, -0.22, 0.18) * drawn
    return jnp.clip(drawn, min=-reach, max=reach).astype(kind)


def setup_inputs(seed: int = 0, part: int = 0) -> dict:
    keys = jax.random.split(jax.random.key(seed), 10)
    part_keys = jax.random.split(jax.random.fold_in(keys[9], part), 10)
    pair_rep = noise(part_keys[0], (N, N, CZ), 1.0, 6.0, ((0, 8), (1, 2)))
    slab_rep = noise(part_keys[1], (R, N, CZ), 1.0, 6.0, ((0, 8),))
    length = jax.random.randint(part_keys[2], (1,), N // 2, N + 1).astype(jnp.int32)
    weight_a = noise(keys[3], (CZ, CH), CZ ** -0.5, 0.5)
    gate_a = noise(keys[4], (CZ, CH), CZ ** -0.5, 0.5)
    weight_b = noise(keys[5], (CZ, CH), CZ ** -0.5, 0.5)
    gate_b = noise(keys[6], (CZ, CH), CZ ** -0.5, 0.5)
    weight_gate = noise(keys[7], (CZ, CZ), CZ ** -0.5, 0.5)
    weight_out = noise(keys[8], (CH, CZ), CH ** -0.5, 0.5)
    return dict(pair_rep=pair_rep, slab_rep=slab_rep, length=length, weight_a=weight_a, gate_a=gate_a, weight_b=weight_b, gate_b=gate_b, weight_gate=weight_gate, weight_out=weight_out)


epsilon = 1e-05

def layer_norm(values):
    values = values.astype(jnp.float32)
    center = lax.optimization_barrier(jnp.mean(values, axis=-1, keepdims=True))
    spread = lax.optimization_barrier(jnp.mean((values - center) ** 2, axis=-1, keepdims=True))
    return (values - center) * lax.rsqrt(spread + epsilon)

def reference(pair_rep, slab_rep, length, weight_a, gate_a, weight_b, gate_b, weight_gate, weight_out):
    live_count = length[0]
    live_k = (jnp.arange(N, dtype=jnp.int32) < live_count).astype(jnp.float32)
    slab_norm = layer_norm(slab_rep).astype(jnp.bfloat16)
    left = jax.nn.sigmoid(jnp.dot(slab_norm, gate_a, preferred_element_type=jnp.float32))
    left = (left * jnp.dot(slab_norm, weight_a, preferred_element_type=jnp.float32) * live_k[None, :, None]).astype(jnp.bfloat16)
    gating = jax.nn.sigmoid(jnp.dot(slab_norm, weight_gate, preferred_element_type=jnp.float32)).astype(jnp.bfloat16)
    left_wide = left.astype(jnp.float32)

    def block_terms(block_index):
        first_row = (block_index * ROWS_DEV).astype(jnp.int32)
        rows_here = lax.dynamic_slice_in_dim(pair_rep, first_row, ROWS_DEV, 0)
        pair_norm = layer_norm(rows_here).astype(jnp.bfloat16)
        live_j = (first_row + jnp.arange(ROWS_DEV, dtype=jnp.int32) < live_count).astype(jnp.float32)
        right = jax.nn.sigmoid(jnp.dot(pair_norm, gate_b, preferred_element_type=jnp.float32))
        right = right * jnp.dot(pair_norm, weight_b, preferred_element_type=jnp.float32)
        right = (right * live_j[:, None, None] * live_k[None, :, None]).astype(jnp.bfloat16)
        return jnp.einsum('ikc,jkc->ijc', left_wide, right.astype(jnp.float32), precision=lax.Precision.HIGHEST)
    blocks = lax.map(block_terms, jnp.arange(N // ROWS_DEV, dtype=jnp.int32))
    tri = jnp.transpose(blocks, (1, 0, 2, 3)).reshape(R, N, CH)
    tri_norm = layer_norm(tri).astype(jnp.bfloat16)
    projected = jnp.dot(tri_norm, weight_out, preferred_element_type=jnp.float32)
    return (projected * gating.astype(jnp.float32)).astype(jnp.bfloat16)
```

```python
import functools

import jax
import jax.numpy as jnp
from jax import lax
from jax.experimental import pallas as pl
from jax.experimental.pallas import tpu as pltpu
from jax.sharding import PartitionSpec as P

EPS = 1e-05
F32 = jnp.float32
BF16 = jnp.bfloat16


def divisor(total, limit, step=1):
    return max(d for d in range(step, total + 1, step) if total % d == 0 and (d <= limit or d == step))


def centering(width):
    row = lax.broadcasted_iota(jnp.int32, (2 * width, 2 * width), 0)
    col = lax.broadcasted_iota(jnp.int32, (2 * width, 2 * width), 1)
    share = jnp.where((row < width) == (col < width), 1.0 / width, 0.0)
    center = jnp.where(row == col, 1.0, 0.0) - share
    return center.astype(BF16), share.astype(BF16)


def normed(x, center, share):
    half = x.shape[0] // 2
    wide = jnp.concatenate([x[:half], x[half:]], axis=1)
    d = jnp.dot(wide, center, preferred_element_type=F32)
    var = jnp.dot((d * d).astype(BF16), share, preferred_element_type=F32)
    return (d * lax.rsqrt(var + EPS)).astype(BF16)


def gated(n, both):
    width = both.shape[1] // 2
    y = jnp.dot(n, both, preferred_element_type=F32)
    value = y[:, width:]
    return value + value * jnp.tanh(y[:, :width])


def pair_weights(gate_ref, weight_ref):
    half = jnp.asarray(0.5, BF16)
    return jnp.concatenate([gate_ref[...] * half, weight_ref[...] * half], axis=1)


def right_kernel(length_ref, pair_ref, gate_ref, weight_ref, out_ref):
    rows, cols, width = pair_ref.shape
    live = length_ref[0]
    first_k = lax.axis_index("col") * cols
    first_j = lax.axis_index("row") * (rows * pl.num_programs(0)) + pl.program_id(0) * rows
    center, share = centering(width)
    both = pair_weights(gate_ref, weight_ref)
    n = normed(pair_ref[...].reshape(rows * cols, width), center, share)
    k = first_k + lax.broadcasted_iota(jnp.int32, (cols, width), 0)
    for side in range(2):
        edge = gated(n[:, side * width : (side + 1) * width], both).reshape(rows // 2, cols, width)
        for r in range(rows // 2):
            j = side * (rows // 2) + r
            reach = jnp.where(first_j + j < live, live, 0)
            out_ref[j] = jnp.where(k < reach, edge[r], 0.0).astype(BF16)


def fold(parts):
    place = lax.broadcasted_iota(jnp.int32, parts[0].shape, 0)
    for step in (1, 2, 4):
        here = (place & step) == 0
        parts = [
            jnp.where(here, a, b) + pltpu.roll(jnp.where(here, b, a), 8 - step, 0)
            for a, b in zip(parts[0::2], parts[1::2])
        ]
    return parts[0]


def tri_kernel(
    length_ref, slab_ref, right_ref, gate_ref, weight_ref, out_gate_ref, send_ref, keep_ref, left_ref, norm_ref,
    *, group,
):
    slabs, depth, width = slab_ref.shape
    block = right_ref.shape[0]
    k_step, j_step = pl.program_id(0), pl.program_id(1)
    half_steps = pl.num_programs(1) // 2
    half_rows = block * half_steps
    side = lax.axis_index("col")
    half_cols = depth * pl.num_programs(0)

    @pl.when(j_step == 0)
    def _():
        center, share = centering(width)
        both = pair_weights(gate_ref, weight_ref)
        n = normed(slab_ref[...].reshape(slabs * depth, width), center, share)
        first_k = side * half_cols + k_step * depth
        k = first_k + lax.broadcasted_iota(jnp.int32, (depth, width), 0)
        live = length_ref[0]
        for part in range(2):
            own = n[:, part * width : (part + 1) * width]
            edge = gated(own, both).reshape(slabs // 2, depth, width)
            norm_ref[pl.ds(part * (slabs // 2 * depth), slabs // 2 * depth), :] = own.astype(F32)
            for i in range(slabs // 2):
                left_ref[part * (slabs // 2) + i] = jnp.where(k < live, edge[i], 0.0).astype(BF16).astype(F32)

    first_j = lax.rem(lax.axis_index("row") * (2 * half_rows), half_cols)

    @pl.when((j_step == 0) & (k_step == first_j // depth))
    def _():
        start = lax.rem(first_j, depth)

        def gates(place, dest_ref):
            rows = [
                norm_ref[pl.ds(start + place * half_rows + j, slabs, stride=depth), :] for j in range(half_rows)
            ]
            rows = jnp.concatenate(rows, axis=0).astype(BF16)
            y = jnp.dot(rows, out_gate_ref[...] * jnp.asarray(0.5, BF16), preferred_element_type=F32)
            dest_ref[1] = (0.5 + 0.5 * jnp.tanh(y)).astype(BF16).astype(F32)

        gates(1 - side, send_ref)
        gates(side, keep_ref)

    def contract(dest_ref, first_row):
        def some_rows(turn, _):
            for i0 in range(0, slabs, 8):
                sums = [[None] * 8 for _ in range(group)]
                for k0 in range(0, depth, 16):
                    edges = [right_ref[turn * group + j, pl.ds(k0, 16), :].astype(F32) for j in range(group)]
                    for i in range(8):
                        left = left_ref[i0 + i, pl.ds(k0, 16), :]
                        for j in range(group):
                            term = left * edges[j]
                            term = term[:8] + term[8:]
                            sums[j][i] = term if k0 == 0 else sums[j][i] + term
                for j in range(group):
                    row = (first_row + turn * group + j) * slabs + i0
                    dest = dest_ref.at[0, pl.ds(pl.multiple_of(row, 8), 8), :]
                    total = fold(sums[j])
                    dest[...] = jnp.where(k_step == 0, total, total + dest[...])
            return 0

        lax.fori_loop(0, block // group, some_rows, 0)

    @pl.when(j_step < half_steps)
    def _():
        contract(send_ref, j_step * block)

    @pl.when(j_step >= half_steps)
    def _():
        contract(keep_ref, (j_step - half_steps) * block)


def last_kernel(keep_ref, got_ref, weight_ref, out_ref, done_ref, *, owner_side):
    slabs, cols, width = out_ref.shape
    tri = keep_ref[0] + got_ref[0]
    d = tri - jnp.mean(tri, axis=-1, keepdims=True)
    var = jnp.mean(d * d, axis=-1, keepdims=True)
    n = (d * lax.rsqrt(var + EPS)).astype(BF16)
    projected = jnp.dot(n, weight_ref[...], preferred_element_type=F32)
    mine = owner_side(lax.axis_index("row")) == lax.axis_index("col")
    done_ref[...] = projected * jnp.where(mine, keep_ref[1], got_ref[1])
    for i in range(slabs):
        out_ref[i] = done_ref[pl.ds(i, cols, stride=slabs), :].astype(BF16)


def gathered(half, axis):
    count = lax.axis_size(axis)
    spread = jnp.broadcast_to(half[None], (count,) + half.shape)
    return lax.all_to_all(spread, axis, split_axis=0, concat_axis=0, tiled=True)


def shards(pair_rep, slab_rep, length, weight_a, gate_a, weight_b, gate_b, weight_gate, weight_out):
    rows_dev, half_cols, width = pair_rep.shape
    hidden = weight_a.shape[1]
    count = lax.axis_size("row")
    side = lax.axis_index("col")
    half_rows = rows_dev // 2
    smem = pl.BlockSpec(memory_space=pltpu.SMEM)
    vmem = pl.BlockSpec(memory_space=pltpu.VMEM)

    half = lax.dynamic_slice_in_dim(slab_rep, side * half_cols, half_cols, 1)
    slab = gathered(half, "row").reshape(-1, half_cols, width)
    slabs = slab.shape[0]

    rows_step = divisor(rows_dev, max(2, 1728 // half_cols), 2)
    whole_weight = pl.BlockSpec((width, hidden), lambda *_: (0, 0))
    right = pl.pallas_call(
        right_kernel,
        out_shape=jax.ShapeDtypeStruct((rows_dev, half_cols, hidden), BF16),
        grid=(rows_dev // rows_step,),
        in_specs=[
            smem,
            pl.BlockSpec((rows_step, half_cols, width), lambda s: (s, 0, 0)),
            whole_weight,
            whole_weight,
        ],
        out_specs=pl.BlockSpec((rows_step, half_cols, hidden), lambda s: (s, 0, 0)),
        compiler_params=pltpu.CompilerParams(vmem_limit_bytes=40 << 20),
        cost_estimate=pl.CostEstimate(
            flops=2 * rows_dev * half_cols * width * hidden * 6,
            bytes_accessed=4 * rows_dev * half_cols * width,
            transcendentals=2 * rows_dev * half_cols * width,
        ),
        name="right",
    )(length, pair_rep, gate_b, weight_b)

    depth = divisor(half_cols, 144, rows_dev)
    j_block = half_rows
    group = 3
    tri_shape = jax.ShapeDtypeStruct((2, half_rows * slabs, hidden), F32)
    tri_spec = pl.BlockSpec((2, half_rows * slabs, hidden), lambda k, j: (0, 0, 0))
    half_steps = half_rows // j_block

    def right_block(k, j):
        flip = 1 - lax.axis_index("col")
        return (lax.rem(j + flip * half_steps, 2 * half_steps), k, 0)

    send, keep = pl.pallas_call(
        functools.partial(tri_kernel, group=group),
        out_shape=(tri_shape, tri_shape),
        grid=(half_cols // depth, 2 * half_steps),
        in_specs=[
            smem,
            pl.BlockSpec((slabs, depth, width), lambda k, j: (0, k, 0)),
            pl.BlockSpec((j_block, depth, hidden), right_block),
            whole_weight,
            whole_weight,
            whole_weight,
        ],
        out_specs=(tri_spec, tri_spec),
        scratch_shapes=[
            pltpu.VMEM((slabs, depth, hidden), F32),
            pltpu.VMEM((slabs * depth, width), F32),
        ],
        compiler_params=pltpu.CompilerParams(vmem_limit_bytes=48 << 20),
        cost_estimate=pl.CostEstimate(
            flops=2 * rows_dev * half_cols * slabs * hidden,
            bytes_accessed=2 * rows_dev * half_cols * width,
            transcendentals=slabs * half_cols * width,
        ),
        name="tri",
    )(length, slab, right, gate_a, weight_a, weight_gate)

    got = lax.ppermute(send, "col", [(0, 1), (1, 0)])

    return pl.pallas_call(
        functools.partial(last_kernel, owner_side=lambda row: (row * rows_dev) // half_cols),
        out_shape=jax.ShapeDtypeStruct((slabs, half_rows, width), BF16),
        in_specs=[vmem, vmem, vmem],
        out_specs=vmem,
        scratch_shapes=[pltpu.VMEM((half_rows * slabs, width), F32)],
        compiler_params=pltpu.CompilerParams(vmem_limit_bytes=32 << 20),
        name="last",
    )(keep, got, weight_out)


def solution(mesh):
    placed = (
        P(("groups", "row"), "col", None),
        P(("groups", "row"), None, None),
        P("groups"),
        P(),
        P(),
        P(),
        P(),
        P(),
        P(),
    )
    return jax.shard_map(
        shards,
        mesh=mesh,
        in_specs=placed,
        out_specs=P("groups", ("row", "col"), None),
        check_vma=False,
    )
```

```python
import functools

import jax
import jax.numpy as jnp
from jax import lax
from jax.experimental import pallas as pl
from jax.experimental.pallas import tpu as pltpu
from jax.sharding import PartitionSpec as P

EPS = 1e-05
F32 = jnp.float32
BF16 = jnp.bfloat16


def divisor(total, limit, step=1):
    return max(d for d in range(step, total + 1, step) if total % d == 0 and (d <= limit or d == step))


def centering(width):
    row = lax.broadcasted_iota(jnp.int32, (2 * width, 2 * width), 0)
    col = lax.broadcasted_iota(jnp.int32, (2 * width, 2 * width), 1)
    share = jnp.where((row < width) == (col < width), 1.0 / width, 0.0)
    center = jnp.where(row == col, 1.0, 0.0) - share
    return center.astype(BF16), share.astype(BF16)


def normed(first, second, center, share):
    wide = jnp.concatenate([first, second], axis=1)
    d = jnp.dot(wide, center, preferred_element_type=F32)
    var = jnp.dot((d * d).astype(BF16), share, preferred_element_type=F32)
    return (d * lax.rsqrt(var + EPS)).astype(BF16)


def gated(n, both):
    width = both.shape[1] // 2
    y = jnp.dot(n, both, preferred_element_type=F32)
    value = y[:, width:]
    return value + value * jnp.tanh(y[:, :width])


def pair_weights(gate_ref, weight_ref):
    half = jnp.asarray(0.5, BF16)
    return jnp.concatenate([gate_ref[...] * half, weight_ref[...] * half], axis=1)


def right_kernel(length_ref, pair_ref, gate_ref, weight_ref, out_ref):
    rows, cols, width = pair_ref.shape
    live = length_ref[0]
    first_k = lax.axis_index("col") * cols
    first_j = lax.axis_index("row") * (rows * pl.num_programs(0)) + pl.program_id(0) * rows
    center, share = centering(width)
    both = pair_weights(gate_ref, weight_ref)
    x = pair_ref[...].reshape(2, rows * cols // 2, width)
    n = normed(x[0], x[1], center, share)
    k = first_k + lax.broadcasted_iota(jnp.int32, (cols, width), 0)
    for side in range(2):
        edge = gated(n[:, side * width : (side + 1) * width], both).reshape(rows // 2, cols, width)
        for r in range(rows // 2):
            j = side * (rows // 2) + r
            reach = jnp.where(first_j + j < live, live, 0)
            out_ref[j] = jnp.where(k < reach, edge[r], 0.0).astype(BF16)


def fold(parts):
    place = lax.broadcasted_iota(jnp.int32, parts[0].shape, 0)
    for step in (1, 2, 4):
        here = (place & step) == 0
        parts = [
            jnp.where(here, a, b) + pltpu.roll(jnp.where(here, b, a), 8 - step, 0)
            for a, b in zip(parts[0::2], parts[1::2])
        ]
    return parts[0]


def tri_kernel(length_ref, right_ref, gate_ref, weight_ref, out_gate_ref, *refs, group):
    slab_refs, (send_ref, keep_ref, left_ref, norm_ref) = refs[:-4], refs[-4:]
    slabs = len(slab_refs)
    _, depth, width = slab_refs[0].shape
    block = right_ref.shape[0]
    k_step, j_step = pl.program_id(0), pl.program_id(1)
    half_steps = pl.num_programs(1) // 2
    half_rows = block * half_steps
    side = lax.axis_index("col")
    half_cols = depth * pl.num_programs(0)

    @pl.when(j_step == 0)
    def _():
        center, share = centering(width)
        both = pair_weights(gate_ref, weight_ref)
        first_k = side * half_cols + k_step * depth
        k = first_k + lax.broadcasted_iota(jnp.int32, (depth, width), 0)
        live = length_ref[0]
        place = lax.axis_index("row")
        for m in range(0, slabs, 2):
            pair = normed(slab_refs[m][0], slab_refs[m + 1][0], center, share)
            for part in range(2):
                i = jnp.bitwise_xor(place, m + part)
                n = pair[:, part * width : (part + 1) * width]
                norm_ref[pl.ds(pl.multiple_of(i * depth, 16), depth), :] = n.astype(F32)
                left_ref[i] = jnp.where(k < live, gated(n, both), 0.0).astype(BF16).astype(F32)

    first_j = lax.rem(lax.axis_index("row") * (2 * half_rows), half_cols)

    @pl.when((j_step == 0) & (k_step == first_j // depth))
    def _():
        start = lax.rem(first_j, depth)

        def gates(place, dest_ref):
            rows = [
                norm_ref[pl.ds(start + place * half_rows + j, slabs, stride=depth), :] for j in range(half_rows)
            ]
            rows = jnp.concatenate(rows, axis=0).astype(BF16)
            y = jnp.dot(rows, out_gate_ref[...] * jnp.asarray(0.5, BF16), preferred_element_type=F32)
            dest_ref[1] = (0.5 + 0.5 * jnp.tanh(y)).astype(BF16).astype(F32)

        gates(1 - side, send_ref)
        gates(side, keep_ref)

    def contract(dest_ref, first_row):
        def some_rows(turn, _):
            for i0 in range(0, slabs, 8):
                sums = [[None] * 8 for _ in range(group)]
                for k0 in range(0, depth, 16):
                    edges = [right_ref[turn * group + j, pl.ds(k0, 16), :].astype(F32) for j in range(group)]
                    for i in range(8):
                        left = left_ref[i0 + i, pl.ds(k0, 16), :]
                        for j in range(group):
                            term = left * edges[j]
                            term = term[:8] + term[8:]
                            sums[j][i] = term if k0 == 0 else sums[j][i] + term
                for j in range(group):
                    row = (first_row + turn * group + j) * slabs + i0
                    dest = dest_ref.at[0, pl.ds(pl.multiple_of(row, 8), 8), :]
                    total = fold(sums[j])
                    dest[...] = jnp.where(k_step == 0, total, total + dest[...])
            return 0

        lax.fori_loop(0, block // group, some_rows, 0)

    @pl.when(j_step < half_steps)
    def _():
        contract(send_ref, j_step * block)

    @pl.when(j_step >= half_steps)
    def _():
        contract(keep_ref, (j_step - half_steps) * block)


def last_kernel(keep_ref, got_ref, weight_ref, out_ref, *, owner_side):
    tri = keep_ref[0] + got_ref[0]
    d = tri - jnp.mean(tri, axis=-1, keepdims=True)
    var = jnp.mean(d * d, axis=-1, keepdims=True)
    n = (d * lax.rsqrt(var + EPS)).astype(BF16)
    projected = jnp.dot(n, weight_ref[...], preferred_element_type=F32)
    mine = owner_side(lax.axis_index("row")) == lax.axis_index("col")
    update = projected * jnp.where(mine, keep_ref[1], got_ref[1])
    out_ref[...] = update.astype(BF16).reshape(out_ref.shape)


def shards(pair_rep, slab_rep, length, weight_a, gate_a, weight_b, gate_b, weight_gate, weight_out):
    rows_dev, half_cols, width = pair_rep.shape
    hidden = weight_a.shape[1]
    count = lax.axis_size("row")
    side = lax.axis_index("col")
    half_rows = rows_dev // 2
    smem = pl.BlockSpec(memory_space=pltpu.SMEM)
    vmem = pl.BlockSpec(memory_space=pltpu.VMEM)

    slabs = count
    half = lax.dynamic_slice_in_dim(slab_rep, side * half_cols, half_cols, 1)
    slab = [half] + [lax.ppermute(half, "row", [(r, r ^ m) for r in range(count)]) for m in range(1, count)]

    rows_step = divisor(rows_dev, max(2, 1728 // half_cols), 2)
    whole_weight = pl.BlockSpec((width, hidden), lambda *_: (0, 0))
    right = pl.pallas_call(
        right_kernel,
        out_shape=jax.ShapeDtypeStruct((rows_dev, half_cols, hidden), BF16),
        grid=(rows_dev // rows_step,),
        in_specs=[
            smem,
            pl.BlockSpec((rows_step, half_cols, width), lambda s: (s, 0, 0)),
            whole_weight,
            whole_weight,
        ],
        out_specs=pl.BlockSpec((rows_step, half_cols, hidden), lambda s: (s, 0, 0)),
        compiler_params=pltpu.CompilerParams(vmem_limit_bytes=40 << 20),
        cost_estimate=pl.CostEstimate(
            flops=2 * rows_dev * half_cols * width * hidden * 6,
            bytes_accessed=4 * rows_dev * half_cols * width,
            transcendentals=2 * rows_dev * half_cols * width,
        ),
        name="right",
    )(length, pair_rep, gate_b, weight_b)

    depth = divisor(half_cols, 144, rows_dev)
    j_block = half_rows
    group = 3
    tri_shape = jax.ShapeDtypeStruct((2, half_rows * slabs, hidden), F32)
    tri_spec = pl.BlockSpec((2, half_rows * slabs, hidden), lambda k, j: (0, 0, 0))
    half_steps = half_rows // j_block

    def right_block(k, j):
        flip = 1 - lax.axis_index("col")
        return (lax.rem(j + flip * half_steps, 2 * half_steps), k, 0)

    send, keep = pl.pallas_call(
        functools.partial(tri_kernel, group=group),
        out_shape=(tri_shape, tri_shape),
        grid=(half_cols // depth, 2 * half_steps),
        in_specs=[
            smem,
            pl.BlockSpec((j_block, depth, hidden), right_block),
            whole_weight,
            whole_weight,
            whole_weight,
        ]
        + [pl.BlockSpec((1, depth, width), lambda k, j: (0, k, 0))] * slabs,
        out_specs=(tri_spec, tri_spec),
        scratch_shapes=[
            pltpu.VMEM((slabs, depth, hidden), F32),
            pltpu.VMEM((slabs * depth, width), F32),
        ],
        compiler_params=pltpu.CompilerParams(vmem_limit_bytes=48 << 20),
        cost_estimate=pl.CostEstimate(
            flops=2 * rows_dev * half_cols * slabs * hidden,
            bytes_accessed=2 * rows_dev * half_cols * width,
            transcendentals=slabs * half_cols * width,
        ),
        name="tri",
    )(length, right, gate_a, weight_a, weight_gate, *slab)

    got = lax.ppermute(send, "col", [(0, 1), (1, 0)])

    update = pl.pallas_call(
        functools.partial(last_kernel, owner_side=lambda row: (row * rows_dev) // half_cols),
        out_shape=jax.ShapeDtypeStruct((half_rows, slabs, width), BF16),
        in_specs=[vmem, vmem, vmem],
        out_specs=vmem,
        compiler_params=pltpu.CompilerParams(vmem_limit_bytes=32 << 20),
        name="last",
    )(keep, got, weight_out)
    return jnp.transpose(update, (1, 0, 2))


def solution(mesh):
    placed = (
        P(("groups", "row"), "col", None),
        P(("groups", "row"), None, None),
        P("groups"),
        P(),
        P(),
        P(),
        P(),
        P(),
        P(),
    )
    return jax.shard_map(
        shards,
        mesh=mesh,
        in_specs=placed,
        out_specs=P("groups", ("row", "col"), None),
        check_vma=False,
    )
```

```python
import functools

import jax
import jax.numpy as jnp
from jax import lax
from jax.experimental import pallas as pl
from jax.experimental.pallas import tpu as pltpu
from jax.sharding import PartitionSpec as P

EPS = 1e-05
F32 = jnp.float32
BF16 = jnp.bfloat16
QUAD = 4
GATE_ROWS = 40


def divisor(total, limit, step=1):
    return max(d for d in range(step, total + 1, step) if total % d == 0 and (d <= limit or d == step))


def doubling(count):
    bits = [1 << b for b in reversed(range(count.bit_length() - 1))]
    return bits, bits[-1:] + bits[:-1]


def slots(steps):
    held = [0]
    for step in steps:
        held = held + [m ^ step for m in held]
    return held


def centering(width):
    row = lax.broadcasted_iota(jnp.int32, (2 * width, 2 * width), 0)
    col = lax.broadcasted_iota(jnp.int32, (2 * width, 2 * width), 1)
    share = jnp.where((row < width) == (col < width), 1.0 / width, 0.0)
    center = jnp.where(row == col, 1.0, 0.0) - share
    return center.astype(BF16), share.astype(BF16)


def normed(first, second, center, share):
    wide = jnp.concatenate([first, second], axis=1)
    d = jnp.dot(wide, center, preferred_element_type=F32)
    var = jnp.dot((d * d).astype(BF16), share, preferred_element_type=F32)
    return (d * lax.rsqrt(var + EPS)).astype(BF16)


def gated(n, both):
    width = both.shape[1] // 2
    y = jnp.dot(n, both, preferred_element_type=F32)
    value = y[:, width:]
    return value + value * jnp.tanh(y[:, :width])


def pair_weights(gate_ref, weight_ref):
    half = jnp.asarray(0.5, BF16)
    return jnp.concatenate([gate_ref[...] * half, weight_ref[...] * half], axis=1)


def right_kernel(length_ref, pair_ref, gate_ref, weight_ref, out_ref, *, flip):
    rows, cols, width = pair_ref.shape
    half_rows = rows * pl.num_programs(0)
    live = length_ref[0]
    side = lax.axis_index("col")
    j_half = 1 - side if flip else side
    first_k = side * cols
    first_j = lax.axis_index("row") * 2 * half_rows + j_half * half_rows + pl.program_id(0) * rows
    center, share = centering(width)
    both = pair_weights(gate_ref, weight_ref)
    x = pair_ref[...].reshape(2, rows * cols // 2, width)
    n = normed(x[0], x[1], center, share)
    k = first_k + lax.broadcasted_iota(jnp.int32, (cols, width), 0)
    for part in range(2):
        edge = gated(n[:, part * width : (part + 1) * width], both).reshape(rows // 2, cols, width)
        for r in range(rows // 2):
            j = part * (rows // 2) + r
            reach = jnp.where(first_j + j < live, live, 0)
            out_ref[j] = jnp.where(k < reach, edge[r], 0.0).astype(BF16)


def fold(parts):
    place = lax.broadcasted_iota(jnp.int32, parts[0].shape, 0)
    for step in (1, 2, 4):
        here = (place & step) == 0
        parts = [
            jnp.where(here, a, b) + pltpu.roll(jnp.where(here, b, a), 8 - step, 0)
            for a, b in zip(parts[0::2], parts[1::2])
        ]
    return parts[0]


def project(length_ref, slab_ref, gate_ref, weight_ref, out_gate_ref, left_ref, gates_ref, norm_ref, half_rows):
    slabs, depth, width = slab_ref.shape
    k_step = pl.program_id(0)
    half_cols = depth * pl.num_programs(0)
    center, share = centering(width)
    both = pair_weights(gate_ref, weight_ref)
    first_k = lax.axis_index("col") * half_cols + k_step * depth
    live = first_k + lax.broadcasted_iota(jnp.int32, (depth, width), 0) < length_ref[0]
    first_j = lax.rem(lax.axis_index("row") * (2 * half_rows), half_cols)
    start = lax.rem(first_j, depth)

    def pair(s):
        n = normed(slab_ref[s], slab_ref[s + 1], center, share)
        for part in range(2):
            norm_ref[pl.ds(part * (depth + GATE_ROWS), depth), :] = n[:, part * width : (part + 1) * width].astype(F32)
            edge = gated(n[:, part * width : (part + 1) * width], both)
            left_ref[s + part] = jnp.where(live, edge, 0.0).astype(BF16).astype(left_ref.dtype)

        @pl.when(k_step == first_j // depth)
        def _():
            own = [norm_ref[pl.ds(start + part * (depth + GATE_ROWS), GATE_ROWS), :] for part in range(2)]
            rows = jnp.concatenate(own, axis=0).astype(BF16)
            y = jnp.dot(rows, out_gate_ref[...] * jnp.asarray(0.5, BF16), preferred_element_type=F32)
            gate = (0.5 + 0.5 * jnp.tanh(y)).astype(BF16).astype(F32)
            gates_ref[pl.ds(pl.multiple_of(s * GATE_ROWS, 8), 2 * GATE_ROWS), :] = gate

    if slabs <= 8:
        for s in range(0, slabs, 2):
            pair(s)
    else:
        pl.loop(0, slabs, step=2)(pair)


def contract(left_ref, right_ref, sums_ref):
    slabs, depth, _ = left_ref.shape
    rows = right_ref.shape[0]
    group = divisor(rows, 6, 2)

    def tile(turn, _):
        q = turn // (rows // group)
        j0 = lax.rem(turn, rows // group) * group
        sums = [[None] * QUAD for _ in range(group)]
        for k0 in range(0, depth, 16):
            edges = [right_ref[j0 + j, pl.ds(k0, 16), :].astype(F32) for j in range(group)]
            for n in range(QUAD):
                left = left_ref[q * QUAD + n, pl.ds(k0, 16), :].astype(F32)
                for j in range(group):
                    term = left * edges[j]
                    term = term[:8] + term[8:]
                    sums[j][n] = term if k0 == 0 else sums[j][n] + term
        for j in range(0, group, 2):
            dest = sums_ref.at[q, pl.ds(pl.multiple_of((j0 + j) * QUAD, 8), 8), :]
            total = fold(sums[j] + sums[j + 1])
            dest[...] = jnp.where(pl.program_id(0) == 0, total, total + dest[...])
        return 0

    lax.fori_loop(0, slabs // QUAD * (rows // group), tile, 0)


def assemble(dest_ref, sums_ref, gates_ref, steps, last, j_half):
    half_rows = sums_ref.shape[1] // QUAD
    count = dest_ref.shape[1] // half_rows
    side, place = lax.axis_index("col"), lax.axis_index("row")
    for n, (m0, m1) in enumerate(zip(*(slots(s[:-1]) for s in steps))):
        if last:
            m0, m1 = m0 ^ steps[0][-1], m1 ^ steps[1][-1]
        i = jnp.bitwise_xor(place, jnp.where(side == 0, m0, m1))
        rows = pl.ds(i, half_rows, stride=count)
        dest_ref[0, rows, :] = sums_ref[n // QUAD, pl.ds(n % QUAD, half_rows, stride=QUAD), :]
        dest_ref[1, rows, :] = gates_ref[pl.ds(n * GATE_ROWS + j_half * half_rows, half_rows), :]


def near_kernel(
    length_ref, mate_ref, own_ref, slab_ref, gate_ref, weight_ref, out_gate_ref,
    mate_sums_ref, own_sums_ref, gates_ref, left_ref, norm_ref,
):
    project(
        length_ref, slab_ref, gate_ref, weight_ref, out_gate_ref, left_ref, gates_ref, norm_ref, mate_ref.shape[0]
    )
    contract(left_ref, mate_ref, mate_sums_ref)
    contract(left_ref, own_ref, own_sums_ref)


def send_kernel(
    length_ref, mate_ref, slab_ref, gate_ref, weight_ref, out_gate_ref, near_sums_ref, near_gates_ref,
    send_ref, left_ref, gates_ref, sums_ref, norm_ref, *, steps,
):
    project(
        length_ref, slab_ref, gate_ref, weight_ref, out_gate_ref, left_ref, gates_ref, norm_ref, mate_ref.shape[0]
    )
    contract(left_ref, mate_ref, sums_ref)

    @pl.when(pl.program_id(0) == pl.num_programs(0) - 1)
    def _():
        flip = 1 - lax.axis_index("col")
        assemble(send_ref, near_sums_ref, near_gates_ref, steps, False, flip)
        assemble(send_ref, sums_ref, gates_ref, steps, True, flip)


def keep_kernel(
    own_ref, left_ref, gates_ref, near_sums_ref, near_gates_ref, keep_ref, sums_ref, *, steps
):
    contract(left_ref, own_ref, sums_ref)

    @pl.when(pl.program_id(0) == pl.num_programs(0) - 1)
    def _():
        side = lax.axis_index("col")
        assemble(keep_ref, near_sums_ref, near_gates_ref, steps, False, side)
        assemble(keep_ref, sums_ref, gates_ref, steps, True, side)


def last_kernel(keep_ref, got_ref, weight_ref, out_ref, *, half_cols):
    rows_dev = 2 * out_ref.shape[0]
    tri = keep_ref[0] + got_ref[0]
    d = tri - jnp.mean(tri, axis=-1, keepdims=True)
    var = jnp.mean(d * d, axis=-1, keepdims=True)
    n = (d * lax.rsqrt(var + EPS)).astype(BF16)
    projected = jnp.dot(n, weight_ref[...], preferred_element_type=F32)
    mine = lax.axis_index("row") * rows_dev // half_cols == lax.axis_index("col")
    update = projected * jnp.where(mine, keep_ref[1], got_ref[1])
    out_ref[...] = update.astype(BF16).reshape(out_ref.shape)


def shards(pair_rep, slab_rep, length, weight_a, gate_a, weight_b, gate_b, weight_gate, weight_out):
    rows_dev, half_cols, width = pair_rep.shape
    hidden = weight_a.shape[1]
    count = lax.axis_size("row")
    side = lax.axis_index("col")
    half_rows = rows_dev // 2
    steps = doubling(count)
    depth = divisor(half_cols, 144, rows_dev)
    blocks = half_cols // depth
    near = count // 2
    smem = pl.BlockSpec(memory_space=pltpu.SMEM)
    vmem = pl.BlockSpec(memory_space=pltpu.VMEM)
    params = pltpu.CompilerParams(vmem_limit_bytes=48 << 20)

    def whole(*shape):
        return pl.BlockSpec(shape, lambda *_: (0,) * len(shape))

    def deep(*shape):
        return pl.BlockSpec(shape, lambda k: (0, k, 0))

    def passed(x, step):
        pairs = []
        for row in range(count):
            for core in range(2):
                pairs.append((row * 2 + core, (row ^ steps[core][step]) * 2 + core))
        return lax.ppermute(x, ("row", "col"), pairs)

    def right_half(pair, flip):
        rows_step = divisor(half_rows, max(2, 1728 // half_cols), 2)
        turns = half_rows // rows_step

        def block(s):
            return ((1 - lax.axis_index("col") if flip else lax.axis_index("col")) * turns + s, 0, 0)

        return pl.pallas_call(
            functools.partial(right_kernel, flip=flip),
            out_shape=jax.ShapeDtypeStruct((half_rows, half_cols, hidden), BF16),
            grid=(turns,),
            in_specs=[
                smem,
                pl.BlockSpec((rows_step, half_cols, width), block),
                whole(width, hidden),
                whole(width, hidden),
            ],
            out_specs=pl.BlockSpec((rows_step, half_cols, hidden), lambda s: (s, 0, 0)),
            compiler_params=pltpu.CompilerParams(vmem_limit_bytes=60 << 20),
            cost_estimate=pl.CostEstimate(
                flops=2 * half_rows * half_cols * width * hidden * 6,
                bytes_accessed=4 * half_rows * half_cols * width,
                transcendentals=2 * half_rows * half_cols * width,
            ),
            name="right_mate" if flip else "right_own",
        )(length, pair, gate_b, weight_b)

    sums = jax.ShapeDtypeStruct((near // QUAD, half_rows * QUAD, hidden), F32)
    gates = jax.ShapeDtypeStruct((near * GATE_ROWS, width), F32)
    swapped = jax.ShapeDtypeStruct((2, half_rows * count, hidden), F32)
    norm = pltpu.VMEM((2 * (depth + GATE_ROWS), width), F32)
    cost = pl.CostEstimate(
        flops=2 * rows_dev * half_cols * near * hidden,
        bytes_accessed=2 * rows_dev * half_cols * width,
        transcendentals=near * half_cols * width,
    )

    held = lax.dynamic_slice_in_dim(slab_rep, side * half_cols, half_cols, 1)
    right = []
    got = None
    for step in range(len(steps[0])):
        if step > 0:
            held = jnp.concatenate([held, got], axis=0)
        if len(right) < step and len(right) < 2:
            made, held = lax.optimization_barrier((right_half(pair_rep, not right), held))
            right.append(made)
        got = passed(held, step)
    right_mate, right_own = right

    near_mate, near_own, near_gates = pl.pallas_call(
        near_kernel,
        out_shape=(sums, sums, gates),
        grid=(blocks,),
        in_specs=[
            smem,
            deep(half_rows, depth, hidden),
            deep(half_rows, depth, hidden),
            deep(near, depth, width),
            whole(width, hidden),
            whole(width, hidden),
            whole(width, width),
        ],
        out_specs=(whole(*sums.shape), whole(*sums.shape), whole(*gates.shape)),
        scratch_shapes=[pltpu.VMEM((near, depth, hidden), F32), norm],
        compiler_params=params,
        cost_estimate=cost,
        name="near",
    )(length, right_mate, right_own, held, gate_a, weight_a, weight_gate)

    send, left, far_gates = pl.pallas_call(
        functools.partial(send_kernel, steps=steps),
        out_shape=(swapped, jax.ShapeDtypeStruct((near, half_cols, hidden), BF16), gates),
        grid=(blocks,),
        in_specs=[
            smem,
            deep(half_rows, depth, hidden),
            deep(near, depth, width),
            whole(width, hidden),
            whole(width, hidden),
            whole(width, width),
            whole(*sums.shape),
            whole(*gates.shape),
        ],
        out_specs=(whole(*swapped.shape), deep(near, depth, hidden), whole(*gates.shape)),
        scratch_shapes=[pltpu.VMEM(sums.shape, F32), norm],
        compiler_params=params,
        name="send",
    )(length, right_mate, got, gate_a, weight_a, weight_gate, near_mate, near_gates)

    swap = lax.ppermute(send, "col", [(0, 1), (1, 0)])

    keep = pl.pallas_call(
        functools.partial(keep_kernel, steps=steps),
        out_shape=swapped,
        grid=(blocks,),
        in_specs=[
            deep(half_rows, depth, hidden),
            deep(near, depth, hidden),
            whole(*gates.shape),
            whole(*sums.shape),
            whole(*gates.shape),
        ],
        out_specs=whole(*swapped.shape),
        scratch_shapes=[pltpu.VMEM(sums.shape, F32)],
        compiler_params=params,
        cost_estimate=cost,
        name="keep",
    )(right_own, left, far_gates, near_own, near_gates)

    update = pl.pallas_call(
        functools.partial(last_kernel, half_cols=half_cols),
        out_shape=jax.ShapeDtypeStruct((half_rows, count, width), BF16),
        in_specs=[vmem, vmem, vmem],
        out_specs=vmem,
        compiler_params=pltpu.CompilerParams(vmem_limit_bytes=32 << 20),
        name="last",
    )(keep, swap, weight_out)
    return jnp.transpose(update, (1, 0, 2))


def solution(mesh):
    placed = (
        P(("groups", "row"), "col", None),
        P(("groups", "row"), None, None),
        P("groups"),
        P(),
        P(),
        P(),
        P(),
        P(),
        P(),
    )
    return jax.shard_map(
        shards,
        mesh=mesh,
        in_specs=placed,
        out_specs=P("groups", ("row", "col"), None),
        check_vma=False,
    )
```

```python
import functools

import jax
import jax.numpy as jnp
from jax import lax
from jax.experimental import pallas as pl
from jax.experimental.pallas import tpu as pltpu
from jax.sharding import PartitionSpec as P

EPS = 1e-05
F32 = jnp.float32
BF16 = jnp.bfloat16
QUAD = 4
GATE_ROWS = 40


def divisor(total, limit, step=1):
    return max(d for d in range(step, total + 1, step) if total % d == 0 and (d <= limit or d == step))


def doubling(count):
    bits = [1 << b for b in reversed(range(count.bit_length() - 1))]
    return bits, bits[-1:] + bits[:-1]


def slots(steps):
    held = [0]
    for step in steps:
        held = held + [m ^ step for m in held]
    return held


def centering(width):
    row = lax.broadcasted_iota(jnp.int32, (2 * width, 2 * width), 0)
    col = lax.broadcasted_iota(jnp.int32, (2 * width, 2 * width), 1)
    share = jnp.where((row < width) == (col < width), 1.0 / width, 0.0)
    center = jnp.where(row == col, 1.0, 0.0) - share
    return center.astype(BF16), share.astype(BF16)


def normed(first, second, center, share):
    wide = jnp.concatenate([first, second], axis=1)
    d = jnp.dot(wide, center, preferred_element_type=F32)
    var = jnp.dot((d * d).astype(BF16), share, preferred_element_type=F32)
    return (d * lax.rsqrt(var + EPS)).astype(BF16)


def gated(n, both):
    width = both.shape[1] // 2
    y = jnp.dot(n, both, preferred_element_type=F32)
    value = y[:, width:]
    return value + value * jnp.tanh(y[:, :width])


def right_rows(pair_ref, out_ref, both, live, j_half, chunk, wait):
    half_rows, cols, width = pair_ref.shape
    first_j = (lax.axis_index("row") * 2 + j_half) * half_rows
    center, share = centering(width)
    k = lax.axis_index("col") * cols + lax.broadcasted_iota(jnp.int32, (cols, width), 0)

    def some(turn, _):
        wait(turn)
        j0 = turn * chunk
        x = pair_ref[pl.ds(j0, chunk)].reshape(2, chunk * cols // 2, width)
        n = normed(x[0], x[1], center, share)
        for part in range(2):
            edge = gated(n[:, part * width : (part + 1) * width], both).reshape(chunk // 2, cols, width)
            for r in range(chunk // 2):
                j = j0 + part * (chunk // 2) + r
                reach = jnp.where(first_j + j < live, live, 0)
                out_ref[j] = jnp.where(k < reach, edge[r], 0.0).astype(BF16)
        return 0

    lax.fori_loop(0, half_rows // chunk, some, 0)


def mate_kernel(
    length_ref, pair_ref, weight_a_ref, gate_a_ref, weight_b_ref, gate_b_ref, weight_gate_ref, weight_out_ref,
    right_ref, own_ref, live_ref, both_a_ref, both_b_ref, out_gate_ref, last_ref,
    mate_ref, raw_ref, count_ref, sems, chunk_sems, *, chunk,
):
    half_rows, cols, width = mate_ref.shape
    side = lax.axis_index("col")
    turns = half_rows // chunk
    sources = [length_ref, weight_b_ref, gate_b_ref, weight_a_ref, gate_a_ref, weight_gate_ref, weight_out_ref]
    places = [count_ref] + [raw_ref.at[n] for n in range(5)] + [last_ref]
    small = [pltpu.make_async_copy(src, dst, sems.at[n]) for n, (src, dst) in enumerate(zip(sources, places))]

    def piece(turn):
        rows = pl.ds((1 - side) * half_rows + turn * chunk, chunk)
        return pltpu.make_async_copy(pair_ref.at[rows], mate_ref.at[pl.ds(turn * chunk, chunk)], chunk_sems.at[turn])

    own = pltpu.make_async_copy(pair_ref.at[pl.ds(side * half_rows, half_rows)], own_ref, sems.at[len(small)])
    for copy in small[:3]:
        copy.start()
    for turn in range(turns):
        piece(turn).start()
    for copy in small[3:]:
        copy.start()
    own.start()
    for copy in small[:3]:
        copy.wait()
    half = jnp.asarray(0.5, BF16)
    both_b_ref[...] = jnp.concatenate([raw_ref[1] * half, raw_ref[0] * half], axis=1)
    live = count_ref[0]
    live_ref[...] = jnp.full(live_ref.shape, live, jnp.int32)
    right_rows(mate_ref, right_ref, both_b_ref[...], live, 1 - side, chunk, lambda turn: piece(turn).wait())
    for copy in small[3:]:
        copy.wait()
    both_a_ref[...] = jnp.concatenate([raw_ref[3] * half, raw_ref[2] * half], axis=1)
    out_gate_ref[...] = raw_ref[4] * half
    own.wait()


def own_kernel(live_ref, pair_ref, both_ref, out_ref, *, chunk):
    live = live_ref[0, 0]
    right_rows(pair_ref, out_ref, both_ref[...], live, lax.axis_index("col"), chunk, lambda turn: None)


def fold(parts):
    place = lax.broadcasted_iota(jnp.int32, parts[0].shape, 0)
    for step in (1, 2, 4):
        here = (place & step) == 0
        parts = [
            jnp.where(here, a, b) + pltpu.roll(jnp.where(here, b, a), 8 - step, 0)
            for a, b in zip(parts[0::2], parts[1::2])
        ]
    return parts[0]


def project(live_ref, slab_ref, both_ref, out_gate_ref, left_ref, gates_ref, norm_ref, half_rows):
    slabs, depth, width = slab_ref.shape
    k_step = pl.program_id(0)
    half_cols = depth * pl.num_programs(0)
    center, share = centering(width)
    both = both_ref[...]
    first_k = lax.axis_index("col") * half_cols + k_step * depth
    live = first_k + lax.broadcasted_iota(jnp.int32, (depth, width), 0) < live_ref[0:1, :]
    first_j = lax.rem(lax.axis_index("row") * (2 * half_rows), half_cols)
    start = lax.rem(first_j, depth)

    def quad(q):
        s = q * QUAD
        x = slab_ref[pl.ds(s, QUAD)].reshape(2, 2 * depth, width)
        n = normed(x[0], x[1], center, share)
        for part in range(2):
            own = n[:, part * width : (part + 1) * width]
            edge = gated(own, both)
            for r in range(2):
                here = slice(r * depth, (r + 1) * depth)
                left_ref[s + 2 * part + r] = jnp.where(live, edge[here], 0.0).astype(BF16).astype(F32)
                norm_ref[2 * part + r, pl.ds(0, depth), :] = own[here].astype(F32)

        @pl.when(k_step == first_j // depth)
        def _():
            rows = jnp.concatenate([norm_ref[n, pl.ds(start, GATE_ROWS), :] for n in range(QUAD)], axis=0)
            y = jnp.dot(rows.astype(BF16), out_gate_ref[...], preferred_element_type=F32)
            gate = (0.5 + 0.5 * jnp.tanh(y)).astype(BF16).astype(F32)
            gates_ref[pl.ds(pl.multiple_of(s * GATE_ROWS, 8), QUAD * GATE_ROWS), :] = gate

    if slabs == QUAD:
        quad(0)
    else:
        pl.loop(0, slabs // QUAD)(quad)


def contract(left_ref, right_ref, sums_ref):
    slabs, depth, _ = left_ref.shape
    rows = right_ref.shape[0]
    group = divisor(rows, 6, 2)

    def tile(turn, _):
        q = turn // (rows // group)
        j0 = lax.rem(turn, rows // group) * group
        sums = [[None] * QUAD for _ in range(group)]
        for k0 in range(0, depth, 16):
            edges = [right_ref[j0 + j, pl.ds(k0, 16), :].astype(F32) for j in range(group)]
            for n in range(QUAD):
                left = left_ref[q * QUAD + n, pl.ds(k0, 16), :].astype(F32)
                for j in range(group):
                    term = left * edges[j]
                    term = term[:8] + term[8:]
                    sums[j][n] = term if k0 == 0 else sums[j][n] + term
        for j in range(0, group, 2):
            dest = sums_ref.at[q, pl.ds(pl.multiple_of((j0 + j) * QUAD, 8), 8), :]
            total = fold(sums[j] + sums[j + 1])
            dest[...] = jnp.where(pl.program_id(0) == 0, total, total + dest[...])
        return 0

    lax.fori_loop(0, slabs // QUAD * (rows // group), tile, 0)


def assemble(dest_ref, sums_ref, gates_ref, steps, last, j_half):
    half_rows = sums_ref.shape[1] // QUAD
    count = dest_ref.shape[1] // half_rows
    side, place = lax.axis_index("col"), lax.axis_index("row")
    for n, (m0, m1) in enumerate(zip(*(slots(s[:-1]) for s in steps))):
        if last:
            m0, m1 = m0 ^ steps[0][-1], m1 ^ steps[1][-1]
        i = jnp.bitwise_xor(place, jnp.where(side == 0, m0, m1))
        rows = pl.ds(i, half_rows, stride=count)
        dest_ref[0, rows, :] = sums_ref[n // QUAD, pl.ds(n % QUAD, half_rows, stride=QUAD), :]
        dest_ref[1, rows, :] = gates_ref[pl.ds(n * GATE_ROWS + j_half * half_rows, half_rows), :]


def near_kernel(
    live_ref, mate_ref, own_ref, slab_ref, both_ref, out_gate_ref,
    mate_sums_ref, own_sums_ref, gates_ref, left_ref, norm_ref,
):
    project(live_ref, slab_ref, both_ref, out_gate_ref, left_ref, gates_ref, norm_ref, mate_ref.shape[0])
    contract(left_ref, mate_ref, mate_sums_ref)
    contract(left_ref, own_ref, own_sums_ref)


def send_kernel(
    live_ref, mate_ref, slab_ref, both_ref, out_gate_ref, near_sums_ref, near_gates_ref,
    send_ref, left_out_ref, gates_ref, left_ref, sums_ref, norm_ref, *, steps,
):
    project(live_ref, slab_ref, both_ref, out_gate_ref, left_ref, gates_ref, norm_ref, mate_ref.shape[0])
    left_out_ref[...] = left_ref[...].astype(BF16)
    contract(left_ref, mate_ref, sums_ref)

    @pl.when(pl.program_id(0) == pl.num_programs(0) - 1)
    def _():
        flip = 1 - lax.axis_index("col")
        assemble(send_ref, near_sums_ref, near_gates_ref, steps, False, flip)
        assemble(send_ref, sums_ref, gates_ref, steps, True, flip)


def keep_kernel(
    own_ref, left_ref, gates_ref, near_sums_ref, near_gates_ref, keep_ref, sums_ref, *, steps
):
    contract(left_ref, own_ref, sums_ref)

    @pl.when(pl.program_id(0) == pl.num_programs(0) - 1)
    def _():
        side = lax.axis_index("col")
        assemble(keep_ref, near_sums_ref, near_gates_ref, steps, False, side)
        assemble(keep_ref, sums_ref, gates_ref, steps, True, side)


def last_kernel(keep_ref, got_ref, weight_ref, out_ref, *, half_cols):
    rows_dev = 2 * out_ref.shape[0]
    tri = keep_ref[0] + got_ref[0]
    d = tri - jnp.mean(tri, axis=-1, keepdims=True)
    var = jnp.mean(d * d, axis=-1, keepdims=True)
    n = (d * lax.rsqrt(var + EPS)).astype(BF16)
    projected = jnp.dot(n, weight_ref[...], preferred_element_type=F32)
    mine = lax.axis_index("row") * rows_dev // half_cols == lax.axis_index("col")
    update = projected * jnp.where(mine, keep_ref[1], got_ref[1])
    out_ref[...] = update.astype(BF16).reshape(out_ref.shape)


def shards(pair_rep, slab_rep, length, weight_a, gate_a, weight_b, gate_b, weight_gate, weight_out):
    rows_dev, half_cols, width = pair_rep.shape
    hidden = weight_a.shape[1]
    count = lax.axis_size("row")
    side = lax.axis_index("col")
    half_rows = rows_dev // 2
    steps = doubling(count)
    depth = divisor(half_cols, 144, rows_dev)
    blocks = half_cols // depth
    near = count // 2
    hbm = pl.BlockSpec(memory_space=pltpu.HBM)
    vmem = pl.BlockSpec(memory_space=pltpu.VMEM)
    params = pltpu.CompilerParams(vmem_limit_bytes=40 << 20)

    def whole(*shape):
        return pl.BlockSpec(shape, lambda *_: (0,) * len(shape))

    def deep(*shape):
        return pl.BlockSpec(shape, lambda k: (0, k, 0))

    def passed(x, step):
        pairs = []
        for row in range(count):
            for core in range(2):
                pairs.append((row * 2 + core, (row ^ steps[core][step]) * 2 + core))
        return lax.ppermute(x, ("row", "col"), pairs)

    chunk = divisor(half_rows, max(2, 1728 // half_cols), 2)
    half_right = jax.ShapeDtypeStruct((half_rows, half_cols, hidden), BF16)
    half_pair = jax.ShapeDtypeStruct((half_rows, half_cols, width), BF16)
    right_cost = pl.CostEstimate(
        flops=2 * half_rows * half_cols * width * hidden * 6,
        bytes_accessed=4 * half_rows * half_cols * width,
        transcendentals=2 * half_rows * half_cols * width,
    )
    mate_call = pl.pallas_call(
        functools.partial(mate_kernel, chunk=chunk),
        out_shape=(
            half_right,
            half_pair,
            jax.ShapeDtypeStruct((8, width), jnp.int32),
            jax.ShapeDtypeStruct((width, 2 * hidden), BF16),
            jax.ShapeDtypeStruct((width, 2 * hidden), BF16),
            jax.ShapeDtypeStruct((width, width), BF16),
            jax.ShapeDtypeStruct((hidden, width), BF16),
        ),
        in_specs=[hbm] * 8,
        out_specs=[vmem] * 7,
        scratch_shapes=[
            pltpu.VMEM(half_pair.shape, BF16),
            pltpu.VMEM((5, width, hidden), BF16),
            pltpu.SMEM((1,), jnp.int32),
            pltpu.SemaphoreType.DMA((8,)),
            pltpu.SemaphoreType.DMA((half_rows // chunk,)),
        ],
        compiler_params=pltpu.CompilerParams(vmem_limit_bytes=58 << 20),
        cost_estimate=right_cost,
        name="right_mate",
    )
    own_call = pl.pallas_call(
        functools.partial(own_kernel, chunk=chunk),
        out_shape=half_right,
        in_specs=[vmem] * 3,
        out_specs=vmem,
        compiler_params=params,
        cost_estimate=right_cost,
        name="right_own",
    )

    sums = jax.ShapeDtypeStruct((near // QUAD, half_rows * QUAD, hidden), F32)
    gates = jax.ShapeDtypeStruct((near * GATE_ROWS, width), F32)
    swapped = jax.ShapeDtypeStruct((2, half_rows * count, hidden), F32)
    norm = pltpu.VMEM((QUAD, depth + GATE_ROWS, width), F32)
    cost = pl.CostEstimate(
        flops=2 * rows_dev * half_cols * near * hidden,
        bytes_accessed=2 * rows_dev * half_cols * width,
        transcendentals=near * half_cols * width,
    )

    held = lax.dynamic_slice_in_dim(slab_rep, side * half_cols, half_cols, 1)
    got = passed(held, 0)
    for step in range(1, len(steps[0])):
        held = jnp.concatenate([held, got], axis=0)
        if step == 1:
            made = mate_call(length, pair_rep, weight_a, gate_a, weight_b, gate_b, weight_gate, weight_out)
            made, held = lax.optimization_barrier((made, held))
            right_mate, pair_own, live, both_a, both_b, out_gate, last_weight = made
        if step == 2:
            right_own, held = lax.optimization_barrier((own_call(live, pair_own, both_b), held))
        got = passed(held, step)

    near_mate, near_own, near_gates = pl.pallas_call(
        near_kernel,
        out_shape=(sums, sums, gates),
        grid=(blocks,),
        in_specs=[
            whole(*live.shape),
            deep(half_rows, depth, hidden),
            deep(half_rows, depth, hidden),
            deep(near, depth, width),
            whole(width, 2 * hidden),
            whole(width, width),
        ],
        out_specs=(whole(*sums.shape), whole(*sums.shape), whole(*gates.shape)),
        scratch_shapes=[pltpu.VMEM((near, depth, hidden), F32), norm],
        compiler_params=params,
        cost_estimate=cost,
        name="near",
    )(live, right_mate, right_own, held, both_a, out_gate)

    send, left, far_gates = pl.pallas_call(
        functools.partial(send_kernel, steps=steps),
        out_shape=(swapped, jax.ShapeDtypeStruct((near, half_cols, hidden), BF16), gates),
        grid=(blocks,),
        in_specs=[
            whole(*live.shape),
            deep(half_rows, depth, hidden),
            deep(near, depth, width),
            whole(width, 2 * hidden),
            whole(width, width),
            whole(*sums.shape),
            whole(*gates.shape),
        ],
        out_specs=(whole(*swapped.shape), deep(near, depth, hidden), whole(*gates.shape)),
        scratch_shapes=[pltpu.VMEM((near, depth, hidden), F32), pltpu.VMEM(sums.shape, F32), norm],
        compiler_params=params,
        name="send",
    )(live, right_mate, got, both_a, out_gate, near_mate, near_gates)

    swap = lax.ppermute(send, "col", [(0, 1), (1, 0)])

    keep = pl.pallas_call(
        functools.partial(keep_kernel, steps=steps),
        out_shape=swapped,
        grid=(blocks,),
        in_specs=[
            deep(half_rows, depth, hidden),
            deep(near, depth, hidden),
            whole(*gates.shape),
            whole(*sums.shape),
            whole(*gates.shape),
        ],
        out_specs=whole(*swapped.shape),
        scratch_shapes=[pltpu.VMEM(sums.shape, F32)],
        compiler_params=params,
        cost_estimate=cost,
        name="keep",
    )(right_own, left, far_gates, near_own, near_gates)

    update = pl.pallas_call(
        functools.partial(last_kernel, half_cols=half_cols),
        out_shape=jax.ShapeDtypeStruct((half_rows, count, width), BF16),
        in_specs=[vmem, vmem, vmem],
        out_specs=vmem,
        compiler_params=pltpu.CompilerParams(vmem_limit_bytes=32 << 20),
        name="last",
    )(keep, swap, last_weight)
    return jnp.transpose(update, (1, 0, 2))


def solution(mesh):
    placed = (
        P(("groups", "row"), "col", None),
        P(("groups", "row"), None, None),
        P("groups"),
        P(),
        P(),
        P(),
        P(),
        P(),
        P(),
    )
    return jax.shard_map(
        shards,
        mesh=mesh,
        in_specs=placed,
        out_specs=P("groups", ("row", "col"), None),
        check_vma=False,
    )
```

```python
import functools

import jax
import jax.numpy as jnp
from jax import lax
from jax.experimental import pallas as pl
from jax.experimental.pallas import tpu as pltpu
from jax.sharding import PartitionSpec as P

EPS = 1e-05
F32 = jnp.float32
BF16 = jnp.bfloat16
QUAD = 4
GATE_ROWS = 40


def divisor(total, limit, step=1):
    return max(d for d in range(step, total + 1, step) if total % d == 0 and (d <= limit or d == step))


def doubling(count):
    bits = [1 << b for b in reversed(range(count.bit_length() - 1))]
    return bits, bits[-1:] + bits[:-1]


def slots(steps):
    held = [0]
    for step in steps:
        held = held + [m ^ step for m in held]
    return held


def centering(width):
    row = lax.broadcasted_iota(jnp.int32, (2 * width, 2 * width), 0)
    col = lax.broadcasted_iota(jnp.int32, (2 * width, 2 * width), 1)
    share = jnp.where((row < width) == (col < width), 1.0 / width, 0.0)
    center = jnp.where(row == col, 1.0, 0.0) - share
    return center.astype(BF16), share.astype(BF16)


def normed(first, second, center, share):
    wide = jnp.concatenate([first, second], axis=1)
    d = jnp.dot(wide, center, preferred_element_type=F32)
    var = jnp.dot((d * d).astype(BF16), share, preferred_element_type=F32)
    return (d * lax.rsqrt(var + EPS)).astype(BF16)


def gated(n, both):
    width = both.shape[1] // 2
    y = jnp.dot(n, both, preferred_element_type=F32)
    value = y[:, width:]
    return value + value * jnp.tanh(y[:, :width])


def right_kernel(
    length_ref, pair_ref, weight_ref, gate_ref, out_ref, x_ref, y_ref, w_ref, count_ref, small_sems, in_sems, out_sems,
    *, chunk,
):
    rows, cols, width = pair_ref.shape
    turns = rows // chunk

    def piece(turn, src, dst, sems):
        here = pl.ds(turn * chunk, chunk)
        return pltpu.make_async_copy(src.at[here], dst.at[here], sems.at[turn])

    small = [
        pltpu.make_async_copy(src, dst, small_sems.at[n])
        for n, (src, dst) in enumerate(
            ((length_ref, count_ref), (gate_ref, w_ref.at[0]), (weight_ref, w_ref.at[1]))
        )
    ]
    for copy in small:
        copy.start()
    for turn in range(turns):
        piece(turn, pair_ref, x_ref, in_sems).start()
    for copy in small:
        copy.wait()
    half = jnp.asarray(0.5, BF16)
    both = jnp.concatenate([w_ref[0] * half, w_ref[1] * half], axis=1)
    live = count_ref[0]
    first_j = lax.axis_index("row") * rows
    center, share = centering(width)
    k = lax.axis_index("col") * cols + lax.broadcasted_iota(jnp.int32, (cols, width), 0)

    def some(turn, _):
        piece(turn, pair_ref, x_ref, in_sems).wait()
        j0 = turn * chunk
        x = x_ref[pl.ds(j0, chunk)].reshape(2, chunk * cols // 2, width)
        n = normed(x[0], x[1], center, share)
        for part in range(2):
            edge = gated(n[:, part * width : (part + 1) * width], both).reshape(chunk // 2, cols, width)
            for r in range(chunk // 2):
                j = j0 + part * (chunk // 2) + r
                reach = jnp.where(first_j + j < live, live, 0)
                y_ref[j] = jnp.where(k < reach, edge[r], 0.0).astype(BF16)
        piece(turn, y_ref, out_ref, out_sems).start()
        return 0

    lax.fori_loop(0, turns, some, 0)
    for turn in range(turns):
        piece(turn, y_ref, out_ref, out_sems).wait()


def fold(parts):
    place = lax.broadcasted_iota(jnp.int32, parts[0].shape, 0)
    for step in (1, 2, 4):
        here = (place & step) == 0
        parts = [
            jnp.where(here, a, b) + pltpu.roll(jnp.where(here, b, a), 8 - step, 0)
            for a, b in zip(parts[0::2], parts[1::2])
        ]
    return parts[0]


def block_of(blocks):
    return 0 if blocks == 1 else pl.program_id(0)


def project(length_ref, slab_ref, gate_ref, weight_ref, out_gate_ref, left_ref, gates_ref, norm_ref, half_rows, blocks):
    slabs, depth, width = slab_ref.shape
    k_step = block_of(blocks)
    half_cols = depth * blocks
    half = jnp.asarray(0.5, BF16)
    center, share = centering(width)
    both = jnp.concatenate([gate_ref[...] * half, weight_ref[...] * half], axis=1)
    first_k = lax.axis_index("col") * half_cols + k_step * depth
    live = first_k + lax.broadcasted_iota(jnp.int32, (depth, width), 0) < length_ref[0]
    first_j = lax.rem(lax.axis_index("row") * (2 * half_rows), half_cols)
    start = lax.rem(first_j, depth)

    def quad(q):
        s = q * QUAD
        x = slab_ref[pl.ds(s, QUAD)].reshape(2, 2 * depth, width)
        n = normed(x[0], x[1], center, share)
        for part in range(2):
            own = n[:, part * width : (part + 1) * width]
            edge = gated(own, both)
            for r in range(2):
                here = slice(r * depth, (r + 1) * depth)
                left_ref[s + 2 * part + r] = jnp.where(live, edge[here], 0.0).astype(BF16).astype(F32)
                norm_ref[2 * part + r, pl.ds(0, depth), :] = own[here].astype(F32)

        def gates():
            rows = jnp.concatenate([norm_ref[n, pl.ds(start, GATE_ROWS), :] for n in range(QUAD)], axis=0)
            y = jnp.dot(rows.astype(BF16), out_gate_ref[...] * half, preferred_element_type=F32)
            gate = (0.5 + 0.5 * jnp.tanh(y)).astype(BF16).astype(F32)
            gates_ref[pl.ds(pl.multiple_of(s * GATE_ROWS, 8), QUAD * GATE_ROWS), :] = gate

        if blocks == 1:
            gates()
        else:
            pl.when(k_step == first_j // depth)(gates)

    if slabs == QUAD:
        quad(0)
    else:
        pl.loop(0, slabs // QUAD)(quad)


def contract(left_ref, right_ref, j_half, sums_ref, blocks):
    slabs, depth, _ = left_ref.shape
    rows = right_ref.shape[0] // 2
    group = divisor(rows, 6, 2)

    def tile(turn, _):
        q = turn // (rows // group)
        j0 = lax.rem(turn, rows // group) * group
        first = j_half * rows + j0
        sums = [[None] * QUAD for _ in range(group)]
        for k0 in range(0, depth, 16):
            edges = [right_ref[first + j, pl.ds(k0, 16), :].astype(F32) for j in range(group)]
            for n in range(QUAD):
                left = left_ref[q * QUAD + n, pl.ds(k0, 16), :].astype(F32)
                for j in range(group):
                    term = left * edges[j]
                    term = term[:8] + term[8:]
                    sums[j][n] = term if k0 == 0 else sums[j][n] + term
        for j in range(0, group, 2):
            dest = sums_ref.at[q, pl.ds(pl.multiple_of((j0 + j) * QUAD, 8), 8), :]
            total = fold(sums[j] + sums[j + 1])
            dest[...] = total if blocks == 1 else jnp.where(block_of(blocks) == 0, total, total + dest[...])
        return 0

    lax.fori_loop(0, slabs // QUAD * (rows // group), tile, 0)


def assemble(dest_ref, sums_ref, gates_ref, places, j_half):
    half_rows = sums_ref.shape[1] // QUAD
    count = dest_ref.shape[1] // half_rows
    side, place = lax.axis_index("col"), lax.axis_index("row")
    for n, (m0, m1) in enumerate(zip(*places)):
        i = jnp.bitwise_xor(place, jnp.where(side == 0, m0, m1))
        rows = pl.ds(i, half_rows, stride=count)
        dest_ref[0, rows, :] = sums_ref[n // QUAD, pl.ds(n % QUAD, half_rows, stride=QUAD), :]
        dest_ref[1, rows, :] = gates_ref[pl.ds(n * GATE_ROWS + j_half * half_rows, half_rows), :]


def near_kernel(
    length_ref, right_ref, slab_ref, gate_ref, weight_ref, out_gate_ref,
    mate_sums_ref, own_sums_ref, gates_ref, left_ref, norm_ref, *, blocks,
):
    side = lax.axis_index("col")
    project(
        length_ref, slab_ref, gate_ref, weight_ref, out_gate_ref, left_ref, gates_ref, norm_ref,
        right_ref.shape[0] // 2, blocks,
    )
    contract(left_ref, right_ref, 1 - side, mate_sums_ref, blocks)
    contract(left_ref, right_ref, side, own_sums_ref, blocks)


def send_kernel(
    length_ref, right_ref, slab_ref, gate_ref, weight_ref, out_gate_ref, near_sums_ref, near_gates_ref,
    send_ref, left_out_ref, gates_ref, left_ref, sums_ref, norm_ref, *, blocks, near_places, far_places,
):
    flip = 1 - lax.axis_index("col")
    project(
        length_ref, slab_ref, gate_ref, weight_ref, out_gate_ref, left_ref, gates_ref, norm_ref,
        right_ref.shape[0] // 2, blocks,
    )
    left_out_ref[...] = left_ref[...].astype(BF16)
    contract(left_ref, right_ref, flip, sums_ref, blocks)

    def rest():
        assemble(send_ref, near_sums_ref, near_gates_ref, near_places, flip)
        assemble(send_ref, sums_ref, gates_ref, far_places, flip)

    if blocks == 1:
        rest()
    else:
        pl.when(pl.program_id(0) == blocks - 1)(rest)


def keep_kernel(
    right_ref, left_ref, gates_ref, near_sums_ref, near_gates_ref, keep_ref, sums_ref,
    *, blocks, near_places, far_places,
):
    side = lax.axis_index("col")
    contract(left_ref, right_ref, side, sums_ref, blocks)

    def rest():
        assemble(keep_ref, near_sums_ref, near_gates_ref, near_places, side)
        assemble(keep_ref, sums_ref, gates_ref, far_places, side)

    if blocks == 1:
        rest()
    else:
        pl.when(pl.program_id(0) == blocks - 1)(rest)


def last_kernel(keep_ref, got_ref, weight_ref, out_ref, *, half_cols):
    rows_dev = 2 * out_ref.shape[0]
    tri = keep_ref[0] + got_ref[0]
    d = tri - jnp.mean(tri, axis=-1, keepdims=True)
    var = jnp.mean(d * d, axis=-1, keepdims=True)
    n = (d * lax.rsqrt(var + EPS)).astype(BF16)
    projected = jnp.dot(n, weight_ref[...], preferred_element_type=F32)
    mine = lax.axis_index("row") * rows_dev // half_cols == lax.axis_index("col")
    update = projected * jnp.where(mine, keep_ref[1], got_ref[1])
    out_ref[...] = update.astype(BF16).reshape(out_ref.shape)


def passed(x, to):
    count = lax.axis_size("row")
    pairs = []
    for row in range(count):
        for core in range(2):
            if (target := to(row, core)) is not None:
                pairs.append((row * 2 + core, target[0] * 2 + target[1]))
    return lax.ppermute(x, ("row", "col"), pairs)


def doubled(half, count, between):
    steps = doubling(count)
    held, got = half, None
    for step in range(len(steps[0])):
        if step > 0:
            held = jnp.concatenate([held, got], axis=0)
        if step == 1:
            held, made = between(held)
        got = passed(held, lambda row, core: (row ^ steps[core][step], core))
    near = [slots(s[:-1]) for s in steps]
    far = [[m ^ s[-1] for m in held_by] for held_by, s in zip(near, steps)]
    return held, got, near, far, made


def direct(slab, half, between):
    half_cols = half.shape[1]
    side = lax.axis_index("col")

    def out(m):
        return passed(slab, lambda row, core: (row ^ m, 1) if core == 0 else None)

    far = [out(m) for m in (4, 5, 6, 7)]
    beside = out(1)
    both, made = between(jnp.concatenate([slab, beside], axis=0))
    pair = passed(both, lambda row, core: (row ^ 2, 0) if core == 1 else None)
    over = jnp.concatenate([beside[:, :half_cols]] * 2, axis=0)
    over = jnp.where(side == 0, pair[:, half_cols:], over)
    over = passed(over, lambda row, core: (row, 1 - core))
    near0 = jnp.concatenate([half, over[:1], pair[:, :half_cols]], axis=0)
    near1 = jnp.concatenate([half, beside[:, half_cols:], over], axis=0)
    near = jnp.where(side == 0, near0, near1)
    _, far = lax.optimization_barrier((near, far))
    crossed = jnp.concatenate([x[:, :half_cols] for x in far], axis=0)
    crossed = passed(crossed, lambda row, core: (row, 0) if core == 1 else None)
    far = jnp.where(side == 0, crossed, jnp.concatenate([x[:, half_cols:] for x in far], axis=0))
    return near, far, [[0, 1, 2, 3]] * 2, [[4, 5, 6, 7]] * 2, made


def shards(pair_rep, slab_rep, length, weight_a, gate_a, weight_b, gate_b, weight_gate, weight_out):
    rows_dev, half_cols, width = pair_rep.shape
    hidden = weight_a.shape[1]
    count = lax.axis_size("row")
    side = lax.axis_index("col")
    half_rows = rows_dev // 2
    depth = divisor(half_cols, 144, rows_dev)
    blocks = half_cols // depth
    grid = () if blocks == 1 else (blocks,)
    near = count // 2
    hbm = pl.BlockSpec(memory_space=pltpu.HBM)
    smem = pl.BlockSpec(memory_space=pltpu.SMEM)
    vmem = pl.BlockSpec(memory_space=pltpu.VMEM)
    params = pltpu.CompilerParams(vmem_limit_bytes=40 << 20)

    def whole(*shape):
        return vmem if blocks == 1 else pl.BlockSpec(shape, lambda *_: (0,) * len(shape))

    def deep(rows):
        return vmem if blocks == 1 else pl.BlockSpec((rows, depth, width), lambda k: (0, k, 0))

    chunk = divisor(rows_dev, max(2, 1728 // half_cols), 2)
    turns = rows_dev // chunk
    right_call = pl.pallas_call(
        functools.partial(right_kernel, chunk=chunk),
        out_shape=jax.ShapeDtypeStruct((rows_dev, half_cols, hidden), BF16),
        in_specs=[hbm] * 4,
        out_specs=hbm,
        scratch_shapes=[
            pltpu.VMEM((rows_dev, half_cols, width), BF16),
            pltpu.VMEM((rows_dev, half_cols, hidden), BF16),
            pltpu.VMEM((2, width, hidden), BF16),
            pltpu.SMEM((1,), jnp.int32),
            pltpu.SemaphoreType.DMA((3,)),
            pltpu.SemaphoreType.DMA((turns,)),
            pltpu.SemaphoreType.DMA((turns,)),
        ],
        compiler_params=pltpu.CompilerParams(vmem_limit_bytes=58 << 20),
        cost_estimate=pl.CostEstimate(
            flops=2 * rows_dev * half_cols * width * hidden * 6,
            bytes_accessed=4 * rows_dev * half_cols * width,
            transcendentals=2 * rows_dev * half_cols * width,
        ),
        name="right",
    )

    def between(held):
        made, held = lax.optimization_barrier((right_call(length, pair_rep, weight_b, gate_b), held))
        return held, made

    half = lax.dynamic_slice_in_dim(slab_rep, side * half_cols, half_cols, 1)
    gather = functools.partial(direct, slab_rep) if count == 8 else functools.partial(doubled, count=count)
    near_slabs, far_slabs, near_places, far_places, right = gather(half, between=between)

    sums = jax.ShapeDtypeStruct((near // QUAD, half_rows * QUAD, hidden), F32)
    gates = jax.ShapeDtypeStruct((near * GATE_ROWS, width), F32)
    swapped = jax.ShapeDtypeStruct((2, half_rows * count, hidden), F32)
    norm = pltpu.VMEM((QUAD, depth + GATE_ROWS, width), F32)
    left_f32 = pltpu.VMEM((near, depth, hidden), F32)
    cost = pl.CostEstimate(
        flops=2 * rows_dev * half_cols * near * hidden,
        bytes_accessed=2 * rows_dev * half_cols * width,
        transcendentals=near * half_cols * width,
    )
    weights = [whole(width, hidden), whole(width, hidden), whole(width, width)]

    near_mate, near_own, near_gates = pl.pallas_call(
        functools.partial(near_kernel, blocks=blocks),
        out_shape=(sums, sums, gates),
        grid=grid,
        in_specs=[smem, deep(rows_dev), deep(near)] + weights,
        out_specs=(whole(*sums.shape), whole(*sums.shape), whole(*gates.shape)),
        scratch_shapes=[left_f32, norm],
        compiler_params=params,
        cost_estimate=cost,
        name="near",
    )(length, right, near_slabs, gate_a, weight_a, weight_gate)

    send, left, far_gates = pl.pallas_call(
        functools.partial(send_kernel, blocks=blocks, near_places=near_places, far_places=far_places),
        out_shape=(swapped, jax.ShapeDtypeStruct((near, half_cols, hidden), BF16), gates),
        grid=grid,
        in_specs=[smem, deep(rows_dev), deep(near)] + weights + [whole(*sums.shape), whole(*gates.shape)],
        out_specs=(whole(*swapped.shape), deep(near), whole(*gates.shape)),
        scratch_shapes=[left_f32, pltpu.VMEM(sums.shape, F32), norm],
        compiler_params=params,
        name="send",
    )(length, right, far_slabs, gate_a, weight_a, weight_gate, near_mate, near_gates)

    swap = passed(send, lambda row, core: (row, 1 - core))

    keep = pl.pallas_call(
        functools.partial(keep_kernel, blocks=blocks, near_places=near_places, far_places=far_places),
        out_shape=swapped,
        grid=grid,
        in_specs=[deep(rows_dev), deep(near), whole(*gates.shape), whole(*sums.shape), whole(*gates.shape)],
        out_specs=whole(*swapped.shape),
        scratch_shapes=[pltpu.VMEM(sums.shape, F32)],
        compiler_params=params,
        cost_estimate=cost,
        name="keep",
    )(right, left, far_gates, near_own, near_gates)

    update = pl.pallas_call(
        functools.partial(last_kernel, half_cols=half_cols),
        out_shape=jax.ShapeDtypeStruct((half_rows, count, width), BF16),
        in_specs=[vmem, vmem, vmem],
        out_specs=vmem,
        compiler_params=pltpu.CompilerParams(vmem_limit_bytes=32 << 20),
        name="last",
    )(keep, swap, weight_out)
    return jnp.transpose(update, (1, 0, 2))


def solution(mesh):
    placed = (
        P(("groups", "row"), "col", None),
        P(("groups", "row"), None, None),
        P("groups"),
        P(),
        P(),
        P(),
        P(),
        P(),
        P(),
    )
    return jax.shard_map(
        shards,
        mesh=mesh,
        in_specs=placed,
        out_specs=P("groups", ("row", "col"), None),
        check_vma=False,
    )
```

```python
import functools

import jax
import jax.numpy as jnp
from jax import lax
from jax.experimental import pallas as pl
from jax.experimental.pallas import tpu as pltpu
from jax.sharding import PartitionSpec as P

EPS = 1e-05
F32 = jnp.float32
BF16 = jnp.bfloat16


def divisor(total, limit, step=1):
    return max(d for d in range(step, total + 1, step) if total % d == 0 and (d <= limit or d == step))


def centering(width):
    row = lax.broadcasted_iota(jnp.int32, (2 * width, 2 * width), 0)
    col = lax.broadcasted_iota(jnp.int32, (2 * width, 2 * width), 1)
    share = jnp.where((row < width) == (col < width), 1.0 / width, 0.0)
    center = jnp.where(row == col, 1.0, 0.0) - share
    return center.astype(BF16), share.astype(BF16)


def normed(first, second, center, share):
    wide = jnp.concatenate([first, second], axis=1)
    d = jnp.dot(wide, center, preferred_element_type=F32)
    var = jnp.dot((d * d).astype(BF16), share, preferred_element_type=F32)
    return (d * lax.rsqrt(var + EPS)).astype(BF16)


def gated(n, both):
    width = both.shape[1] // 2
    y = jnp.dot(n, both, preferred_element_type=F32)
    value = y[:, width:]
    return value + value * jnp.tanh(y[:, :width])


def right_kernel(
    length_ref, pair_ref, weight_ref, gate_ref, out_ref, x_ref, y_ref, w_ref, count_ref, small_sems, in_sems, out_sems,
    *, chunk,
):
    rows, cols, width = pair_ref.shape
    turns = rows // chunk

    def piece(turn, src, dst, sems):
        here = pl.ds(turn * chunk, chunk)
        return pltpu.make_async_copy(src.at[here], dst.at[here], sems.at[turn])

    small = [
        pltpu.make_async_copy(src, dst, small_sems.at[n])
        for n, (src, dst) in enumerate(
            ((length_ref, count_ref), (gate_ref, w_ref.at[0]), (weight_ref, w_ref.at[1]))
        )
    ]
    for copy in small:
        copy.start()
    for turn in range(turns):
        piece(turn, pair_ref, x_ref, in_sems).start()
    for copy in small:
        copy.wait()
    half = jnp.asarray(0.5, BF16)
    both = jnp.concatenate([w_ref[0] * half, w_ref[1] * half], axis=1)
    live = count_ref[0]
    first_j = lax.axis_index("row") * rows
    center, share = centering(width)
    k = lax.axis_index("col") * cols + lax.broadcasted_iota(jnp.int32, (cols, width), 0)

    def some(turn, _):
        piece(turn, pair_ref, x_ref, in_sems).wait()
        j0 = turn * chunk
        x = x_ref[pl.ds(j0, chunk)].reshape(2, chunk * cols // 2, width)
        n = normed(x[0], x[1], center, share)
        for part in range(2):
            edge = gated(n[:, part * width : (part + 1) * width], both).reshape(chunk // 2, cols, width)
            for r in range(chunk // 2):
                j = j0 + part * (chunk // 2) + r
                reach = jnp.where(first_j + j < live, live, 0)
                y_ref[j] = jnp.where(k < reach, edge[r], 0.0).astype(BF16)
        piece(turn, y_ref, out_ref, out_sems).start()
        return 0

    lax.fori_loop(0, turns, some, 0)
    for turn in range(turns):
        piece(turn, y_ref, out_ref, out_sems).wait()


def fold(parts):
    place = lax.broadcasted_iota(jnp.int32, parts[0].shape, 0)
    for step in (1, 2, 4):
        here = (place & step) == 0
        parts = [
            jnp.where(here, a, b) + pltpu.roll(jnp.where(here, b, a), 8 - step, 0)
            for a, b in zip(parts[0::2], parts[1::2])
        ]
    return parts[0]


def block_of(blocks):
    return 0 if blocks == 1 else pl.program_id(0)


def only(condition, blocks, body):
    if blocks == 1:
        body()
    else:
        pl.when(condition)(body)


def contract(left_ref, right_ref, j_half, dest_ref, blocks):
    slabs, depth, _ = left_ref.shape
    rows = right_ref.shape[0] // 2
    group = divisor(rows, 3)

    def tile(turn, _):
        i0 = turn // (rows // group) * 8
        j0 = lax.rem(turn, rows // group) * group
        first = j_half * rows + j0
        sums = [[None] * 8 for _ in range(group)]
        for k0 in range(0, depth, 16):
            edges = [right_ref[first + j, pl.ds(k0, 16), :].astype(F32) for j in range(group)]
            for i in range(8):
                left = left_ref[i0 + i, pl.ds(k0, 16), :].astype(F32)
                for j in range(group):
                    term = left * edges[j]
                    term = term[:8] + term[8:]
                    sums[j][i] = term if k0 == 0 else sums[j][i] + term
        for j in range(group):
            dest = dest_ref.at[0, pl.ds(pl.multiple_of((j0 + j) * slabs + i0, 8), 8), :]
            total = fold(sums[j])
            dest[...] = total if blocks == 1 else jnp.where(block_of(blocks) == 0, total, total + dest[...])
        return 0

    lax.fori_loop(0, slabs // 8 * (rows // group), tile, 0)


def send_kernel(
    length_ref, right_ref, slab_ref, gate_ref, weight_ref, out_gate_ref,
    send_ref, left_ref, own_gates_ref, norm_ref, *, blocks,
):
    slabs, depth, width = slab_ref.shape
    half_rows = right_ref.shape[0] // 2
    half_cols = depth * blocks
    side = lax.axis_index("col")
    half = jnp.asarray(0.5, BF16)
    center, share = centering(width)
    both = jnp.concatenate([gate_ref[...] * half, weight_ref[...] * half], axis=1)
    first_k = side * half_cols + block_of(blocks) * depth
    live = first_k + lax.broadcasted_iota(jnp.int32, (depth, width), 0) < length_ref[0]

    def quad(q):
        s = q * 4
        x = slab_ref[pl.ds(s, 4)].reshape(2, 2 * depth, width)
        n = normed(x[0], x[1], center, share)
        for part in range(2):
            own = n[:, part * width : (part + 1) * width]
            edge = gated(own, both)
            norm_ref[pl.ds(pl.multiple_of((s + 2 * part) * depth, 16), 2 * depth), :] = own.astype(F32)
            for r in range(2):
                kept = jnp.where(live, edge[r * depth : (r + 1) * depth], 0.0)
                left_ref[s + 2 * part + r] = kept.astype(BF16).astype(left_ref.dtype)

    if slabs <= 8:
        for q in range(slabs // 4):
            quad(q)
    else:
        pl.loop(0, slabs // 4)(quad)

    first_j = lax.rem(lax.axis_index("row") * (2 * half_rows), half_cols)
    start = lax.rem(first_j, depth)

    def gates():
        for place, dest in ((1 - side, send_ref.at[1]), (side, own_gates_ref)):
            rows = [
                norm_ref[pl.ds(start + place * half_rows + j, slabs, stride=depth), :] for j in range(half_rows)
            ]
            rows = jnp.concatenate(rows, axis=0).astype(BF16)
            y = jnp.dot(rows, out_gate_ref[...] * half, preferred_element_type=F32)
            dest[...] = (0.5 + 0.5 * jnp.tanh(y)).astype(BF16).astype(F32)

    only(block_of(blocks) == first_j // depth, blocks, gates)
    contract(left_ref, right_ref, 1 - side, send_ref, blocks)


def keep_kernel(right_ref, left_ref, keep_ref, *, blocks):
    contract(left_ref, right_ref, lax.axis_index("col"), keep_ref, blocks)


def last_kernel(keep_ref, own_gates_ref, got_ref, weight_ref, out_ref, *, half_cols):
    rows_dev = 2 * out_ref.shape[0]
    tri = keep_ref[0] + got_ref[0]
    d = tri - jnp.mean(tri, axis=-1, keepdims=True)
    var = jnp.mean(d * d, axis=-1, keepdims=True)
    n = (d * lax.rsqrt(var + EPS)).astype(BF16)
    projected = jnp.dot(n, weight_ref[...], preferred_element_type=F32)
    mine = lax.axis_index("row") * rows_dev // half_cols == lax.axis_index("col")
    update = projected * jnp.where(mine, own_gates_ref[...], got_ref[1])
    out_ref[...] = update.astype(BF16).reshape(out_ref.shape)


def spread_kernel(slab_ref, out_ref):
    count, half_cols, _ = out_ref.shape
    own = slab_ref[0, pl.ds(pl.multiple_of(lax.axis_index("col") * half_cols, 16), half_cols), :]
    for row in range(count):
        out_ref[row] = own


def shards(pair_rep, slab_rep, length, weight_a, gate_a, weight_b, gate_b, weight_gate, weight_out):
    rows_dev, half_cols, width = pair_rep.shape
    hidden = weight_a.shape[1]
    count = lax.axis_size("row")
    half_rows = rows_dev // 2
    depth = divisor(half_cols, 144, rows_dev)
    blocks = half_cols // depth
    grid = () if blocks == 1 else (blocks,)
    hbm = pl.BlockSpec(memory_space=pltpu.HBM)
    smem = pl.BlockSpec(memory_space=pltpu.SMEM)
    vmem = pl.BlockSpec(memory_space=pltpu.VMEM)
    params = pltpu.CompilerParams(vmem_limit_bytes=40 << 20)

    def whole(*shape):
        return vmem if blocks == 1 else pl.BlockSpec(shape, lambda *_: (0,) * len(shape))

    def deep(rows):
        return vmem if blocks == 1 else pl.BlockSpec((rows, depth, width), lambda k: (0, k, 0))

    spread = pl.pallas_call(
        spread_kernel,
        out_shape=jax.ShapeDtypeStruct((count, half_cols, width), BF16),
        in_specs=[vmem],
        out_specs=vmem,
        compiler_params=params,
        name="spread",
    )(slab_rep)
    spread, length = lax.optimization_barrier((spread, length))
    slabs = lax.all_to_all(spread, "row", split_axis=0, concat_axis=0, tiled=True)

    chunk = divisor(rows_dev, max(2, 1728 // half_cols), 2)
    turns = rows_dev // chunk
    right = pl.pallas_call(
        functools.partial(right_kernel, chunk=chunk),
        out_shape=jax.ShapeDtypeStruct((rows_dev, half_cols, hidden), BF16),
        in_specs=[hbm] * 4,
        out_specs=hbm,
        scratch_shapes=[
            pltpu.VMEM((rows_dev, half_cols, width), BF16),
            pltpu.VMEM((rows_dev, half_cols, hidden), BF16),
            pltpu.VMEM((2, width, hidden), BF16),
            pltpu.SMEM((1,), jnp.int32),
            pltpu.SemaphoreType.DMA((3,)),
            pltpu.SemaphoreType.DMA((turns,)),
            pltpu.SemaphoreType.DMA((turns,)),
        ],
        compiler_params=pltpu.CompilerParams(vmem_limit_bytes=58 << 20),
        cost_estimate=pl.CostEstimate(
            flops=2 * rows_dev * half_cols * width * hidden * 6,
            bytes_accessed=4 * rows_dev * half_cols * width,
            transcendentals=2 * rows_dev * half_cols * width,
        ),
        name="right",
    )(length, pair_rep, weight_b, gate_b)

    swapped = jax.ShapeDtypeStruct((2, half_rows * count, hidden), F32)
    kept = jax.ShapeDtypeStruct((1, half_rows * count, hidden), F32)
    gates = jax.ShapeDtypeStruct((half_rows * count, width), F32)
    send, left, own_gates = pl.pallas_call(
        functools.partial(send_kernel, blocks=blocks),
        out_shape=(swapped, jax.ShapeDtypeStruct((count, half_cols, hidden), F32 if blocks == 1 else BF16), gates),
        grid=grid,
        in_specs=[
            smem, deep(rows_dev), deep(count), whole(width, hidden), whole(width, hidden), whole(width, width),
        ],
        out_specs=(whole(*swapped.shape), deep(count), whole(*gates.shape)),
        scratch_shapes=[pltpu.VMEM((count * depth, width), F32)],
        compiler_params=params,
        name="send",
    )(length, right, slabs, gate_a, weight_a, weight_gate)

    got = lax.ppermute(send, "col", [(0, 1), (1, 0)])

    keep = pl.pallas_call(
        functools.partial(keep_kernel, blocks=blocks),
        out_shape=kept,
        grid=grid,
        in_specs=[deep(rows_dev), deep(count)],
        out_specs=whole(*kept.shape),
        compiler_params=params,
        cost_estimate=pl.CostEstimate(
            flops=rows_dev * half_cols * count * hidden,
            bytes_accessed=2 * rows_dev * half_cols * width,
            transcendentals=0,
        ),
        name="keep",
    )(right, left)

    update = pl.pallas_call(
        functools.partial(last_kernel, half_cols=half_cols),
        out_shape=jax.ShapeDtypeStruct((half_rows, count, width), BF16),
        in_specs=[vmem] * 4,
        out_specs=vmem,
        compiler_params=pltpu.CompilerParams(vmem_limit_bytes=32 << 20),
        name="last",
    )(keep, own_gates, got, weight_out)
    return jnp.transpose(update, (1, 0, 2))


def solution(mesh):
    placed = (
        P(("groups", "row"), "col", None),
        P(("groups", "row"), None, None),
        P("groups"),
        P(),
        P(),
        P(),
        P(),
        P(),
        P(),
    )
    return jax.shard_map(
        shards,
        mesh=mesh,
        in_specs=placed,
        out_specs=P("groups", ("row", "col"), None),
        check_vma=False,
    )
```

```python
import functools

import jax
import jax.numpy as jnp
from jax import lax
from jax.experimental import pallas as pl
from jax.experimental.pallas import tpu as pltpu
from jax.sharding import PartitionSpec as P

EPS = 1e-05
F32 = jnp.float32
BF16 = jnp.bfloat16
QUAD = 4
GATE_ROWS = 40


def divisor(total, limit, step=1):
    return max(d for d in range(step, total + 1, step) if total % d == 0 and (d <= limit or d == step))


def doubling(count):
    bits = [1 << b for b in reversed(range(count.bit_length() - 1))]
    return bits, bits[-1:] + bits[:-1]


def slots(steps):
    held = [0]
    for step in steps:
        held = held + [m ^ step for m in held]
    return held


def centering(width):
    row = lax.broadcasted_iota(jnp.int32, (2 * width, 2 * width), 0)
    col = lax.broadcasted_iota(jnp.int32, (2 * width, 2 * width), 1)
    share = jnp.where((row < width) == (col < width), 1.0 / width, 0.0)
    center = jnp.where(row == col, 1.0, 0.0) - share
    return center.astype(BF16), share.astype(BF16)


def normed(first, second, center, share):
    wide = jnp.concatenate([first, second], axis=1)
    d = jnp.dot(wide, center, preferred_element_type=F32)
    var = jnp.dot((d * d).astype(BF16), share, preferred_element_type=F32)
    return (d * lax.rsqrt(var + EPS)).astype(BF16)


def gated(n, both):
    width = both.shape[1] // 2
    y = jnp.dot(n, both, preferred_element_type=F32)
    value = y[:, width:]
    return value + value * jnp.tanh(y[:, :width])


def right_kernel(length_ref, weight_ref, gate_ref, pair_ref, out_ref, x_ref, sems, *, chunk):
    rows, cols, width = pair_ref.shape
    turns = rows // chunk

    def piece(turn):
        here = pl.ds(turn * chunk, chunk)
        return pltpu.make_async_copy(pair_ref.at[here], x_ref.at[here], sems.at[turn])

    for turn in range(turns):
        piece(turn).start()
    half = jnp.asarray(0.5, BF16)
    both = jnp.concatenate([gate_ref[...] * half, weight_ref[...] * half], axis=1)
    live = length_ref[0]
    first_j = lax.axis_index("row") * rows
    center, share = centering(width)
    k = lax.axis_index("col") * cols + lax.broadcasted_iota(jnp.int32, (cols, width), 0)

    def some(turn, _):
        piece(turn).wait()
        j0 = turn * chunk
        x = x_ref[pl.ds(j0, chunk)].reshape(2, chunk * cols // 2, width)
        n = normed(x[0], x[1], center, share)
        for part in range(2):
            edge = gated(n[:, part * width : (part + 1) * width], both).reshape(chunk // 2, cols, width)
            for r in range(chunk // 2):
                j = j0 + part * (chunk // 2) + r
                reach = jnp.where(first_j + j < live, live, 0)
                out_ref[j] = jnp.where(k < reach, edge[r], 0.0).astype(BF16)
        return 0

    lax.fori_loop(0, turns, some, 0)


def fold(parts):
    place = lax.broadcasted_iota(jnp.int32, parts[0].shape, 0)
    for step in (1, 2, 4):
        here = (place & step) == 0
        parts = [
            jnp.where(here, a, b) + pltpu.roll(jnp.where(here, b, a), 8 - step, 0)
            for a, b in zip(parts[0::2], parts[1::2])
        ]
    return parts[0]


def block_of(blocks):
    return 0 if blocks == 1 else pl.program_id(0)


def project(length_ref, slab_ref, gate_ref, weight_ref, out_gate_ref, left_ref, gates_ref, norm_ref, half_rows, blocks):
    slabs, depth, width = slab_ref.shape
    k_step = block_of(blocks)
    half_cols = depth * blocks
    half = jnp.asarray(0.5, BF16)
    center, share = centering(width)
    both = jnp.concatenate([gate_ref[...] * half, weight_ref[...] * half], axis=1)
    first_k = lax.axis_index("col") * half_cols + k_step * depth
    live = first_k + lax.broadcasted_iota(jnp.int32, (depth, width), 0) < length_ref[0]
    first_j = lax.rem(lax.axis_index("row") * (2 * half_rows), half_cols)
    start = lax.rem(first_j, depth)

    def quad(q):
        s = q * QUAD
        x = slab_ref[pl.ds(s, QUAD)].reshape(2, 2 * depth, width)
        n = normed(x[0], x[1], center, share)
        for part in range(2):
            own = n[:, part * width : (part + 1) * width]
            edge = gated(own, both)
            for r in range(2):
                here = slice(r * depth, (r + 1) * depth)
                left_ref[s + 2 * part + r] = jnp.where(live, edge[here], 0.0).astype(BF16).astype(F32)
                norm_ref[2 * part + r, pl.ds(0, depth), :] = own[here].astype(F32)

        def gates():
            rows = jnp.concatenate([norm_ref[n, pl.ds(start, GATE_ROWS), :] for n in range(QUAD)], axis=0)
            y = jnp.dot(rows.astype(BF16), out_gate_ref[...] * half, preferred_element_type=F32)
            gate = (0.5 + 0.5 * jnp.tanh(y)).astype(BF16).astype(F32)
            gates_ref[pl.ds(pl.multiple_of(s * GATE_ROWS, 8), QUAD * GATE_ROWS), :] = gate

        if blocks == 1:
            gates()
        else:
            pl.when(k_step == first_j // depth)(gates)

    if slabs == QUAD:
        quad(0)
    else:
        pl.loop(0, slabs // QUAD)(quad)


def contract(left_ref, right_ref, j_half, sums_ref, blocks):
    slabs, depth, _ = left_ref.shape
    rows = right_ref.shape[0] // 2
    group = divisor(rows, 6, 2)

    def tile(turn, _):
        q = turn // (rows // group)
        j0 = lax.rem(turn, rows // group) * group
        first = j_half * rows + j0
        sums = [[None] * QUAD for _ in range(group)]
        for k0 in range(0, depth, 16):
            edges = [right_ref[first + j, pl.ds(k0, 16), :].astype(F32) for j in range(group)]
            for n in range(QUAD):
                left = left_ref[q * QUAD + n, pl.ds(k0, 16), :].astype(F32)
                for j in range(group):
                    term = left * edges[j]
                    term = term[:8] + term[8:]
                    sums[j][n] = term if k0 == 0 else sums[j][n] + term
        for j in range(0, group, 2):
            dest = sums_ref.at[q, pl.ds(pl.multiple_of((j0 + j) * QUAD, 8), 8), :]
            total = fold(sums[j] + sums[j + 1])
            dest[...] = total if blocks == 1 else jnp.where(block_of(blocks) == 0, total, total + dest[...])
        return 0

    lax.fori_loop(0, slabs // QUAD * (rows // group), tile, 0)


def assemble(dest_ref, sums_ref, gates_ref, places, j_half):
    half_rows = sums_ref.shape[1] // QUAD
    count = dest_ref.shape[1] // half_rows
    side, place = lax.axis_index("col"), lax.axis_index("row")
    for n, (m0, m1) in enumerate(zip(*places)):
        i = jnp.bitwise_xor(place, jnp.where(side == 0, m0, m1))
        rows = pl.ds(i, half_rows, stride=count)
        dest_ref[0, rows, :] = sums_ref[n // QUAD, pl.ds(n % QUAD, half_rows, stride=QUAD), :]
        dest_ref[1, rows, :] = gates_ref[pl.ds(n * GATE_ROWS + j_half * half_rows, half_rows), :]


def near_kernel(
    length_ref, right_ref, slab_ref, gate_ref, weight_ref, out_gate_ref,
    mate_sums_ref, own_sums_ref, gates_ref, left_ref, norm_ref, *, blocks,
):
    side = lax.axis_index("col")
    project(
        length_ref, slab_ref, gate_ref, weight_ref, out_gate_ref, left_ref, gates_ref, norm_ref,
        right_ref.shape[0] // 2, blocks,
    )
    contract(left_ref, right_ref, 1 - side, mate_sums_ref, blocks)
    contract(left_ref, right_ref, side, own_sums_ref, blocks)


def send_kernel(
    length_ref, right_ref, slab_ref, gate_ref, weight_ref, out_gate_ref, near_sums_ref, near_gates_ref,
    send_ref, left_out_ref, gates_ref, left_ref, sums_ref, norm_ref, *, blocks, near_places, far_places,
):
    flip = 1 - lax.axis_index("col")
    project(
        length_ref, slab_ref, gate_ref, weight_ref, out_gate_ref, left_ref, gates_ref, norm_ref,
        right_ref.shape[0] // 2, blocks,
    )
    left_out_ref[...] = left_ref[...].astype(BF16)
    contract(left_ref, right_ref, flip, sums_ref, blocks)

    def rest():
        assemble(send_ref, near_sums_ref, near_gates_ref, near_places, flip)
        assemble(send_ref, sums_ref, gates_ref, far_places, flip)

    if blocks == 1:
        rest()
    else:
        pl.when(pl.program_id(0) == blocks - 1)(rest)


def keep_kernel(
    right_ref, left_ref, gates_ref, near_sums_ref, near_gates_ref, keep_ref, sums_ref,
    *, blocks, near_places, far_places,
):
    side = lax.axis_index("col")
    contract(left_ref, right_ref, side, sums_ref, blocks)

    def rest():
        assemble(keep_ref, near_sums_ref, near_gates_ref, near_places, side)
        assemble(keep_ref, sums_ref, gates_ref, far_places, side)

    if blocks == 1:
        rest()
    else:
        pl.when(pl.program_id(0) == blocks - 1)(rest)


def last_kernel(keep_ref, got_ref, weight_ref, out_ref, *, half_cols):
    rows_dev = 2 * out_ref.shape[0]
    tri = keep_ref[0] + got_ref[0]
    d = tri - jnp.mean(tri, axis=-1, keepdims=True)
    var = jnp.mean(d * d, axis=-1, keepdims=True)
    n = (d * lax.rsqrt(var + EPS)).astype(BF16)
    projected = jnp.dot(n, weight_ref[...], preferred_element_type=F32)
    mine = lax.axis_index("row") * rows_dev // half_cols == lax.axis_index("col")
    update = projected * jnp.where(mine, keep_ref[1], got_ref[1])
    out_ref[...] = update.astype(BF16).reshape(out_ref.shape)


def passed(x, to):
    count = lax.axis_size("row")
    pairs = []
    for row in range(count):
        for core in range(2):
            if (target := to(row, core)) is not None:
                pairs.append((row * 2 + core, target[0] * 2 + target[1]))
    return lax.ppermute(x, ("row", "col"), pairs)


def doubled(half, count, between):
    steps = doubling(count)
    held, got = half, None
    for step in range(len(steps[0])):
        if step > 0:
            held = jnp.concatenate([held, got], axis=0)
        if step == 1:
            held, made = between(held)
        got = passed(held, lambda row, core: (row ^ steps[core][step], core))
    near = [slots(s[:-1]) for s in steps]
    far = [[m ^ s[-1] for m in held_by] for held_by, s in zip(near, steps)]
    return held, got, near, far, made


def direct(slab, half, between):
    half_cols = half.shape[1]
    side = lax.axis_index("col")

    def out(*m):
        return passed(slab, lambda row, core: (row ^ m[core], core))

    def part(x, which):
        return lax.dynamic_slice_in_dim(x, which * half_cols, half_cols, 1)

    steps = ((3, 2), (5, 4), (7, 6), (1, 1))
    first, second, third, beside = [out(*m) for m in steps]
    over = jnp.concatenate([part(x, 1 - side) for x in (first, second, third)], axis=0)
    over, made = between(over)
    over = passed(over, lambda row, core: (row, 1 - core))
    near = jnp.concatenate([half, part(beside, side), part(first, side), part(second, side)], axis=0)
    far = jnp.concatenate([part(third, side), over], axis=0)
    return near, far, [[0, 1, 3, 5], [0, 1, 2, 4]], [[7, 2, 4, 6], [6, 3, 5, 7]], made


def shards(pair_rep, slab_rep, length, weight_a, gate_a, weight_b, gate_b, weight_gate, weight_out):
    rows_dev, half_cols, width = pair_rep.shape
    hidden = weight_a.shape[1]
    count = lax.axis_size("row")
    side = lax.axis_index("col")
    half_rows = rows_dev // 2
    depth = divisor(half_cols, 144, rows_dev)
    blocks = half_cols // depth
    grid = () if blocks == 1 else (blocks,)
    near = count // 2
    hbm = pl.BlockSpec(memory_space=pltpu.HBM)
    smem = pl.BlockSpec(memory_space=pltpu.SMEM)
    vmem = pl.BlockSpec(memory_space=pltpu.VMEM)
    params = pltpu.CompilerParams(vmem_limit_bytes=40 << 20)

    def whole(*shape):
        return vmem if blocks == 1 else pl.BlockSpec(shape, lambda *_: (0,) * len(shape))

    def deep(rows):
        return vmem if blocks == 1 else pl.BlockSpec((rows, depth, width), lambda k: (0, k, 0))

    chunk = divisor(rows_dev, max(2, 1728 // half_cols), 2)
    turns = rows_dev // chunk
    right_call = pl.pallas_call(
        functools.partial(right_kernel, chunk=chunk),
        out_shape=jax.ShapeDtypeStruct((rows_dev, half_cols, hidden), BF16),
        in_specs=[smem, vmem, vmem, hbm],
        out_specs=vmem,
        scratch_shapes=[pltpu.VMEM((rows_dev, half_cols, width), BF16), pltpu.SemaphoreType.DMA((turns,))],
        compiler_params=pltpu.CompilerParams(vmem_limit_bytes=52 << 20),
        cost_estimate=pl.CostEstimate(
            flops=2 * rows_dev * half_cols * width * hidden * 6,
            bytes_accessed=4 * rows_dev * half_cols * width,
            transcendentals=2 * rows_dev * half_cols * width,
        ),
        name="right",
    )

    def between(held):
        made, held = lax.optimization_barrier((right_call(length, weight_b, gate_b, pair_rep), held))
        return held, made

    half = lax.dynamic_slice_in_dim(slab_rep, side * half_cols, half_cols, 1)
    gather = functools.partial(direct, slab_rep) if count == 8 else functools.partial(doubled, count=count)
    near_slabs, far_slabs, near_places, far_places, right = gather(half, between=between)

    sums = jax.ShapeDtypeStruct((near // QUAD, half_rows * QUAD, hidden), F32)
    gates = jax.ShapeDtypeStruct((near * GATE_ROWS, width), F32)
    swapped = jax.ShapeDtypeStruct((2, half_rows * count, hidden), F32)
    norm = pltpu.VMEM((QUAD, depth + GATE_ROWS, width), F32)
    left_f32 = pltpu.VMEM((near, depth, hidden), F32)
    cost = pl.CostEstimate(
        flops=2 * rows_dev * half_cols * near * hidden,
        bytes_accessed=2 * rows_dev * half_cols * width,
        transcendentals=near * half_cols * width,
    )
    weights = [whole(width, hidden), whole(width, hidden), whole(width, width)]

    near_mate, near_own, near_gates = pl.pallas_call(
        functools.partial(near_kernel, blocks=blocks),
        out_shape=(sums, sums, gates),
        grid=grid,
        in_specs=[smem, deep(rows_dev), deep(near)] + weights,
        out_specs=(whole(*sums.shape), whole(*sums.shape), whole(*gates.shape)),
        scratch_shapes=[left_f32, norm],
        compiler_params=params,
        cost_estimate=cost,
        name="near",
    )(length, right, near_slabs, gate_a, weight_a, weight_gate)

    send, left, far_gates = pl.pallas_call(
        functools.partial(send_kernel, blocks=blocks, near_places=near_places, far_places=far_places),
        out_shape=(swapped, jax.ShapeDtypeStruct((near, half_cols, hidden), BF16), gates),
        grid=grid,
        in_specs=[smem, deep(rows_dev), deep(near)] + weights + [whole(*sums.shape), whole(*gates.shape)],
        out_specs=(whole(*swapped.shape), deep(near), whole(*gates.shape)),
        scratch_shapes=[left_f32, pltpu.VMEM(sums.shape, F32), norm],
        compiler_params=params,
        name="send",
    )(length, right, far_slabs, gate_a, weight_a, weight_gate, near_mate, near_gates)

    swap = passed(send, lambda row, core: (row, 1 - core))

    keep = pl.pallas_call(
        functools.partial(keep_kernel, blocks=blocks, near_places=near_places, far_places=far_places),
        out_shape=swapped,
        grid=grid,
        in_specs=[deep(rows_dev), deep(near), whole(*gates.shape), whole(*sums.shape), whole(*gates.shape)],
        out_specs=whole(*swapped.shape),
        scratch_shapes=[pltpu.VMEM(sums.shape, F32)],
        compiler_params=params,
        cost_estimate=cost,
        name="keep",
    )(right, left, far_gates, near_own, near_gates)

    update = pl.pallas_call(
        functools.partial(last_kernel, half_cols=half_cols),
        out_shape=jax.ShapeDtypeStruct((half_rows, count, width), BF16),
        in_specs=[vmem, vmem, vmem],
        out_specs=vmem,
        compiler_params=pltpu.CompilerParams(vmem_limit_bytes=32 << 20),
        name="last",
    )(keep, swap, weight_out)
    return jnp.transpose(update, (1, 0, 2))


def solution(mesh):
    placed = (
        P(("groups", "row"), "col", None),
        P(("groups", "row"), None, None),
        P("groups"),
        P(),
        P(),
        P(),
        P(),
        P(),
        P(),
    )
    return jax.shard_map(
        shards,
        mesh=mesh,
        in_specs=placed,
        out_specs=P("groups", ("row", "col"), None),
        check_vma=False,
    )
```

```python
import functools

import jax
import jax.numpy as jnp
from jax import lax
from jax.experimental import pallas as pl
from jax.experimental.pallas import tpu as pltpu
from jax.sharding import PartitionSpec as P

EPS = 1e-05
F32 = jnp.float32
BF16 = jnp.bfloat16
QUAD = 4
GATE_ROWS = 40


def divisor(total, limit, step=1):
    return max(d for d in range(step, total + 1, step) if total % d == 0 and (d <= limit or d == step))


def doubling(count):
    bits = [1 << b for b in reversed(range(count.bit_length() - 1))]
    return bits, bits[-1:] + bits[:-1]


def slots(steps):
    held = [0]
    for step in steps:
        held = held + [m ^ step for m in held]
    return held


def centering_kernel(center_ref, share_ref):
    width = center_ref.shape[0] // 2
    row = lax.broadcasted_iota(jnp.int32, (2 * width, 2 * width), 0)
    col = lax.broadcasted_iota(jnp.int32, (2 * width, 2 * width), 1)
    share = jnp.where((row < width) == (col < width), 1.0 / width, 0.0)
    center_ref[...] = (jnp.where(row == col, 1.0, 0.0) - share).astype(BF16)
    share_ref[...] = share.astype(BF16)


def normed(first, second, center, share):
    wide = jnp.concatenate([first, second], axis=1)
    d = jnp.dot(wide, center, preferred_element_type=F32)
    var = jnp.dot((d * d).astype(BF16), share, preferred_element_type=F32)
    return (d * lax.rsqrt(var + EPS)).astype(BF16)


def gated(n, both):
    width = both.shape[1] // 2
    y = jnp.dot(n, both, preferred_element_type=F32)
    value = y[:, width:]
    return value + value * jnp.tanh(y[:, :width])


def right_kernel(center_ref, share_ref, weight_ref, gate_ref, pair_ref, out_ref, *, chunk):
    rows, cols, width = pair_ref.shape
    half = jnp.asarray(0.5, BF16)
    both = jnp.concatenate([gate_ref[...] * half, weight_ref[...] * half], axis=1)

    def some(turn, _):
        j0 = turn * chunk
        x = pair_ref[pl.ds(j0, chunk)].reshape(2, chunk * cols // 2, width)
        n = normed(x[0], x[1], center_ref[...], share_ref[...])
        for part in range(2):
            edge = gated(n[:, part * width : (part + 1) * width], both).astype(BF16)
            out_ref[pl.ds(j0 + part * (chunk // 2), chunk // 2)] = edge.reshape(chunk // 2, cols, width)
        return 0

    lax.fori_loop(0, rows // chunk, some, 0)


def fold(parts):
    place = lax.broadcasted_iota(jnp.int32, parts[0].shape, 0)
    for step in (1, 2, 4):
        here = (place & step) == 0
        parts = [
            jnp.where(here, a, b) + pltpu.roll(jnp.where(here, b, a), 8 - step, 0)
            for a, b in zip(parts[0::2], parts[1::2])
        ]
    return parts[0]


def block_of(blocks):
    return 0 if blocks == 1 else pl.program_id(0)


def project(
    length_ref, center_ref, share_ref, slab_ref, gate_ref, weight_ref, out_gate_ref, left_ref, gates_ref, norm_ref,
    half_rows, blocks,
):
    slabs, depth, width = slab_ref.shape
    k_step = block_of(blocks)
    half_cols = depth * blocks
    half = jnp.asarray(0.5, BF16)
    both = jnp.concatenate([gate_ref[...] * half, weight_ref[...] * half], axis=1)
    first_k = lax.axis_index("col") * half_cols + k_step * depth
    live = first_k + lax.broadcasted_iota(jnp.int32, (depth, width), 0) < length_ref[0]
    first_j = lax.rem(lax.axis_index("row") * (2 * half_rows), half_cols)
    start = lax.rem(first_j, depth)

    def quad(q):
        s = q * QUAD
        x = slab_ref[pl.ds(s, QUAD)].reshape(2, 2 * depth, width)
        n = normed(x[0], x[1], center_ref[...], share_ref[...])
        for part in range(2):
            own = n[:, part * width : (part + 1) * width]
            edge = gated(own, both)
            for r in range(2):
                here = slice(r * depth, (r + 1) * depth)
                left_ref[s + 2 * part + r] = jnp.where(live, edge[here], 0.0).astype(BF16).astype(F32)
                norm_ref[2 * part + r, pl.ds(0, depth), :] = own[here].astype(F32)

        def gates():
            rows = jnp.concatenate([norm_ref[n, pl.ds(start, GATE_ROWS), :] for n in range(QUAD)], axis=0)
            y = jnp.dot(rows.astype(BF16), out_gate_ref[...] * half, preferred_element_type=F32)
            gate = (0.5 + 0.5 * jnp.tanh(y)).astype(BF16).astype(F32)
            gates_ref[pl.ds(pl.multiple_of(s * GATE_ROWS, 8), QUAD * GATE_ROWS), :] = gate

        if blocks == 1:
            gates()
        else:
            pl.when(k_step == first_j // depth)(gates)

    if slabs == QUAD:
        quad(0)
    else:
        pl.loop(0, slabs // QUAD)(quad)


def contract(length_ref, left_ref, right_ref, j_half, sums_ref, blocks):
    slabs, depth, _ = left_ref.shape
    rows = right_ref.shape[0] // 2
    group = divisor(rows, 6, 2)
    live_rows = length_ref[0] - lax.axis_index("row") * (2 * rows)
    second = lax.broadcasted_iota(jnp.int32, (8, left_ref.shape[2]), 0) // QUAD

    def tile(turn, _):
        q = turn // (rows // group)
        j0 = lax.rem(turn, rows // group) * group
        first = j_half * rows + j0
        sums = [[None] * QUAD for _ in range(group)]
        for k0 in range(0, depth, 16):
            edges = [right_ref[first + j, pl.ds(k0, 16), :].astype(F32) for j in range(group)]
            for n in range(QUAD):
                left = left_ref[q * QUAD + n, pl.ds(k0, 16), :].astype(F32)
                for j in range(group):
                    term = left * edges[j]
                    term = term[:8] + term[8:]
                    sums[j][n] = term if k0 == 0 else sums[j][n] + term
        for j in range(0, group, 2):
            dest = sums_ref.at[q, pl.ds(pl.multiple_of((j0 + j) * QUAD, 8), 8), :]
            total = jnp.where(first + j + second < live_rows, fold(sums[j] + sums[j + 1]), 0.0)
            dest[...] = total if blocks == 1 else jnp.where(block_of(blocks) == 0, total, total + dest[...])
        return 0

    lax.fori_loop(0, slabs // QUAD * (rows // group), tile, 0)


def assemble(dest_ref, sums_ref, gates_ref, places, j_half):
    half_rows = sums_ref.shape[1] // QUAD
    count = dest_ref.shape[1] // half_rows
    side, place = lax.axis_index("col"), lax.axis_index("row")
    for n, (m0, m1) in enumerate(zip(*places)):
        i = jnp.bitwise_xor(place, jnp.where(side == 0, m0, m1))
        rows = pl.ds(i, half_rows, stride=count)
        dest_ref[0, rows, :] = sums_ref[n // QUAD, pl.ds(n % QUAD, half_rows, stride=QUAD), :]
        dest_ref[1, rows, :] = gates_ref[pl.ds(n * GATE_ROWS + j_half * half_rows, half_rows), :]


def near_kernel(
    length_ref, center_ref, share_ref, right_ref, slab_ref, gate_ref, weight_ref, out_gate_ref,
    mate_sums_ref, own_sums_ref, gates_ref, left_ref, norm_ref, *, blocks,
):
    side = lax.axis_index("col")
    project(
        length_ref, center_ref, share_ref, slab_ref, gate_ref, weight_ref, out_gate_ref,
        left_ref, gates_ref, norm_ref, right_ref.shape[0] // 2, blocks,
    )
    contract(length_ref, left_ref, right_ref, 1 - side, mate_sums_ref, blocks)
    contract(length_ref, left_ref, right_ref, side, own_sums_ref, blocks)


def send_kernel(
    length_ref, center_ref, share_ref, right_ref, slab_ref, gate_ref, weight_ref, out_gate_ref, near_sums_ref, near_gates_ref,
    send_ref, left_out_ref, gates_ref, left_ref, sums_ref, norm_ref, *, blocks, near_places, far_places,
):
    flip = 1 - lax.axis_index("col")
    project(
        length_ref, center_ref, share_ref, slab_ref, gate_ref, weight_ref, out_gate_ref,
        left_ref, gates_ref, norm_ref, right_ref.shape[0] // 2, blocks,
    )
    left_out_ref[...] = left_ref[...].astype(BF16)
    contract(length_ref, left_ref, right_ref, flip, sums_ref, blocks)

    def rest():
        assemble(send_ref, near_sums_ref, near_gates_ref, near_places, flip)
        assemble(send_ref, sums_ref, gates_ref, far_places, flip)

    if blocks == 1:
        rest()
    else:
        pl.when(pl.program_id(0) == blocks - 1)(rest)


def keep_kernel(
    length_ref, right_ref, left_ref, gates_ref, near_sums_ref, near_gates_ref, keep_ref, sums_ref,
    *, blocks, near_places, far_places,
):
    side = lax.axis_index("col")
    contract(length_ref, left_ref, right_ref, side, sums_ref, blocks)

    def rest():
        assemble(keep_ref, near_sums_ref, near_gates_ref, near_places, side)
        assemble(keep_ref, sums_ref, gates_ref, far_places, side)

    if blocks == 1:
        rest()
    else:
        pl.when(pl.program_id(0) == blocks - 1)(rest)


def last_kernel(keep_ref, got_ref, weight_ref, out_ref, *, half_cols):
    rows_dev = 2 * out_ref.shape[0]
    tri = keep_ref[0] + got_ref[0]
    d = tri - jnp.mean(tri, axis=-1, keepdims=True)
    var = jnp.mean(d * d, axis=-1, keepdims=True)
    n = (d * lax.rsqrt(var + EPS)).astype(BF16)
    projected = jnp.dot(n, weight_ref[...], preferred_element_type=F32)
    mine = lax.axis_index("row") * rows_dev // half_cols == lax.axis_index("col")
    update = projected * jnp.where(mine, keep_ref[1], got_ref[1])
    out_ref[...] = update.astype(BF16).reshape(out_ref.shape)


def passed(x, to):
    count = lax.axis_size("row")
    pairs = []
    for row in range(count):
        for core in range(2):
            if (target := to(row, core)) is not None:
                pairs.append((row * 2 + core, target[0] * 2 + target[1]))
    return lax.ppermute(x, ("row", "col"), pairs)


def doubled(half, count, between):
    steps = doubling(count)
    held, got = half, None
    for step in range(len(steps[0])):
        if step > 0:
            held = jnp.concatenate([held, got], axis=0)
        if step == 1:
            held, made = between(held)
        got = passed(held, lambda row, core: (row ^ steps[core][step], core))
    near = [slots(s[:-1]) for s in steps]
    far = [[m ^ s[-1] for m in held_by] for held_by, s in zip(near, steps)]
    return held, got, near, far, made


def direct(slab, half, between):
    half_cols = half.shape[1]
    side = lax.axis_index("col")

    def out(*m):
        return passed(slab, lambda row, core: (row ^ m[core], core))

    def part(x, which):
        return lax.dynamic_slice_in_dim(x, which * half_cols, half_cols, 1)

    steps = ((2, 3), (4, 5), (7, 6), (1, 1))
    first, second, third, beside = [out(*m) for m in steps]
    over = jnp.concatenate([part(x, 1 - side) for x in (first, second, third)], axis=0)
    over, made = between(over)
    over = passed(over, lambda row, core: (row, 1 - core))
    near = jnp.concatenate([half, part(beside, side), part(first, side), part(second, side)], axis=0)
    far = jnp.concatenate([part(third, side), over], axis=0)
    return near, far, [[0, 1, 2, 4], [0, 1, 3, 5]], [[7, 3, 5, 6], [6, 2, 4, 7]], made


def shards(pair_rep, slab_rep, length, weight_a, gate_a, weight_b, gate_b, weight_gate, weight_out):
    rows_dev, half_cols, width = pair_rep.shape
    hidden = weight_a.shape[1]
    count = lax.axis_size("row")
    side = lax.axis_index("col")
    half_rows = rows_dev // 2
    depth = divisor(half_cols, 144, rows_dev)
    blocks = half_cols // depth
    grid = () if blocks == 1 else (blocks,)
    near = count // 2
    smem = pl.BlockSpec(memory_space=pltpu.SMEM)
    vmem = pl.BlockSpec(memory_space=pltpu.VMEM)
    params = pltpu.CompilerParams(vmem_limit_bytes=40 << 20)

    def whole(*shape):
        return vmem if blocks == 1 else pl.BlockSpec(shape, lambda *_: (0,) * len(shape))

    def deep(rows):
        return vmem if blocks == 1 else pl.BlockSpec((rows, depth, width), lambda k: (0, k, 0))

    chunk = divisor(rows_dev, max(2, 1728 // half_cols), 2)
    square = jax.ShapeDtypeStruct((2 * width, 2 * width), BF16)
    center, share = pl.pallas_call(
        centering_kernel,
        out_shape=(square, square),
        out_specs=(vmem, vmem),
        compiler_params=pltpu.CompilerParams(vmem_limit_bytes=8 << 20),
        cost_estimate=pl.CostEstimate(flops=4 * 10**9, bytes_accessed=8 * 10**6, transcendentals=0),
        name="centering",
    )()
    right_call = pl.pallas_call(
        functools.partial(right_kernel, chunk=chunk),
        out_shape=jax.ShapeDtypeStruct((rows_dev, half_cols, hidden), BF16),
        in_specs=[vmem] * 5,
        out_specs=vmem,
        compiler_params=params,
        cost_estimate=pl.CostEstimate(
            flops=2 * rows_dev * half_cols * width * hidden * 6,
            bytes_accessed=4 * rows_dev * half_cols * width,
            transcendentals=2 * rows_dev * half_cols * width,
        ),
        name="right",
    )

    def between(held):
        made, held = lax.optimization_barrier((right_call(center, share, weight_b, gate_b, pair_rep), held))
        return held, made

    half = lax.dynamic_slice_in_dim(slab_rep, side * half_cols, half_cols, 1)
    gather = functools.partial(direct, slab_rep) if count == 8 else functools.partial(doubled, count=count)
    near_slabs, far_slabs, near_places, far_places, right = gather(half, between=between)

    sums = jax.ShapeDtypeStruct((near // QUAD, half_rows * QUAD, hidden), F32)
    gates = jax.ShapeDtypeStruct((near * GATE_ROWS, width), F32)
    swapped = jax.ShapeDtypeStruct((2, half_rows * count, hidden), F32)
    norm = pltpu.VMEM((QUAD, depth + GATE_ROWS, width), F32)
    left_f32 = pltpu.VMEM((near, depth, hidden), F32)
    cost = pl.CostEstimate(
        flops=2 * rows_dev * half_cols * near * hidden,
        bytes_accessed=2 * rows_dev * half_cols * width,
        transcendentals=near * half_cols * width,
    )
    squares = [whole(*square.shape)] * 2
    weights = [whole(width, hidden), whole(width, hidden), whole(width, width)]

    near_mate, near_own, near_gates = pl.pallas_call(
        functools.partial(near_kernel, blocks=blocks),
        out_shape=(sums, sums, gates),
        grid=grid,
        in_specs=[smem] + squares + [deep(rows_dev), deep(near)] + weights,
        out_specs=(whole(*sums.shape), whole(*sums.shape), whole(*gates.shape)),
        scratch_shapes=[left_f32, norm],
        compiler_params=params,
        cost_estimate=cost,
        name="near",
    )(length, center, share, right, near_slabs, gate_a, weight_a, weight_gate)

    send, left, far_gates = pl.pallas_call(
        functools.partial(send_kernel, blocks=blocks, near_places=near_places, far_places=far_places),
        out_shape=(swapped, jax.ShapeDtypeStruct((near, half_cols, hidden), BF16), gates),
        grid=grid,
        in_specs=[smem] + squares + [deep(rows_dev), deep(near)] + weights + [whole(*sums.shape), whole(*gates.shape)],
        out_specs=(whole(*swapped.shape), deep(near), whole(*gates.shape)),
        scratch_shapes=[left_f32, pltpu.VMEM(sums.shape, F32), norm],
        compiler_params=params,
        name="send",
    )(length, center, share, right, far_slabs, gate_a, weight_a, weight_gate, near_mate, near_gates)

    swap = passed(send, lambda row, core: (row, 1 - core))

    keep = pl.pallas_call(
        functools.partial(keep_kernel, blocks=blocks, near_places=near_places, far_places=far_places),
        out_shape=swapped,
        grid=grid,
        in_specs=[smem, deep(rows_dev), deep(near), whole(*gates.shape), whole(*sums.shape), whole(*gates.shape)],
        out_specs=whole(*swapped.shape),
        scratch_shapes=[pltpu.VMEM(sums.shape, F32)],
        compiler_params=params,
        cost_estimate=cost,
        name="keep",
    )(length, right, left, far_gates, near_own, near_gates)

    update = pl.pallas_call(
        functools.partial(last_kernel, half_cols=half_cols),
        out_shape=jax.ShapeDtypeStruct((half_rows, count, width), BF16),
        in_specs=[vmem, vmem, vmem],
        out_specs=vmem,
        compiler_params=pltpu.CompilerParams(vmem_limit_bytes=32 << 20),
        name="last",
    )(keep, swap, weight_out)
    return jnp.transpose(update, (1, 0, 2))


def solution(mesh):
    placed = (
        P(("groups", "row"), "col", None),
        P(("groups", "row"), None, None),
        P("groups"),
        P(),
        P(),
        P(),
        P(),
        P(),
        P(),
    )
    return jax.shard_map(
        shards,
        mesh=mesh,
        in_specs=placed,
        out_specs=P("groups", ("row", "col"), None),
        check_vma=False,
    )
```

```python
import functools

import jax
import jax.numpy as jnp
from jax import lax
from jax.experimental import pallas as pl
from jax.experimental.pallas import tpu as pltpu
from jax.sharding import PartitionSpec as P

EPS = 1e-05
F32 = jnp.float32
BF16 = jnp.bfloat16
QUAD = 4
GATE_ROWS = 40


def divisor(total, limit, step=1):
    return max(d for d in range(step, total + 1, step) if total % d == 0 and (d <= limit or d == step))


def doubling(count):
    bits = [1 << b for b in reversed(range(count.bit_length() - 1))]
    return bits, bits[-1:] + bits[:-1]


def slots(steps):
    held = [0]
    for step in steps:
        held = held + [m ^ step for m in held]
    return held


def centering_kernel(center_ref, share_ref):
    width = center_ref.shape[0] // 2
    row = lax.broadcasted_iota(jnp.int32, (2 * width, 2 * width), 0)
    col = lax.broadcasted_iota(jnp.int32, (2 * width, 2 * width), 1)
    share = jnp.where((row < width) == (col < width), 1.0 / width, 0.0)
    center_ref[...] = (jnp.where(row == col, 1.0, 0.0) - share).astype(BF16)
    share_ref[...] = share.astype(BF16)


def normed(first, second, center, share):
    wide = jnp.concatenate([first, second], axis=1)
    d = jnp.dot(wide, center, preferred_element_type=F32)
    var = jnp.dot((d * d).astype(BF16), share, preferred_element_type=F32)
    return (d * lax.rsqrt(var + EPS)).astype(BF16)


def gated(n, both):
    width = both.shape[1] // 2
    y = jnp.dot(n, both, preferred_element_type=F32)
    value = y[:, width:]
    return value + value * jnp.tanh(y[:, :width])


def right_kernel(center_ref, share_ref, weight_ref, gate_ref, pair_ref, out_ref, *, chunk):
    rows, cols, width = pair_ref.shape
    half = jnp.asarray(0.5, BF16)
    both = jnp.concatenate([gate_ref[...] * half, weight_ref[...] * half], axis=1)

    def some(turn, _):
        j0 = turn * chunk
        x = pair_ref[pl.ds(j0, chunk)].reshape(2, chunk * cols // 2, width)
        n = normed(x[0], x[1], center_ref[...], share_ref[...])
        for part in range(2):
            edge = gated(n[:, part * width : (part + 1) * width], both).astype(BF16)
            out_ref[pl.ds(j0 + part * (chunk // 2), chunk // 2)] = edge.reshape(chunk // 2, cols, width)
        return 0

    lax.fori_loop(0, rows // chunk, some, 0)


def fold(parts):
    place = lax.broadcasted_iota(jnp.int32, parts[0].shape, 0)
    for step in (1, 2, 4):
        here = (place & step) == 0
        parts = [
            jnp.where(here, a, b) + pltpu.roll(jnp.where(here, b, a), 8 - step, 0)
            for a, b in zip(parts[0::2], parts[1::2])
        ]
    return parts[0]


def block_of(blocks):
    return 0 if blocks == 1 else pl.program_id(0)


def project(
    length_ref, center_ref, share_ref, slab_ref, gate_ref, weight_ref, out_gate_ref, left_ref, gates_ref, norm_ref,
    half_rows, blocks,
):
    slabs, depth, width = slab_ref.shape
    k_step = block_of(blocks)
    half_cols = depth * blocks
    half = jnp.asarray(0.5, BF16)
    both = jnp.concatenate([gate_ref[...] * half, weight_ref[...] * half], axis=1)
    first_k = lax.axis_index("col") * half_cols + k_step * depth
    live = first_k + lax.broadcasted_iota(jnp.int32, (depth, width), 0) < length_ref[0]
    first_j = lax.rem(lax.axis_index("row") * (2 * half_rows), half_cols)
    start = lax.rem(first_j, depth)

    def quad(q):
        s = q * QUAD
        x = slab_ref[pl.ds(s, QUAD)].reshape(2, 2 * depth, width)
        n = normed(x[0], x[1], center_ref[...], share_ref[...])
        for part in range(2):
            own = n[:, part * width : (part + 1) * width]
            edge = gated(own, both)
            for r in range(2):
                here = slice(r * depth, (r + 1) * depth)
                left_ref[s + 2 * part + r] = jnp.where(live, edge[here], 0.0).astype(BF16).astype(F32)
                norm_ref[2 * part + r, pl.ds(0, depth), :] = own[here].astype(F32)

        def gates():
            rows = jnp.concatenate([norm_ref[n, pl.ds(start, GATE_ROWS), :] for n in range(QUAD)], axis=0)
            y = jnp.dot(rows.astype(BF16), out_gate_ref[...] * half, preferred_element_type=F32)
            gate = (0.5 + 0.5 * jnp.tanh(y)).astype(BF16).astype(F32)
            gates_ref[pl.ds(pl.multiple_of(s * GATE_ROWS, 8), QUAD * GATE_ROWS), :] = gate

        if blocks == 1:
            gates()
        else:
            pl.when(k_step == first_j // depth)(gates)

    if slabs == QUAD:
        quad(0)
    else:
        pl.loop(0, slabs // QUAD)(quad)


def contract(length_ref, left_ref, right_ref, j_half, sums_ref, blocks):
    slabs, depth, _ = left_ref.shape
    rows = right_ref.shape[0] // 2
    group = divisor(rows, 6, 2)
    live_rows = length_ref[0] - lax.axis_index("row") * (2 * rows)
    second = lax.broadcasted_iota(jnp.int32, (8, left_ref.shape[2]), 0) // QUAD

    def tile(turn, _):
        q = turn // (rows // group)
        j0 = lax.rem(turn, rows // group) * group
        first = j_half * rows + j0
        sums = [[None] * QUAD for _ in range(group)]
        for k0 in range(0, depth, 16):
            edges = [right_ref[first + j, pl.ds(k0, 16), :].astype(F32) for j in range(group)]
            for n in range(QUAD):
                left = left_ref[q * QUAD + n, pl.ds(k0, 16), :].astype(F32)
                for j in range(group):
                    term = left * edges[j]
                    term = term[:8] + term[8:]
                    sums[j][n] = term if k0 == 0 else sums[j][n] + term
        for j in range(0, group, 2):
            dest = sums_ref.at[q, pl.ds(pl.multiple_of((j0 + j) * QUAD, 8), 8), :]
            total = jnp.where(first + j + second < live_rows, fold(sums[j] + sums[j + 1]), 0.0)
            dest[...] = total if blocks == 1 else jnp.where(block_of(blocks) == 0, total, total + dest[...])
        return 0

    lax.fori_loop(0, slabs // QUAD * (rows // group), tile, 0)


def assemble(dest_ref, sums_ref, gates_ref, places, j_half):
    half_rows = sums_ref.shape[1] // QUAD
    count = dest_ref.shape[1] // half_rows
    side, place = lax.axis_index("col"), lax.axis_index("row")
    for n, (m0, m1) in enumerate(zip(*places)):
        i = jnp.bitwise_xor(place, jnp.where(side == 0, m0, m1))
        rows = pl.ds(i, half_rows, stride=count)
        dest_ref[0, rows, :] = sums_ref[n // QUAD, pl.ds(n % QUAD, half_rows, stride=QUAD), :]
        dest_ref[1, rows, :] = gates_ref[pl.ds(n * GATE_ROWS + j_half * half_rows, half_rows), :]


def near_kernel(
    length_ref, center_ref, share_ref, right_ref, slab_ref, gate_ref, weight_ref, out_gate_ref,
    sums_ref, gates_ref, left_out_ref, left_ref, norm_ref, *, blocks,
):
    project(
        length_ref, center_ref, share_ref, slab_ref, gate_ref, weight_ref, out_gate_ref,
        left_ref, gates_ref, norm_ref, right_ref.shape[0] // 2, blocks,
    )
    left_out_ref[...] = left_ref[...].astype(BF16)
    contract(length_ref, left_ref, right_ref, 1 - lax.axis_index("col"), sums_ref, blocks)


def send_kernel(
    length_ref, center_ref, share_ref, right_ref, slab_ref, gate_ref, weight_ref, out_gate_ref, near_sums_ref, near_gates_ref,
    send_ref, left_out_ref, gates_ref, left_ref, sums_ref, norm_ref, *, blocks, near_places, far_places,
):
    flip = 1 - lax.axis_index("col")
    project(
        length_ref, center_ref, share_ref, slab_ref, gate_ref, weight_ref, out_gate_ref,
        left_ref, gates_ref, norm_ref, right_ref.shape[0] // 2, blocks,
    )
    left_out_ref[...] = left_ref[...].astype(BF16)
    contract(length_ref, left_ref, right_ref, flip, sums_ref, blocks)

    def rest():
        assemble(send_ref, near_sums_ref, near_gates_ref, near_places, flip)
        assemble(send_ref, sums_ref, gates_ref, far_places, flip)

    if blocks == 1:
        rest()
    else:
        pl.when(pl.program_id(0) == blocks - 1)(rest)


def keep_kernel(
    length_ref, right_ref, near_left_ref, far_left_ref, near_gates_ref, far_gates_ref,
    keep_ref, near_sums_ref, far_sums_ref, *, blocks, near_places, far_places,
):
    side = lax.axis_index("col")
    contract(length_ref, near_left_ref, right_ref, side, near_sums_ref, blocks)
    contract(length_ref, far_left_ref, right_ref, side, far_sums_ref, blocks)

    def rest():
        assemble(keep_ref, near_sums_ref, near_gates_ref, near_places, side)
        assemble(keep_ref, far_sums_ref, far_gates_ref, far_places, side)

    if blocks == 1:
        rest()
    else:
        pl.when(pl.program_id(0) == blocks - 1)(rest)


def last_kernel(keep_ref, got_ref, weight_ref, out_ref, *, half_cols):
    rows_dev = 2 * out_ref.shape[0]
    tri = keep_ref[0] + got_ref[0]
    d = tri - jnp.mean(tri, axis=-1, keepdims=True)
    var = jnp.mean(d * d, axis=-1, keepdims=True)
    n = (d * lax.rsqrt(var + EPS)).astype(BF16)
    projected = jnp.dot(n, weight_ref[...], preferred_element_type=F32)
    mine = lax.axis_index("row") * rows_dev // half_cols == lax.axis_index("col")
    update = projected * jnp.where(mine, keep_ref[1], got_ref[1])
    out_ref[...] = update.astype(BF16).reshape(out_ref.shape)


def passed(x, to):
    count = lax.axis_size("row")
    pairs = []
    for row in range(count):
        for core in range(2):
            if (target := to(row, core)) is not None:
                pairs.append((row * 2 + core, target[0] * 2 + target[1]))
    return lax.ppermute(x, ("row", "col"), pairs)


def doubled(half, count, between):
    steps = doubling(count)
    held, got = half, None
    for step in range(len(steps[0])):
        if step > 0:
            held = jnp.concatenate([held, got], axis=0)
        if step == 1:
            held, made = between(held)
        got = passed(held, lambda row, core: (row ^ steps[core][step], core))
    near = [slots(s[:-1]) for s in steps]
    far = [[m ^ s[-1] for m in held_by] for held_by, s in zip(near, steps)]
    return held, got, near, far, made


def direct(slab, slab_late, half, between):
    half_cols = half.shape[1]
    side = lax.axis_index("col")

    def out(x, *m):
        return passed(x, lambda row, core: (row ^ m[core], core))

    def part(x, which):
        return lax.dynamic_slice_in_dim(x, which * half_cols, half_cols, 1)

    first, second, third = [out(slab, *m) for m in ((7, 6), (2, 3), (4, 5))]
    beside = out(slab_late, 1, 1)
    over = jnp.concatenate([part(x, 1 - side) for x in (first, second, third)], axis=0)
    over, made = between(over)
    over = passed(over, lambda row, core: (row, 1 - core))
    near = jnp.concatenate([half, part(beside, side), part(first, side), part(second, side)], axis=0)
    far = jnp.concatenate([part(third, side), over], axis=0)
    return near, far, [[0, 1, 7, 2], [0, 1, 6, 3]], [[4, 6, 3, 5], [5, 7, 2, 4]], made


def shards(pair_rep, slab_rep, length, weight_a, gate_a, weight_b, gate_b, weight_gate, weight_out):
    rows_dev, half_cols, width = pair_rep.shape
    hidden = weight_a.shape[1]
    count = lax.axis_size("row")
    side = lax.axis_index("col")
    half_rows = rows_dev // 2
    depth = divisor(half_cols, 144, rows_dev)
    blocks = half_cols // depth
    grid = () if blocks == 1 else (blocks,)
    near = count // 2
    smem = pl.BlockSpec(memory_space=pltpu.SMEM)
    vmem = pl.BlockSpec(memory_space=pltpu.VMEM)
    params = pltpu.CompilerParams(vmem_limit_bytes=40 << 20)

    def whole(*shape):
        return vmem if blocks == 1 else pl.BlockSpec(shape, lambda *_: (0,) * len(shape))

    def deep(rows):
        return vmem if blocks == 1 else pl.BlockSpec((rows, depth, width), lambda k: (0, k, 0))

    square = jax.ShapeDtypeStruct((2 * width, 2 * width), BF16)
    center, share = pl.pallas_call(
        centering_kernel,
        out_shape=(square, square),
        out_specs=(vmem, vmem),
        compiler_params=pltpu.CompilerParams(vmem_limit_bytes=8 << 20),
        cost_estimate=pl.CostEstimate(flops=4 * 10**9, bytes_accessed=8 * 10**6, transcendentals=0),
        name="centering",
    )()
    slab_late, center, share = lax.optimization_barrier((slab_rep, center, share))

    chunk = divisor(rows_dev, max(2, 2592 // half_cols), 2)
    right_call = pl.pallas_call(
        functools.partial(right_kernel, chunk=chunk),
        out_shape=jax.ShapeDtypeStruct((rows_dev, half_cols, hidden), BF16),
        in_specs=[vmem] * 5,
        out_specs=vmem,
        compiler_params=params,
        cost_estimate=pl.CostEstimate(
            flops=2 * rows_dev * half_cols * width * hidden * 6,
            bytes_accessed=4 * rows_dev * half_cols * width,
            transcendentals=2 * rows_dev * half_cols * width,
        ),
        name="right",
    )

    def between(held):
        made, held = lax.optimization_barrier((right_call(center, share, weight_b, gate_b, pair_rep), held))
        return held, made

    half = lax.dynamic_slice_in_dim(slab_late, side * half_cols, half_cols, 1)
    gather = functools.partial(direct, slab_rep, slab_late) if count == 8 else functools.partial(doubled, count=count)
    near_slabs, far_slabs, near_places, far_places, right = gather(half, between=between)

    sums = jax.ShapeDtypeStruct((near // QUAD, half_rows * QUAD, hidden), F32)
    gates = jax.ShapeDtypeStruct((near * GATE_ROWS, width), F32)
    swapped = jax.ShapeDtypeStruct((2, half_rows * count, hidden), F32)
    norm = pltpu.VMEM((QUAD, depth + GATE_ROWS, width), F32)
    left_f32 = pltpu.VMEM((near, depth, hidden), F32)
    cost = pl.CostEstimate(
        flops=2 * rows_dev * half_cols * near * hidden,
        bytes_accessed=2 * rows_dev * half_cols * width,
        transcendentals=near * half_cols * width,
    )
    squares = [whole(*square.shape)] * 2
    weights = [whole(width, hidden), whole(width, hidden), whole(width, width)]

    left_shape = jax.ShapeDtypeStruct((near, half_cols, hidden), BF16)
    near_sums, near_gates, near_left = pl.pallas_call(
        functools.partial(near_kernel, blocks=blocks),
        out_shape=(sums, gates, left_shape),
        grid=grid,
        in_specs=[smem] + squares + [deep(rows_dev), deep(near)] + weights,
        out_specs=(whole(*sums.shape), whole(*gates.shape), deep(near)),
        scratch_shapes=[left_f32, norm],
        compiler_params=params,
        cost_estimate=cost,
        name="near",
    )(length, center, share, right, near_slabs, gate_a, weight_a, weight_gate)

    send, far_left, far_gates = pl.pallas_call(
        functools.partial(send_kernel, blocks=blocks, near_places=near_places, far_places=far_places),
        out_shape=(swapped, left_shape, gates),
        grid=grid,
        in_specs=[smem] + squares + [deep(rows_dev), deep(near)] + weights + [whole(*sums.shape), whole(*gates.shape)],
        out_specs=(whole(*swapped.shape), deep(near), whole(*gates.shape)),
        scratch_shapes=[left_f32, pltpu.VMEM(sums.shape, F32), norm],
        compiler_params=params,
        name="send",
    )(length, center, share, right, far_slabs, gate_a, weight_a, weight_gate, near_sums, near_gates)

    swap = passed(send, lambda row, core: (row, 1 - core))

    keep = pl.pallas_call(
        functools.partial(keep_kernel, blocks=blocks, near_places=near_places, far_places=far_places),
        out_shape=swapped,
        grid=grid,
        in_specs=[smem, deep(rows_dev), deep(near), deep(near), whole(*gates.shape), whole(*gates.shape)],
        out_specs=whole(*swapped.shape),
        scratch_shapes=[pltpu.VMEM(sums.shape, F32), pltpu.VMEM(sums.shape, F32)],
        compiler_params=params,
        cost_estimate=cost,
        name="keep",
    )(length, right, near_left, far_left, near_gates, far_gates)

    update = pl.pallas_call(
        functools.partial(last_kernel, half_cols=half_cols),
        out_shape=jax.ShapeDtypeStruct((half_rows, count, width), BF16),
        in_specs=[vmem, vmem, vmem],
        out_specs=vmem,
        compiler_params=pltpu.CompilerParams(vmem_limit_bytes=32 << 20),
        name="last",
    )(keep, swap, weight_out)
    return jnp.transpose(update, (1, 0, 2))


def solution(mesh):
    placed = (
        P(("groups", "row"), "col", None),
        P(("groups", "row"), None, None),
        P("groups"),
        P(),
        P(),
        P(),
        P(),
        P(),
        P(),
    )
    return jax.shard_map(
        shards,
        mesh=mesh,
        in_specs=placed,
        out_specs=P("groups", ("row", "col"), None),
        check_vma=False,
    )
```

```python
import functools

import jax
import jax.numpy as jnp
from jax import lax
from jax.experimental import pallas as pl
from jax.experimental.pallas import tpu as pltpu
from jax.sharding import PartitionSpec as P

EPS = 1e-05
F32 = jnp.float32
BF16 = jnp.bfloat16
QUAD = 4
GATE_ROWS = 40


def divisor(total, limit, step=1):
    return max(d for d in range(step, total + 1, step) if total % d == 0 and (d <= limit or d == step))


def doubling(count):
    bits = [1 << b for b in reversed(range(count.bit_length() - 1))]
    return bits, bits[-1:] + bits[:-1]


def slots(steps):
    held = [0]
    for step in steps:
        held = held + [m ^ step for m in held]
    return held


def centering_kernel(center_ref, share_ref):
    width = center_ref.shape[0] // 2
    row = lax.broadcasted_iota(jnp.int32, (2 * width, 2 * width), 0)
    col = lax.broadcasted_iota(jnp.int32, (2 * width, 2 * width), 1)
    share = jnp.where((row < width) == (col < width), 1.0 / width, 0.0)
    center_ref[...] = (jnp.where(row == col, 1.0, 0.0) - share).astype(BF16)
    share_ref[...] = share.astype(BF16)


def normed(first, second, center, share):
    wide = jnp.concatenate([first, second], axis=1)
    d = jnp.dot(wide, center, preferred_element_type=F32)
    var = jnp.dot((d * d).astype(BF16), share, preferred_element_type=F32)
    return (d * lax.rsqrt(var + EPS)).astype(BF16)


def gated(n, both):
    width = both.shape[1] // 2
    y = jnp.dot(n, both, preferred_element_type=F32)
    value = y[:, width:]
    return value + value * jnp.tanh(y[:, :width])


def right_kernel(center_ref, share_ref, weight_ref, gate_ref, pair_ref, out_ref, *, chunk):
    rows, cols, width = pair_ref.shape
    half = jnp.asarray(0.5, BF16)
    both = jnp.concatenate([gate_ref[...] * half, weight_ref[...] * half], axis=1)

    def some(turn, _):
        j0 = turn * chunk
        x = pair_ref[pl.ds(j0, chunk)].reshape(2, chunk * cols // 2, width)
        n = normed(x[0], x[1], center_ref[...], share_ref[...])
        for part in range(2):
            edge = gated(n[:, part * width : (part + 1) * width], both).astype(BF16)
            out_ref[pl.ds(j0 + part * (chunk // 2), chunk // 2)] = edge.reshape(chunk // 2, cols, width)
        return 0

    lax.fori_loop(0, rows // chunk, some, 0)


def fold(parts):
    place = lax.broadcasted_iota(jnp.int32, parts[0].shape, 0)
    for step in (1, 2, 4):
        here = (place & step) == 0
        parts = [
            jnp.where(here, a, b) + pltpu.roll(jnp.where(here, b, a), 8 - step, 0)
            for a, b in zip(parts[0::2], parts[1::2])
        ]
    return parts[0]


def block_of(blocks):
    return 0 if blocks == 1 else pl.program_id(0)


def project(
    length_ref, center_ref, share_ref, slab_ref, gate_ref, weight_ref, out_gate_ref, left_ref, gates_ref, norm_ref,
    half_rows, blocks,
):
    slabs, depth, width = slab_ref.shape
    k_step = block_of(blocks)
    half_cols = depth * blocks
    half = jnp.asarray(0.5, BF16)
    both = jnp.concatenate([gate_ref[...] * half, weight_ref[...] * half], axis=1)
    first_k = lax.axis_index("col") * half_cols + k_step * depth
    live = first_k + lax.broadcasted_iota(jnp.int32, (depth, width), 0) < length_ref[0]
    first_j = lax.rem(lax.axis_index("row") * (2 * half_rows), half_cols)
    start = lax.rem(first_j, depth)

    def quad(q):
        s = q * QUAD
        x = slab_ref[pl.ds(s, QUAD)].reshape(2, 2 * depth, width)
        n = normed(x[0], x[1], center_ref[...], share_ref[...])
        for part in range(2):
            own = n[:, part * width : (part + 1) * width]
            edge = gated(own, both)
            for r in range(2):
                here = slice(r * depth, (r + 1) * depth)
                left_ref[s + 2 * part + r] = jnp.where(live, edge[here], 0.0).astype(BF16).astype(F32)
                norm_ref[2 * part + r, pl.ds(0, depth), :] = own[here].astype(F32)

        def gates():
            rows = jnp.concatenate([norm_ref[n, pl.ds(start, GATE_ROWS), :] for n in range(QUAD)], axis=0)
            y = jnp.dot(rows.astype(BF16), out_gate_ref[...] * half, preferred_element_type=F32)
            gate = (0.5 + 0.5 * jnp.tanh(y)).astype(BF16).astype(F32)
            gates_ref[pl.ds(pl.multiple_of(s * GATE_ROWS, 8), QUAD * GATE_ROWS), :] = gate

        if blocks == 1:
            gates()
        else:
            pl.when(k_step == first_j // depth)(gates)

    if slabs == QUAD:
        quad(0)
    else:
        pl.loop(0, slabs // QUAD)(quad)


def contract(length_ref, left_ref, right_ref, j_half, sums_ref, blocks):
    slabs, depth, _ = left_ref.shape
    rows = right_ref.shape[0] // 2
    group = divisor(rows, 6, 2)
    live_rows = length_ref[0] - lax.axis_index("row") * (2 * rows)
    second = lax.broadcasted_iota(jnp.int32, (8, left_ref.shape[2]), 0) // QUAD

    def tile(turn, _):
        q = turn // (rows // group)
        j0 = lax.rem(turn, rows // group) * group
        first = j_half * rows + j0
        sums = [[None] * QUAD for _ in range(group)]
        for k0 in range(0, depth, 16):
            edges = [right_ref[first + j, pl.ds(k0, 16), :].astype(F32) for j in range(group)]
            for n in range(QUAD):
                left = left_ref[q * QUAD + n, pl.ds(k0, 16), :].astype(F32)
                for j in range(group):
                    term = left * edges[j]
                    term = term[:8] + term[8:]
                    sums[j][n] = term if k0 == 0 else sums[j][n] + term
        for j in range(0, group, 2):
            dest = sums_ref.at[q, pl.ds(pl.multiple_of((j0 + j) * QUAD, 8), 8), :]
            total = jnp.where(first + j + second < live_rows, fold(sums[j] + sums[j + 1]), 0.0)
            dest[...] = total if blocks == 1 else jnp.where(block_of(blocks) == 0, total, total + dest[...])
        return 0

    lax.fori_loop(0, slabs // QUAD * (rows // group), tile, 0)


def assemble(dest_ref, sums_ref, gates_ref, places, j_half):
    half_rows = sums_ref.shape[1] // QUAD
    count = dest_ref.shape[1] // half_rows
    side, place = lax.axis_index("col"), lax.axis_index("row")
    for n, (m0, m1) in enumerate(zip(*places)):
        i = jnp.bitwise_xor(place, jnp.where(side == 0, m0, m1))
        rows = pl.ds(i, half_rows, stride=count)
        dest_ref[0, rows, :] = sums_ref[n // QUAD, pl.ds(n % QUAD, half_rows, stride=QUAD), :]
        dest_ref[1, rows, :] = gates_ref[pl.ds(n * GATE_ROWS + j_half * half_rows, half_rows), :]


def near_kernel(
    length_ref, center_ref, share_ref, right_ref, slab_ref, gate_ref, weight_ref, out_gate_ref,
    sums_ref, gates_ref, left_out_ref, left_ref, norm_ref, *, blocks,
):
    project(
        length_ref, center_ref, share_ref, slab_ref, gate_ref, weight_ref, out_gate_ref,
        left_ref, gates_ref, norm_ref, right_ref.shape[0] // 2, blocks,
    )
    left_out_ref[...] = left_ref[...].astype(BF16)
    contract(length_ref, left_ref, right_ref, 1 - lax.axis_index("col"), sums_ref, blocks)


def send_kernel(
    length_ref, center_ref, share_ref, right_ref, slab_ref, gate_ref, weight_ref, out_gate_ref, near_sums_ref, near_gates_ref,
    send_ref, left_out_ref, gates_ref, left_ref, sums_ref, norm_ref, *, blocks, near_places, far_places,
):
    flip = 1 - lax.axis_index("col")
    project(
        length_ref, center_ref, share_ref, slab_ref, gate_ref, weight_ref, out_gate_ref,
        left_ref, gates_ref, norm_ref, right_ref.shape[0] // 2, blocks,
    )
    left_out_ref[...] = left_ref[...].astype(BF16)
    contract(length_ref, left_ref, right_ref, flip, sums_ref, blocks)

    def rest():
        assemble(send_ref, near_sums_ref, near_gates_ref, near_places, flip)
        assemble(send_ref, sums_ref, gates_ref, far_places, flip)

    if blocks == 1:
        rest()
    else:
        pl.when(pl.program_id(0) == blocks - 1)(rest)


def keep_kernel(
    length_ref, right_ref, near_left_ref, far_left_ref, near_gates_ref, far_gates_ref,
    keep_ref, near_sums_ref, far_sums_ref, *, blocks, near_places, far_places,
):
    side = lax.axis_index("col")
    contract(length_ref, near_left_ref, right_ref, side, near_sums_ref, blocks)
    contract(length_ref, far_left_ref, right_ref, side, far_sums_ref, blocks)

    def rest():
        assemble(keep_ref, near_sums_ref, near_gates_ref, near_places, side)
        assemble(keep_ref, far_sums_ref, far_gates_ref, far_places, side)

    if blocks == 1:
        rest()
    else:
        pl.when(pl.program_id(0) == blocks - 1)(rest)


def last_kernel(keep_ref, got_ref, weight_ref, out_ref, *, half_cols):
    rows_dev = 2 * out_ref.shape[0]
    tri = keep_ref[0] + got_ref[0]
    d = tri - jnp.mean(tri, axis=-1, keepdims=True)
    var = jnp.mean(d * d, axis=-1, keepdims=True)
    n = (d * lax.rsqrt(var + EPS)).astype(BF16)
    projected = jnp.dot(n, weight_ref[...], preferred_element_type=F32)
    mine = lax.axis_index("row") * rows_dev // half_cols == lax.axis_index("col")
    update = projected * jnp.where(mine, keep_ref[1], got_ref[1])
    out_ref[...] = update.astype(BF16).reshape(out_ref.shape)


def passed(x, to):
    count = lax.axis_size("row")
    pairs = []
    for row in range(count):
        for core in range(2):
            if (target := to(row, core)) is not None:
                pairs.append((row * 2 + core, target[0] * 2 + target[1]))
    return lax.ppermute(x, ("row", "col"), pairs)


def doubled(half, count, between):
    steps = doubling(count)
    held, got = half, None
    for step in range(len(steps[0])):
        if step > 0:
            held = jnp.concatenate([held, got], axis=0)
        if step == 1:
            held, made = between(held)
        got = passed(held, lambda row, core: (row ^ steps[core][step], core))
    near = [slots(s[:-1]) for s in steps]
    far = [[m ^ s[-1] for m in held_by] for held_by, s in zip(near, steps)]
    return held, got, near, far, made


def direct(slab, slab_late, half, between):
    half_cols = half.shape[1]
    side = lax.axis_index("col")

    def out(x, *m):
        return passed(x, lambda row, core: (row ^ m[core], core))

    def part(x, which):
        return lax.dynamic_slice_in_dim(x, which * half_cols, half_cols, 1)

    first, second, third = [out(slab, *m) for m in ((5, 4), (2, 3), (6, 7))]
    beside = out(slab_late, 1, 1)
    over = jnp.concatenate([part(x, 1 - side) for x in (first, second, third)], axis=0)
    over, made = between(over)
    over = passed(over, lambda row, core: (row, 1 - core))
    near = jnp.concatenate([half, part(beside, side), part(first, side), part(second, side)], axis=0)
    far = jnp.concatenate([part(third, side), over], axis=0)
    return near, far, [[0, 1, 5, 2], [0, 1, 4, 3]], [[6, 4, 3, 7], [7, 5, 2, 6]], made


def shards(pair_rep, slab_rep, length, weight_a, gate_a, weight_b, gate_b, weight_gate, weight_out):
    rows_dev, half_cols, width = pair_rep.shape
    hidden = weight_a.shape[1]
    count = lax.axis_size("row")
    side = lax.axis_index("col")
    half_rows = rows_dev // 2
    depth = divisor(half_cols, 144, rows_dev)
    blocks = half_cols // depth
    grid = () if blocks == 1 else (blocks,)
    near = count // 2
    smem = pl.BlockSpec(memory_space=pltpu.SMEM)
    vmem = pl.BlockSpec(memory_space=pltpu.VMEM)
    params = pltpu.CompilerParams(vmem_limit_bytes=40 << 20)

    def whole(*shape):
        return vmem if blocks == 1 else pl.BlockSpec(shape, lambda *_: (0,) * len(shape))

    def deep(rows):
        return vmem if blocks == 1 else pl.BlockSpec((rows, depth, width), lambda k: (0, k, 0))

    square = jax.ShapeDtypeStruct((2 * width, 2 * width), BF16)
    center, share = pl.pallas_call(
        centering_kernel,
        out_shape=(square, square),
        out_specs=(vmem, vmem),
        compiler_params=pltpu.CompilerParams(vmem_limit_bytes=8 << 20),
        cost_estimate=pl.CostEstimate(flops=4 * 10**9, bytes_accessed=8 * 10**6, transcendentals=0),
        name="centering",
    )()
    slab_late, center, share = lax.optimization_barrier((slab_rep, center, share))

    chunk = divisor(rows_dev, max(2, 2592 // half_cols), 2)
    right_call = pl.pallas_call(
        functools.partial(right_kernel, chunk=chunk),
        out_shape=jax.ShapeDtypeStruct((rows_dev, half_cols, hidden), BF16),
        in_specs=[vmem] * 5,
        out_specs=vmem,
        compiler_params=params,
        cost_estimate=pl.CostEstimate(
            flops=2 * rows_dev * half_cols * width * hidden * 6,
            bytes_accessed=4 * rows_dev * half_cols * width,
            transcendentals=2 * rows_dev * half_cols * width,
        ),
        name="right",
    )

    def between(held):
        made, held = lax.optimization_barrier((right_call(center, share, weight_b, gate_b, pair_rep), held))
        return held, made

    half = lax.dynamic_slice_in_dim(slab_late, side * half_cols, half_cols, 1)
    gather = functools.partial(direct, slab_rep, slab_late) if count == 8 else functools.partial(doubled, count=count)
    near_slabs, far_slabs, near_places, far_places, right = gather(half, between=between)

    sums = jax.ShapeDtypeStruct((near // QUAD, half_rows * QUAD, hidden), F32)
    gates = jax.ShapeDtypeStruct((near * GATE_ROWS, width), F32)
    swapped = jax.ShapeDtypeStruct((2, half_rows * count, hidden), F32)
    norm = pltpu.VMEM((QUAD, depth + GATE_ROWS, width), F32)
    left_f32 = pltpu.VMEM((near, depth, hidden), F32)
    cost = pl.CostEstimate(
        flops=2 * rows_dev * half_cols * near * hidden,
        bytes_accessed=2 * rows_dev * half_cols * width,
        transcendentals=near * half_cols * width,
    )
    squares = [whole(*square.shape)] * 2
    weights = [whole(width, hidden), whole(width, hidden), whole(width, width)]

    left_shape = jax.ShapeDtypeStruct((near, half_cols, hidden), BF16)
    near_sums, near_gates, near_left = pl.pallas_call(
        functools.partial(near_kernel, blocks=blocks),
        out_shape=(sums, gates, left_shape),
        grid=grid,
        in_specs=[smem] + squares + [deep(rows_dev), deep(near)] + weights,
        out_specs=(whole(*sums.shape), whole(*gates.shape), deep(near)),
        scratch_shapes=[left_f32, norm],
        compiler_params=params,
        cost_estimate=cost,
        name="near",
    )(length, center, share, right, near_slabs, gate_a, weight_a, weight_gate)

    send, far_left, far_gates = pl.pallas_call(
        functools.partial(send_kernel, blocks=blocks, near_places=near_places, far_places=far_places),
        out_shape=(swapped, left_shape, gates),
        grid=grid,
        in_specs=[smem] + squares + [deep(rows_dev), deep(near)] + weights + [whole(*sums.shape), whole(*gates.shape)],
        out_specs=(whole(*swapped.shape), deep(near), whole(*gates.shape)),
        scratch_shapes=[left_f32, pltpu.VMEM(sums.shape, F32), norm],
        compiler_params=params,
        name="send",
    )(length, center, share, right, far_slabs, gate_a, weight_a, weight_gate, near_sums, near_gates)

    swap = passed(send, lambda row, core: (row, 1 - core))

    keep = pl.pallas_call(
        functools.partial(keep_kernel, blocks=blocks, near_places=near_places, far_places=far_places),
        out_shape=swapped,
        grid=grid,
        in_specs=[smem, deep(rows_dev), deep(near), deep(near), whole(*gates.shape), whole(*gates.shape)],
        out_specs=whole(*swapped.shape),
        scratch_shapes=[pltpu.VMEM(sums.shape, F32), pltpu.VMEM(sums.shape, F32)],
        compiler_params=params,
        cost_estimate=cost,
        name="keep",
    )(length, right, near_left, far_left, near_gates, far_gates)

    update = pl.pallas_call(
        functools.partial(last_kernel, half_cols=half_cols),
        out_shape=jax.ShapeDtypeStruct((half_rows, count, width), BF16),
        in_specs=[vmem, vmem, vmem],
        out_specs=vmem,
        compiler_params=pltpu.CompilerParams(vmem_limit_bytes=32 << 20),
        name="last",
    )(keep, swap, weight_out)
    return jnp.transpose(update, (1, 0, 2))


def solution(mesh):
    placed = (
        P(("groups", "row"), "col", None),
        P(("groups", "row"), None, None),
        P("groups"),
        P(),
        P(),
        P(),
        P(),
        P(),
        P(),
    )
    return jax.shard_map(
        shards,
        mesh=mesh,
        in_specs=placed,
        out_specs=P("groups", ("row", "col"), None),
        check_vma=False,
    )
```

```python
import functools

import jax
import jax.numpy as jnp
from jax import lax
from jax.experimental import pallas as pl
from jax.experimental.pallas import tpu as pltpu
from jax.sharding import PartitionSpec as P

EPS = 1e-05
F32 = jnp.float32
BF16 = jnp.bfloat16
QUAD = 4
GATE_ROWS = 40


def divisor(total, limit, step=1):
    return max(d for d in range(step, total + 1, step) if total % d == 0 and (d <= limit or d == step))


def doubling(count):
    bits = [1 << b for b in reversed(range(count.bit_length() - 1))]
    return bits, bits[-1:] + bits[:-1]


def slots(steps):
    held = [0]
    for step in steps:
        held = held + [m ^ step for m in held]
    return held


def centering_kernel(center_ref, share_ref):
    width = center_ref.shape[0] // 2
    row = lax.broadcasted_iota(jnp.int32, (2 * width, 2 * width), 0)
    col = lax.broadcasted_iota(jnp.int32, (2 * width, 2 * width), 1)
    share = jnp.where((row < width) == (col < width), 1.0 / width, 0.0)
    center_ref[...] = (jnp.where(row == col, 1.0, 0.0) - share).astype(BF16)
    share_ref[...] = share.astype(BF16)


def normed(first, second, center, share):
    wide = jnp.concatenate([first, second], axis=1)
    d = jnp.dot(wide, center, preferred_element_type=F32)
    var = jnp.dot((d * d).astype(BF16), share, preferred_element_type=F32)
    return (d * lax.rsqrt(var + EPS)).astype(BF16)


def gated(n, both):
    width = both.shape[1] // 2
    y = jnp.dot(n, both, preferred_element_type=F32)
    value = y[:, width:]
    return value + value * jnp.tanh(y[:, :width])


def right_kernel(center_ref, share_ref, weight_ref, gate_ref, pair_ref, out_ref, *, chunk):
    rows, cols, width = pair_ref.shape
    half = jnp.asarray(0.5, BF16)
    both = jnp.concatenate([gate_ref[...] * half, weight_ref[...] * half], axis=1)

    def some(turn, _):
        j0 = turn * chunk
        x = pair_ref[pl.ds(j0, chunk)].reshape(2, chunk * cols // 2, width)
        n = normed(x[0], x[1], center_ref[...], share_ref[...])
        for part in range(2):
            edge = gated(n[:, part * width : (part + 1) * width], both).astype(BF16)
            out_ref[pl.ds(j0 + part * (chunk // 2), chunk // 2)] = edge.reshape(chunk // 2, cols, width)
        return 0

    lax.fori_loop(0, rows // chunk, some, 0)


def fold(parts):
    place = lax.broadcasted_iota(jnp.int32, parts[0].shape, 0)
    for step in (1, 2, 4):
        here = (place & step) == 0
        parts = [
            jnp.where(here, a, b) + pltpu.roll(jnp.where(here, b, a), 8 - step, 0)
            for a, b in zip(parts[0::2], parts[1::2])
        ]
    return parts[0]


def block_of(blocks):
    return 0 if blocks == 1 else pl.program_id(0)


def project(
    length_ref, center_ref, share_ref, slab_ref, gate_ref, weight_ref, out_gate_ref, left_ref, gates_ref, norm_ref,
    half_rows, blocks,
):
    slabs, depth, width = slab_ref.shape
    k_step = block_of(blocks)
    half_cols = depth * blocks
    half = jnp.asarray(0.5, BF16)
    both = jnp.concatenate([gate_ref[...] * half, weight_ref[...] * half], axis=1)
    first_k = lax.axis_index("col") * half_cols + k_step * depth
    live = first_k + lax.broadcasted_iota(jnp.int32, (depth, width), 0) < length_ref[0]
    first_j = lax.rem(lax.axis_index("row") * (2 * half_rows), half_cols)
    start = lax.rem(first_j, depth)

    def quad(q):
        s = q * QUAD
        x = slab_ref[pl.ds(s, QUAD)].reshape(2, 2 * depth, width)
        n = normed(x[0], x[1], center_ref[...], share_ref[...])
        for part in range(2):
            own = n[:, part * width : (part + 1) * width]
            edge = gated(own, both)
            for r in range(2):
                here = slice(r * depth, (r + 1) * depth)
                left_ref[s + 2 * part + r] = jnp.where(live, edge[here], 0.0).astype(BF16).astype(left_ref.dtype)
                norm_ref[2 * part + r, pl.ds(0, depth), :] = own[here].astype(F32)

        def gates():
            rows = jnp.concatenate([norm_ref[n, pl.ds(start, GATE_ROWS), :] for n in range(QUAD)], axis=0)
            y = jnp.dot(rows.astype(BF16), out_gate_ref[...] * half, preferred_element_type=F32)
            gate = (0.5 + 0.5 * jnp.tanh(y)).astype(BF16).astype(F32)
            gates_ref[pl.ds(pl.multiple_of(s * GATE_ROWS, 8), QUAD * GATE_ROWS), :] = gate

        if blocks == 1:
            gates()
        else:
            pl.when(k_step == first_j // depth)(gates)

    if slabs == QUAD:
        quad(0)
    else:
        pl.loop(0, slabs // QUAD)(quad)


def contract(length_ref, left_ref, right_ref, j_half, sums_ref, blocks):
    slabs, depth, _ = left_ref.shape
    rows = right_ref.shape[0] // 2
    group = divisor(rows, 6, 2)
    live_rows = length_ref[0] - lax.axis_index("row") * (2 * rows)
    second = lax.broadcasted_iota(jnp.int32, (8, left_ref.shape[2]), 0) // QUAD

    def tile(turn, _):
        q = turn // (rows // group)
        j0 = lax.rem(turn, rows // group) * group
        first = j_half * rows + j0
        sums = [[None] * QUAD for _ in range(group)]
        for k0 in range(0, depth, 16):
            edges = [right_ref[first + j, pl.ds(k0, 16), :].astype(F32) for j in range(group)]
            for n in range(QUAD):
                left = left_ref[q * QUAD + n, pl.ds(k0, 16), :].astype(F32)
                for j in range(group):
                    term = left * edges[j]
                    term = term[:8] + term[8:]
                    sums[j][n] = term if k0 == 0 else sums[j][n] + term
        for j in range(0, group, 2):
            dest = sums_ref.at[q, pl.ds(pl.multiple_of((j0 + j) * QUAD, 8), 8), :]
            total = jnp.where(first + j + second < live_rows, fold(sums[j] + sums[j + 1]), 0.0)
            dest[...] = total if blocks == 1 else jnp.where(block_of(blocks) == 0, total, total + dest[...])
        return 0

    lax.fori_loop(0, slabs // QUAD * (rows // group), tile, 0)


def assemble(dest_ref, sums_ref, gates_ref, places, j_half):
    half_rows = sums_ref.shape[1] // QUAD
    count = dest_ref.shape[1] // half_rows
    side, place = lax.axis_index("col"), lax.axis_index("row")
    for n, (m0, m1) in enumerate(zip(*places)):
        i = jnp.bitwise_xor(place, jnp.where(side == 0, m0, m1))
        rows = pl.ds(i, half_rows, stride=count)
        dest_ref[0, rows, :] = sums_ref[n // QUAD, pl.ds(n % QUAD, half_rows, stride=QUAD), :]
        dest_ref[1, rows, :] = gates_ref[pl.ds(n * GATE_ROWS + j_half * half_rows, half_rows), :]


def near_kernel(
    length_ref, center_ref, share_ref, right_ref, slab_ref, gate_ref, weight_ref, out_gate_ref,
    sums_ref, gates_ref, left_ref, norm_ref, *, blocks,
):
    project(
        length_ref, center_ref, share_ref, slab_ref, gate_ref, weight_ref, out_gate_ref,
        left_ref, gates_ref, norm_ref, right_ref.shape[0] // 2, blocks,
    )
    contract(length_ref, left_ref, right_ref, 1 - lax.axis_index("col"), sums_ref, blocks)


def send_kernel(
    length_ref, center_ref, share_ref, right_ref, slab_ref, gate_ref, weight_ref, out_gate_ref, near_sums_ref, near_gates_ref,
    send_ref, left_ref, gates_ref, sums_ref, norm_ref, *, blocks, near_places, far_places,
):
    flip = 1 - lax.axis_index("col")

    def at_end(body):
        if blocks == 1:
            body()
        else:
            pl.when(pl.program_id(0) == blocks - 1)(body)

    at_end(lambda: assemble(send_ref, near_sums_ref, near_gates_ref, near_places, flip))
    project(
        length_ref, center_ref, share_ref, slab_ref, gate_ref, weight_ref, out_gate_ref,
        left_ref, gates_ref, norm_ref, right_ref.shape[0] // 2, blocks,
    )
    contract(length_ref, left_ref, right_ref, flip, sums_ref, blocks)

    at_end(lambda: assemble(send_ref, sums_ref, gates_ref, far_places, flip))


def keep_kernel(
    length_ref, right_ref, near_left_ref, far_left_ref, near_gates_ref, far_gates_ref,
    keep_ref, near_sums_ref, far_sums_ref, *, blocks, near_places, far_places,
):
    side = lax.axis_index("col")
    contract(length_ref, near_left_ref, right_ref, side, near_sums_ref, blocks)
    contract(length_ref, far_left_ref, right_ref, side, far_sums_ref, blocks)

    def rest():
        assemble(keep_ref, near_sums_ref, near_gates_ref, near_places, side)
        assemble(keep_ref, far_sums_ref, far_gates_ref, far_places, side)

    if blocks == 1:
        rest()
    else:
        pl.when(pl.program_id(0) == blocks - 1)(rest)


def last_kernel(keep_ref, got_ref, weight_ref, out_ref, *, half_cols):
    rows_dev = 2 * out_ref.shape[0]
    tri = keep_ref[0] + got_ref[0]
    d = tri - jnp.mean(tri, axis=-1, keepdims=True)
    var = jnp.mean(d * d, axis=-1, keepdims=True)
    n = (d * lax.rsqrt(var + EPS)).astype(BF16)
    projected = jnp.dot(n, weight_ref[...], preferred_element_type=F32)
    mine = lax.axis_index("row") * rows_dev // half_cols == lax.axis_index("col")
    update = projected * jnp.where(mine, keep_ref[1], got_ref[1])
    out_ref[...] = update.astype(BF16).reshape(out_ref.shape)


def passed(x, to):
    count = lax.axis_size("row")
    pairs = []
    for row in range(count):
        for core in range(2):
            if (target := to(row, core)) is not None:
                pairs.append((row * 2 + core, target[0] * 2 + target[1]))
    return lax.ppermute(x, ("row", "col"), pairs)


def doubled(half, count, between):
    steps = doubling(count)
    held, got = half, None
    for step in range(len(steps[0])):
        if step > 0:
            held = jnp.concatenate([held, got], axis=0)
        if step == 1:
            held, made = between(held)
        got = passed(held, lambda row, core: (row ^ steps[core][step], core))
    near = [slots(s[:-1]) for s in steps]
    far = [[m ^ s[-1] for m in held_by] for held_by, s in zip(near, steps)]
    return held, got, near, far, made


def direct(slab, slab_late, half, between):
    half_cols = half.shape[1]
    side = lax.axis_index("col")

    def out(x, *m):
        return passed(x, lambda row, core: (row ^ m[core], core))

    def part(x, which):
        return lax.dynamic_slice_in_dim(x, which * half_cols, half_cols, 1)

    first, second, third = [out(slab, *m) for m in ((7, 6), (2, 3), (4, 5))]
    beside = out(slab_late, 1, 1)
    over = jnp.concatenate([part(x, 1 - side) for x in (first, second, third)], axis=0)
    over, made = between(over)
    over = passed(over, lambda row, core: (row, 1 - core))
    near = jnp.concatenate([half, part(beside, side), part(first, side), part(second, side)], axis=0)
    far = jnp.concatenate([part(third, side), over], axis=0)
    return near, far, [[0, 1, 7, 2], [0, 1, 6, 3]], [[4, 6, 3, 5], [5, 7, 2, 4]], made


def shards(pair_rep, slab_rep, length, weight_a, gate_a, weight_b, gate_b, weight_gate, weight_out):
    rows_dev, half_cols, width = pair_rep.shape
    hidden = weight_a.shape[1]
    count = lax.axis_size("row")
    side = lax.axis_index("col")
    half_rows = rows_dev // 2
    depth = divisor(half_cols, 144, rows_dev)
    blocks = half_cols // depth
    grid = () if blocks == 1 else (blocks,)
    near = count // 2
    smem = pl.BlockSpec(memory_space=pltpu.SMEM)
    vmem = pl.BlockSpec(memory_space=pltpu.VMEM)
    params = pltpu.CompilerParams(vmem_limit_bytes=40 << 20)

    def whole(*shape):
        return vmem if blocks == 1 else pl.BlockSpec(shape, lambda *_: (0,) * len(shape))

    def deep(rows):
        return vmem if blocks == 1 else pl.BlockSpec((rows, depth, width), lambda k: (0, k, 0))

    square = jax.ShapeDtypeStruct((2 * width, 2 * width), BF16)
    center, share = pl.pallas_call(
        centering_kernel,
        out_shape=(square, square),
        out_specs=(vmem, vmem),
        compiler_params=pltpu.CompilerParams(vmem_limit_bytes=8 << 20),
        cost_estimate=pl.CostEstimate(flops=4 * 10**9, bytes_accessed=8 * 10**6, transcendentals=0),
        name="centering",
    )()
    slab_late, center, share = lax.optimization_barrier((slab_rep, center, share))

    chunk = divisor(rows_dev, max(2, 2592 // half_cols), 2)
    right_call = pl.pallas_call(
        functools.partial(right_kernel, chunk=chunk),
        out_shape=jax.ShapeDtypeStruct((rows_dev, half_cols, hidden), BF16),
        in_specs=[vmem] * 5,
        out_specs=vmem,
        compiler_params=params,
        cost_estimate=pl.CostEstimate(
            flops=2 * rows_dev * half_cols * width * hidden * 6,
            bytes_accessed=4 * rows_dev * half_cols * width,
            transcendentals=2 * rows_dev * half_cols * width,
        ),
        name="right",
    )

    def between(held):
        made, held = lax.optimization_barrier((right_call(center, share, weight_b, gate_b, pair_rep), held))
        return held, made

    half = lax.dynamic_slice_in_dim(slab_late, side * half_cols, half_cols, 1)
    gather = functools.partial(direct, slab_rep, slab_late) if count == 8 else functools.partial(doubled, count=count)
    near_slabs, far_slabs, near_places, far_places, right = gather(half, between=between)

    sums = jax.ShapeDtypeStruct((near // QUAD, half_rows * QUAD, hidden), F32)
    gates = jax.ShapeDtypeStruct((near * GATE_ROWS, width), F32)
    swapped = jax.ShapeDtypeStruct((2, half_rows * count, hidden), F32)
    norm = pltpu.VMEM((QUAD, depth + GATE_ROWS, width), F32)
    cost = pl.CostEstimate(
        flops=2 * rows_dev * half_cols * near * hidden,
        bytes_accessed=2 * rows_dev * half_cols * width,
        transcendentals=near * half_cols * width,
    )
    squares = [whole(*square.shape)] * 2
    weights = [whole(width, hidden), whole(width, hidden), whole(width, width)]

    left_shape = jax.ShapeDtypeStruct((near, half_cols, hidden), F32 if blocks == 1 else BF16)
    near_sums, near_gates, near_left = pl.pallas_call(
        functools.partial(near_kernel, blocks=blocks),
        out_shape=(sums, gates, left_shape),
        grid=grid,
        in_specs=[smem] + squares + [deep(rows_dev), deep(near)] + weights,
        out_specs=(whole(*sums.shape), whole(*gates.shape), deep(near)),
        scratch_shapes=[norm],
        compiler_params=params,
        cost_estimate=cost,
        name="near",
    )(length, center, share, right, near_slabs, gate_a, weight_a, weight_gate)

    send, far_left, far_gates = pl.pallas_call(
        functools.partial(send_kernel, blocks=blocks, near_places=near_places, far_places=far_places),
        out_shape=(swapped, left_shape, gates),
        grid=grid,
        in_specs=[smem] + squares + [deep(rows_dev), deep(near)] + weights + [whole(*sums.shape), whole(*gates.shape)],
        out_specs=(whole(*swapped.shape), deep(near), whole(*gates.shape)),
        scratch_shapes=[pltpu.VMEM(sums.shape, F32), norm],
        compiler_params=params,
        name="send",
    )(length, center, share, right, far_slabs, gate_a, weight_a, weight_gate, near_sums, near_gates)

    swap = passed(send, lambda row, core: (row, 1 - core))

    keep = pl.pallas_call(
        functools.partial(keep_kernel, blocks=blocks, near_places=near_places, far_places=far_places),
        out_shape=swapped,
        grid=grid,
        in_specs=[smem, deep(rows_dev), deep(near), deep(near), whole(*gates.shape), whole(*gates.shape)],
        out_specs=whole(*swapped.shape),
        scratch_shapes=[pltpu.VMEM(sums.shape, F32), pltpu.VMEM(sums.shape, F32)],
        compiler_params=params,
        cost_estimate=cost,
        name="keep",
    )(length, right, near_left, far_left, near_gates, far_gates)

    update = pl.pallas_call(
        functools.partial(last_kernel, half_cols=half_cols),
        out_shape=jax.ShapeDtypeStruct((half_rows, count, width), BF16),
        in_specs=[vmem, vmem, vmem],
        out_specs=vmem,
        compiler_params=pltpu.CompilerParams(vmem_limit_bytes=32 << 20),
        name="last",
    )(keep, swap, weight_out)
    return jnp.transpose(update, (1, 0, 2))


def solution(mesh):
    placed = (
        P(("groups", "row"), "col", None),
        P(("groups", "row"), None, None),
        P("groups"),
        P(),
        P(),
        P(),
        P(),
        P(),
        P(),
    )
    return jax.shard_map(
        shards,
        mesh=mesh,
        in_specs=placed,
        out_specs=P("groups", ("row", "col"), None),
        check_vma=False,
    )
```

```python
import functools

import jax
import jax.numpy as jnp
from jax import lax
from jax.experimental import pallas as pl
from jax.experimental.pallas import tpu as pltpu
from jax.sharding import PartitionSpec as P

EPS = 1e-05
F32 = jnp.float32
BF16 = jnp.bfloat16
QUAD = 4
GATE_ROWS = 40


def divisor(total, limit, step=1):
    return max(d for d in range(step, total + 1, step) if total % d == 0 and (d <= limit or d == step))


def doubling(count):
    bits = [1 << b for b in reversed(range(count.bit_length() - 1))]
    return bits, bits[-1:] + bits[:-1]


def slots(steps):
    held = [0]
    for step in steps:
        held = held + [m ^ step for m in held]
    return held


def centering_kernel(center_ref, share_ref):
    width = center_ref.shape[0] // 2
    row = lax.broadcasted_iota(jnp.int32, (2 * width, 2 * width), 0)
    col = lax.broadcasted_iota(jnp.int32, (2 * width, 2 * width), 1)
    share = jnp.where((row < width) == (col < width), 1.0 / width, 0.0)
    center_ref[...] = (jnp.where(row == col, 1.0, 0.0) - share).astype(BF16)
    share_ref[...] = share.astype(BF16)


def normed(first, second, center, share):
    wide = jnp.concatenate([first, second], axis=1)
    d = jnp.dot(wide, center, preferred_element_type=F32)
    var = jnp.dot((d * d).astype(BF16), share, preferred_element_type=F32)
    return (d * lax.rsqrt(var + EPS)).astype(BF16)


def gated(n, both):
    width = both.shape[1] // 2
    y = jnp.dot(n, both, preferred_element_type=F32)
    value = y[:, width:]
    return value + value * jnp.tanh(y[:, :width])


def right_kernel(center_ref, share_ref, weight_ref, gate_ref, pair_ref, out_ref, *, chunk):
    rows, cols, width = pair_ref.shape
    half = jnp.asarray(0.5, BF16)
    both = jnp.concatenate([gate_ref[...] * half, weight_ref[...] * half], axis=1)

    def some(turn, _):
        j0 = turn * chunk
        x = pair_ref[pl.ds(j0, chunk)].reshape(2, chunk * cols // 2, width)
        n = normed(x[0], x[1], center_ref[...], share_ref[...])
        for part in range(2):
            edge = gated(n[:, part * width : (part + 1) * width], both).astype(BF16)
            out_ref[pl.ds(j0 + part * (chunk // 2), chunk // 2)] = edge.reshape(chunk // 2, cols, width)
        return 0

    lax.fori_loop(0, rows // chunk, some, 0)


def fold(parts):
    place = lax.broadcasted_iota(jnp.int32, parts[0].shape, 0)
    for step in (1, 2, 4):
        here = (place & step) == 0
        parts = [
            jnp.where(here, a, b) + pltpu.roll(jnp.where(here, b, a), 8 - step, 0)
            for a, b in zip(parts[0::2], parts[1::2])
        ]
    return parts[0]


def block_of(blocks):
    return 0 if blocks == 1 else pl.program_id(0)


def project(
    length_ref, center_ref, share_ref, slab_ref, gate_ref, weight_ref, out_gate_ref, left_ref, gates_ref, norm_ref,
    half_rows, blocks,
):
    slabs, depth, width = slab_ref.shape
    k_step = block_of(blocks)
    half_cols = depth * blocks
    half = jnp.asarray(0.5, BF16)
    both = jnp.concatenate([gate_ref[...] * half, weight_ref[...] * half], axis=1)
    first_k = lax.axis_index("col") * half_cols + k_step * depth
    live = first_k + lax.broadcasted_iota(jnp.int32, (depth, width), 0) < length_ref[0]
    first_j = lax.rem(lax.axis_index("row") * (2 * half_rows), half_cols)
    start = lax.rem(first_j, depth)

    def quad(q):
        s = q * QUAD
        x = slab_ref[pl.ds(s, QUAD)].reshape(2, 2 * depth, width)
        n = normed(x[0], x[1], center_ref[...], share_ref[...])
        for part in range(2):
            own = n[:, part * width : (part + 1) * width]
            edge = gated(own, both)
            for r in range(2):
                here = slice(r * depth, (r + 1) * depth)
                left_ref[s + 2 * part + r] = jnp.where(live, edge[here], 0.0).astype(BF16).astype(left_ref.dtype)
                norm_ref[2 * part + r, pl.ds(0, depth), :] = own[here].astype(F32)

        def gates():
            rows = jnp.concatenate([norm_ref[n, pl.ds(start, GATE_ROWS), :] for n in range(QUAD)], axis=0)
            y = jnp.dot(rows.astype(BF16), out_gate_ref[...] * half, preferred_element_type=F32)
            gate = (0.5 + 0.5 * jnp.tanh(y)).astype(BF16).astype(F32)
            gates_ref[pl.ds(pl.multiple_of(s * GATE_ROWS, 8), QUAD * GATE_ROWS), :] = gate

        if blocks == 1:
            gates()
        else:
            pl.when(k_step == first_j // depth)(gates)

    if slabs == QUAD:
        quad(0)
    else:
        pl.loop(0, slabs // QUAD)(quad)


def contract(length_ref, left_ref, right_ref, j_half, sums_ref, blocks):
    slabs, depth, _ = left_ref.shape
    rows = right_ref.shape[0] // 2
    group = divisor(rows, 6, 2)
    live_rows = length_ref[0] - lax.axis_index("row") * (2 * rows)
    second = lax.broadcasted_iota(jnp.int32, (8, left_ref.shape[2]), 0) // QUAD

    def tile(turn, _):
        q = turn // (rows // group)
        j0 = lax.rem(turn, rows // group) * group
        first = j_half * rows + j0
        sums = [[None] * QUAD for _ in range(group)]
        for k0 in range(0, depth, 16):
            edges = [right_ref[first + j, pl.ds(k0, 16), :].astype(F32) for j in range(group)]
            for n in range(QUAD):
                left = left_ref[q * QUAD + n, pl.ds(k0, 16), :].astype(F32)
                for j in range(group):
                    term = left * edges[j]
                    term = term[:8] + term[8:]
                    sums[j][n] = term if k0 == 0 else sums[j][n] + term
        for j in range(0, group, 2):
            dest = sums_ref.at[q, pl.ds(pl.multiple_of((j0 + j) * QUAD, 8), 8), :]
            total = jnp.where(first + j + second < live_rows, fold(sums[j] + sums[j + 1]), 0.0)
            dest[...] = total if blocks == 1 else jnp.where(block_of(blocks) == 0, total, total + dest[...])
        return 0

    lax.fori_loop(0, slabs // QUAD * (rows // group), tile, 0)


def assemble(dest_ref, sums_ref, gates_ref, places, j_half):
    half_rows = sums_ref.shape[1] // QUAD
    count = dest_ref.shape[1] // half_rows
    side, place = lax.axis_index("col"), lax.axis_index("row")
    for n, (m0, m1) in enumerate(zip(*places)):
        i = jnp.bitwise_xor(place, jnp.where(side == 0, m0, m1))
        rows = pl.ds(i, half_rows, stride=count)
        dest_ref[0, rows, :] = sums_ref[n // QUAD, pl.ds(n % QUAD, half_rows, stride=QUAD), :]
        dest_ref[1, rows, :] = gates_ref[pl.ds(n * GATE_ROWS + j_half * half_rows, half_rows), :]


def near_kernel(
    length_ref, center_ref, share_ref, right_ref, slab_ref, gate_ref, weight_ref, out_gate_ref,
    sums_ref, gates_ref, left_ref, norm_ref, *, blocks,
):
    project(
        length_ref, center_ref, share_ref, slab_ref, gate_ref, weight_ref, out_gate_ref,
        left_ref, gates_ref, norm_ref, right_ref.shape[0] // 2, blocks,
    )
    contract(length_ref, left_ref, right_ref, 1 - lax.axis_index("col"), sums_ref, blocks)


def send_kernel(
    length_ref, center_ref, share_ref, right_ref, slab_ref, gate_ref, weight_ref, out_gate_ref, near_sums_ref, near_gates_ref,
    send_ref, left_ref, gates_ref, sums_ref, norm_ref, *, blocks, near_places, far_places,
):
    flip = 1 - lax.axis_index("col")

    def at_end(body):
        if blocks == 1:
            body()
        else:
            pl.when(pl.program_id(0) == blocks - 1)(body)

    at_end(lambda: assemble(send_ref, near_sums_ref, near_gates_ref, near_places, flip))
    project(
        length_ref, center_ref, share_ref, slab_ref, gate_ref, weight_ref, out_gate_ref,
        left_ref, gates_ref, norm_ref, right_ref.shape[0] // 2, blocks,
    )
    contract(length_ref, left_ref, right_ref, flip, sums_ref, blocks)

    at_end(lambda: assemble(send_ref, sums_ref, gates_ref, far_places, flip))


def keep_kernel(
    length_ref, right_ref, near_left_ref, far_left_ref, near_gates_ref, far_gates_ref,
    keep_ref, near_sums_ref, far_sums_ref, *, blocks, near_places, far_places,
):
    side = lax.axis_index("col")
    contract(length_ref, near_left_ref, right_ref, side, near_sums_ref, blocks)
    contract(length_ref, far_left_ref, right_ref, side, far_sums_ref, blocks)

    def rest():
        assemble(keep_ref, near_sums_ref, near_gates_ref, near_places, side)
        assemble(keep_ref, far_sums_ref, far_gates_ref, far_places, side)

    if blocks == 1:
        rest()
    else:
        pl.when(pl.program_id(0) == blocks - 1)(rest)


def last_kernel(keep_ref, got_ref, weight_ref, out_ref, *, half_cols):
    rows_dev = 2 * out_ref.shape[0]
    tri = keep_ref[0] + got_ref[0]
    d = tri - jnp.mean(tri, axis=-1, keepdims=True)
    var = jnp.mean(d * d, axis=-1, keepdims=True)
    n = (d * lax.rsqrt(var + EPS)).astype(BF16)
    projected = jnp.dot(n, weight_ref[...], preferred_element_type=F32)
    mine = lax.axis_index("row") * rows_dev // half_cols == lax.axis_index("col")
    update = projected * jnp.where(mine, keep_ref[1], got_ref[1])
    out_ref[...] = update.astype(BF16).reshape(out_ref.shape)


def passed(x, to):
    count = lax.axis_size("row")
    pairs = []
    for row in range(count):
        for core in range(2):
            if (target := to(row, core)) is not None:
                pairs.append((row * 2 + core, target[0] * 2 + target[1]))
    return lax.ppermute(x, ("row", "col"), pairs)


def doubled(half, count, between):
    steps = doubling(count)
    held, got = half, None
    for step in range(len(steps[0])):
        if step > 0:
            held = jnp.concatenate([held, got], axis=0)
        if step == 1:
            held, made = between(held)
        got = passed(held, lambda row, core: (row ^ steps[core][step], core))
    near = [slots(s[:-1]) for s in steps]
    far = [[m ^ s[-1] for m in held_by] for held_by, s in zip(near, steps)]
    return held, got, near, far, made


def direct(slab, slab_late, half, between):
    half_cols = half.shape[1]
    side = lax.axis_index("col")

    def out(x, *m):
        return passed(x, lambda row, core: (row ^ m[core], core))

    def part(x, which):
        return lax.dynamic_slice_in_dim(x, which * half_cols, half_cols, 1)

    first, second, third = [out(slab, *m) for m in ((4, 7), (3, 6), (5, 2))]
    beside = out(slab_late, 1, 1)
    over = jnp.concatenate([part(x, 1 - side) for x in (first, second, third)], axis=0)
    over, made = between(over)
    over = passed(over, lambda row, core: (row, 1 - core))
    near = jnp.concatenate([half, part(beside, side), part(first, side), part(second, side)], axis=0)
    far = jnp.concatenate([part(third, side), over], axis=0)
    return near, far, [[0, 1, 4, 3], [0, 1, 7, 6]], [[5, 7, 6, 2], [2, 4, 3, 5]], made


def shards(pair_rep, slab_rep, length, weight_a, gate_a, weight_b, gate_b, weight_gate, weight_out):
    rows_dev, half_cols, width = pair_rep.shape
    hidden = weight_a.shape[1]
    count = lax.axis_size("row")
    side = lax.axis_index("col")
    half_rows = rows_dev // 2
    depth = divisor(half_cols, 144, rows_dev)
    blocks = half_cols // depth
    grid = () if blocks == 1 else (blocks,)
    near = count // 2
    smem = pl.BlockSpec(memory_space=pltpu.SMEM)
    vmem = pl.BlockSpec(memory_space=pltpu.VMEM)
    params = pltpu.CompilerParams(vmem_limit_bytes=40 << 20)

    def whole(*shape):
        return vmem if blocks == 1 else pl.BlockSpec(shape, lambda *_: (0,) * len(shape))

    def deep(rows):
        return vmem if blocks == 1 else pl.BlockSpec((rows, depth, width), lambda k: (0, k, 0))

    square = jax.ShapeDtypeStruct((2 * width, 2 * width), BF16)
    center, share = pl.pallas_call(
        centering_kernel,
        out_shape=(square, square),
        out_specs=(vmem, vmem),
        compiler_params=pltpu.CompilerParams(vmem_limit_bytes=8 << 20),
        cost_estimate=pl.CostEstimate(flops=4 * 10**9, bytes_accessed=8 * 10**6, transcendentals=0),
        name="centering",
    )()
    slab_late, center, share = lax.optimization_barrier((slab_rep, center, share))

    chunk = divisor(rows_dev, max(2, 2592 // half_cols), 2)
    right_call = pl.pallas_call(
        functools.partial(right_kernel, chunk=chunk),
        out_shape=jax.ShapeDtypeStruct((rows_dev, half_cols, hidden), BF16),
        in_specs=[vmem] * 5,
        out_specs=vmem,
        compiler_params=params,
        cost_estimate=pl.CostEstimate(
            flops=2 * rows_dev * half_cols * width * hidden * 6,
            bytes_accessed=4 * rows_dev * half_cols * width,
            transcendentals=2 * rows_dev * half_cols * width,
        ),
        name="right",
    )

    def between(held):
        made, held = lax.optimization_barrier((right_call(center, share, weight_b, gate_b, pair_rep), held))
        return held, made

    half = lax.dynamic_slice_in_dim(slab_late, side * half_cols, half_cols, 1)
    gather = functools.partial(direct, slab_rep, slab_late) if count == 8 else functools.partial(doubled, count=count)
    near_slabs, far_slabs, near_places, far_places, right = gather(half, between=between)

    sums = jax.ShapeDtypeStruct((near // QUAD, half_rows * QUAD, hidden), F32)
    gates = jax.ShapeDtypeStruct((near * GATE_ROWS, width), F32)
    swapped = jax.ShapeDtypeStruct((2, half_rows * count, hidden), F32)
    norm = pltpu.VMEM((QUAD, depth + GATE_ROWS, width), F32)
    cost = pl.CostEstimate(
        flops=2 * rows_dev * half_cols * near * hidden,
        bytes_accessed=2 * rows_dev * half_cols * width,
        transcendentals=near * half_cols * width,
    )
    squares = [whole(*square.shape)] * 2
    weights = [whole(width, hidden), whole(width, hidden), whole(width, width)]

    left_shape = jax.ShapeDtypeStruct((near, half_cols, hidden), F32 if blocks == 1 else BF16)
    near_sums, near_gates, near_left = pl.pallas_call(
        functools.partial(near_kernel, blocks=blocks),
        out_shape=(sums, gates, left_shape),
        grid=grid,
        in_specs=[smem] + squares + [deep(rows_dev), deep(near)] + weights,
        out_specs=(whole(*sums.shape), whole(*gates.shape), deep(near)),
        scratch_shapes=[norm],
        compiler_params=params,
        cost_estimate=cost,
        name="near",
    )(length, center, share, right, near_slabs, gate_a, weight_a, weight_gate)

    send, far_left, far_gates = pl.pallas_call(
        functools.partial(send_kernel, blocks=blocks, near_places=near_places, far_places=far_places),
        out_shape=(swapped, left_shape, gates),
        grid=grid,
        in_specs=[smem] + squares + [deep(rows_dev), deep(near)] + weights + [whole(*sums.shape), whole(*gates.shape)],
        out_specs=(whole(*swapped.shape), deep(near), whole(*gates.shape)),
        scratch_shapes=[pltpu.VMEM(sums.shape, F32), norm],
        compiler_params=params,
        name="send",
    )(length, center, share, right, far_slabs, gate_a, weight_a, weight_gate, near_sums, near_gates)

    swap = passed(send, lambda row, core: (row, 1 - core))

    keep = pl.pallas_call(
        functools.partial(keep_kernel, blocks=blocks, near_places=near_places, far_places=far_places),
        out_shape=swapped,
        grid=grid,
        in_specs=[smem, deep(rows_dev), deep(near), deep(near), whole(*gates.shape), whole(*gates.shape)],
        out_specs=whole(*swapped.shape),
        scratch_shapes=[pltpu.VMEM(sums.shape, F32), pltpu.VMEM(sums.shape, F32)],
        compiler_params=params,
        cost_estimate=cost,
        name="keep",
    )(length, right, near_left, far_left, near_gates, far_gates)

    update = pl.pallas_call(
        functools.partial(last_kernel, half_cols=half_cols),
        out_shape=jax.ShapeDtypeStruct((half_rows, count, width), BF16),
        in_specs=[vmem, vmem, vmem],
        out_specs=vmem,
        compiler_params=pltpu.CompilerParams(vmem_limit_bytes=32 << 20),
        name="last",
    )(keep, swap, weight_out)
    return jnp.transpose(update, (1, 0, 2))


def solution(mesh):
    placed = (
        P(("groups", "row"), "col", None),
        P(("groups", "row"), None, None),
        P("groups"),
        P(),
        P(),
        P(),
        P(),
        P(),
        P(),
    )
    return jax.shard_map(
        shards,
        mesh=mesh,
        in_specs=placed,
        out_specs=P("groups", ("row", "col"), None),
        check_vma=False,
    )
```

```python
import functools

import jax
import jax.numpy as jnp
from jax import lax
from jax.experimental import pallas as pl
from jax.experimental.pallas import tpu as pltpu
from jax.sharding import PartitionSpec as P

EPS = 1e-05
F32 = jnp.float32
BF16 = jnp.bfloat16
QUAD = 4
GATE_ROWS = 40


def divisor(total, limit, step=1):
    return max(d for d in range(step, total + 1, step) if total % d == 0 and (d <= limit or d == step))


def doubling(count):
    bits = [1 << b for b in reversed(range(count.bit_length() - 1))]
    return bits, bits[-1:] + bits[:-1]


def slots(steps):
    held = [0]
    for step in steps:
        held = held + [m ^ step for m in held]
    return held


def centering_kernel(center_ref, share_ref):
    width = center_ref.shape[0] // 2
    row = lax.broadcasted_iota(jnp.int32, (2 * width, 2 * width), 0)
    col = lax.broadcasted_iota(jnp.int32, (2 * width, 2 * width), 1)
    share = jnp.where((row < width) == (col < width), 1.0 / width, 0.0)
    center_ref[...] = (jnp.where(row == col, 1.0, 0.0) - share).astype(BF16)
    share_ref[...] = share.astype(BF16)


def normed(first, second, center, share):
    wide = jnp.concatenate([first, second], axis=1)
    d = jnp.dot(wide, center, preferred_element_type=F32)
    var = jnp.dot((d * d).astype(BF16), share, preferred_element_type=F32)
    return (d * lax.rsqrt(var + EPS)).astype(BF16)


def gated(n, both):
    width = both.shape[1] // 2
    y = jnp.dot(n, both, preferred_element_type=F32)
    value = y[:, width:]
    return value + value * jnp.tanh(y[:, :width])


def right_kernel(center_ref, share_ref, weight_ref, gate_ref, pair_ref, out_ref, *, chunk):
    rows, cols, width = pair_ref.shape
    half = jnp.asarray(0.5, BF16)
    both = jnp.concatenate([gate_ref[...] * half, weight_ref[...] * half], axis=1)

    def some(turn, _):
        j0 = turn * chunk
        x = pair_ref[pl.ds(j0, chunk)].reshape(2, chunk * cols // 2, width)
        n = normed(x[0], x[1], center_ref[...], share_ref[...])
        for part in range(2):
            edge = gated(n[:, part * width : (part + 1) * width], both).astype(BF16)
            out_ref[pl.ds(j0 + part * (chunk // 2), chunk // 2)] = edge.reshape(chunk // 2, cols, width)
        return 0

    lax.fori_loop(0, rows // chunk, some, 0)


def fold(parts):
    place = lax.broadcasted_iota(jnp.int32, parts[0].shape, 0)
    for step in (1, 2, 4):
        here = (place & step) == 0
        parts = [
            jnp.where(here, a, b) + pltpu.roll(jnp.where(here, b, a), 8 - step, 0)
            for a, b in zip(parts[0::2], parts[1::2])
        ]
    return parts[0]


def block_of(blocks):
    return 0 if blocks == 1 else pl.program_id(0)


def project(
    length_ref, center_ref, share_ref, slab_ref, gate_ref, weight_ref, out_gate_ref, left_ref, gates_ref, norm_ref,
    half_rows, blocks,
):
    slabs, depth, width = slab_ref.shape
    k_step = block_of(blocks)
    half_cols = depth * blocks
    half = jnp.asarray(0.5, BF16)
    both = jnp.concatenate([gate_ref[...] * half, weight_ref[...] * half], axis=1)
    first_k = lax.axis_index("col") * half_cols + k_step * depth
    live = first_k + lax.broadcasted_iota(jnp.int32, (depth, width), 0) < length_ref[0]
    first_j = lax.rem(lax.axis_index("row") * (2 * half_rows), half_cols)
    start = lax.rem(first_j, depth)

    def quad(q):
        s = q * QUAD
        x = slab_ref[pl.ds(s, QUAD)].reshape(2, 2 * depth, width)
        n = normed(x[0], x[1], center_ref[...], share_ref[...])
        for part in range(2):
            own = n[:, part * width : (part + 1) * width]
            edge = gated(own, both)
            for r in range(2):
                here = slice(r * depth, (r + 1) * depth)
                left_ref[s + 2 * part + r] = jnp.where(live, edge[here], 0.0).astype(BF16).astype(left_ref.dtype)
                norm_ref[2 * part + r, pl.ds(0, depth), :] = own[here].astype(F32)

        def gates():
            rows = jnp.concatenate([norm_ref[n, pl.ds(start, GATE_ROWS), :] for n in range(QUAD)], axis=0)
            y = jnp.dot(rows.astype(BF16), out_gate_ref[...] * half, preferred_element_type=F32)
            gate = (0.5 + 0.5 * jnp.tanh(y)).astype(BF16).astype(F32)
            gates_ref[pl.ds(pl.multiple_of(s * GATE_ROWS, 8), QUAD * GATE_ROWS), :] = gate

        if blocks == 1:
            gates()
        else:
            pl.when(k_step == first_j // depth)(gates)

    if slabs == QUAD:
        quad(0)
    else:
        pl.loop(0, slabs // QUAD)(quad)


def contract(length_ref, left_ref, right_ref, j_half, sums_ref, blocks):
    slabs, depth, _ = left_ref.shape
    rows = right_ref.shape[0] // 2
    group = divisor(rows, 6, 2)
    live_rows = length_ref[0] - lax.axis_index("row") * (2 * rows)
    second = lax.broadcasted_iota(jnp.int32, (8, left_ref.shape[2]), 0) // QUAD

    def tile(turn, _):
        q = turn // (rows // group)
        j0 = lax.rem(turn, rows // group) * group
        first = j_half * rows + j0
        sums = [[None] * QUAD for _ in range(group)]
        for k0 in range(0, depth, 16):
            edges = [right_ref[first + j, pl.ds(k0, 16), :].astype(F32) for j in range(group)]
            for n in range(QUAD):
                left = left_ref[q * QUAD + n, pl.ds(k0, 16), :].astype(F32)
                for j in range(group):
                    term = left * edges[j]
                    term = term[:8] + term[8:]
                    sums[j][n] = term if k0 == 0 else sums[j][n] + term
        for j in range(0, group, 2):
            dest = sums_ref.at[q, pl.ds(pl.multiple_of((j0 + j) * QUAD, 8), 8), :]
            total = jnp.where(first + j + second < live_rows, fold(sums[j] + sums[j + 1]), 0.0)
            dest[...] = total if blocks == 1 else jnp.where(block_of(blocks) == 0, total, total + dest[...])
        return 0

    lax.fori_loop(0, slabs // QUAD * (rows // group), tile, 0)


def assemble(dest_ref, sums_ref, gates_ref, places, j_half):
    half_rows = sums_ref.shape[1] // QUAD
    count = dest_ref.shape[1] // half_rows
    side, place = lax.axis_index("col"), lax.axis_index("row")
    for n, (m0, m1) in enumerate(zip(*places)):
        i = jnp.bitwise_xor(place, jnp.where(side == 0, m0, m1))
        rows = pl.ds(i, half_rows, stride=count)
        dest_ref[0, rows, :] = sums_ref[n // QUAD, pl.ds(n % QUAD, half_rows, stride=QUAD), :]
        dest_ref[1, rows, :] = gates_ref[pl.ds(n * GATE_ROWS + j_half * half_rows, half_rows), :]


def near_kernel(
    length_ref, center_ref, share_ref, right_ref, slab_ref, gate_ref, weight_ref, out_gate_ref,
    sums_ref, gates_ref, left_ref, norm_ref, *, blocks,
):
    project(
        length_ref, center_ref, share_ref, slab_ref, gate_ref, weight_ref, out_gate_ref,
        left_ref, gates_ref, norm_ref, right_ref.shape[0] // 2, blocks,
    )
    contract(length_ref, left_ref, right_ref, 1 - lax.axis_index("col"), sums_ref, blocks)


def send_kernel(
    length_ref, center_ref, share_ref, right_ref, slab_ref, gate_ref, weight_ref, out_gate_ref, near_sums_ref, near_gates_ref,
    send_ref, left_ref, gates_ref, wide_ref, sums_ref, norm_ref, *, blocks, near_places, far_places,
):
    flip = 1 - lax.axis_index("col")

    def at_end(body):
        if blocks == 1:
            body()
        else:
            pl.when(pl.program_id(0) == blocks - 1)(body)

    at_end(lambda: assemble(wide_ref, near_sums_ref, near_gates_ref, near_places, flip))
    project(
        length_ref, center_ref, share_ref, slab_ref, gate_ref, weight_ref, out_gate_ref,
        left_ref, gates_ref, norm_ref, right_ref.shape[0] // 2, blocks,
    )
    contract(length_ref, left_ref, right_ref, flip, sums_ref, blocks)

    def rest():
        assemble(wide_ref, sums_ref, gates_ref, far_places, flip)
        send_ref[...] = wide_ref[...].astype(BF16)

    at_end(rest)


def keep_kernel(
    length_ref, right_ref, near_left_ref, far_left_ref, near_gates_ref, far_gates_ref,
    keep_ref, near_sums_ref, far_sums_ref, *, blocks, near_places, far_places,
):
    side = lax.axis_index("col")
    contract(length_ref, near_left_ref, right_ref, side, near_sums_ref, blocks)
    contract(length_ref, far_left_ref, right_ref, side, far_sums_ref, blocks)

    def rest():
        assemble(keep_ref, near_sums_ref, near_gates_ref, near_places, side)
        assemble(keep_ref, far_sums_ref, far_gates_ref, far_places, side)

    if blocks == 1:
        rest()
    else:
        pl.when(pl.program_id(0) == blocks - 1)(rest)


def last_kernel(keep_ref, got_ref, weight_ref, out_ref, *, half_cols):
    rows_dev = 2 * out_ref.shape[0]
    tri = keep_ref[0] + got_ref[0].astype(F32)
    d = tri - jnp.mean(tri, axis=-1, keepdims=True)
    var = jnp.mean(d * d, axis=-1, keepdims=True)
    n = (d * lax.rsqrt(var + EPS)).astype(BF16)
    projected = jnp.dot(n, weight_ref[...], preferred_element_type=F32)
    mine = lax.axis_index("row") * rows_dev // half_cols == lax.axis_index("col")
    update = projected * jnp.where(mine, keep_ref[1], got_ref[1].astype(F32))
    out_ref[...] = update.astype(BF16).reshape(out_ref.shape)


def passed(x, to):
    count = lax.axis_size("row")
    pairs = []
    for row in range(count):
        for core in range(2):
            if (target := to(row, core)) is not None:
                pairs.append((row * 2 + core, target[0] * 2 + target[1]))
    return lax.ppermute(x, ("row", "col"), pairs)


def doubled(half, count, between):
    steps = doubling(count)
    held, got = half, None
    for step in range(len(steps[0])):
        if step > 0:
            held = jnp.concatenate([held, got], axis=0)
        if step == 1:
            held, made = between(held)
        got = passed(held, lambda row, core: (row ^ steps[core][step], core))
    near = [slots(s[:-1]) for s in steps]
    far = [[m ^ s[-1] for m in held_by] for held_by, s in zip(near, steps)]
    return held, got, near, far, made


def direct(slab, slab_late, half, between):
    half_cols = half.shape[1]
    side = lax.axis_index("col")

    def out(x, *m):
        return passed(x, lambda row, core: (row ^ m[core], core))

    def part(x, which):
        return lax.dynamic_slice_in_dim(x, which * half_cols, half_cols, 1)

    first, second, third = [out(slab, *m) for m in ((5, 4), (2, 3), (6, 7))]
    beside = out(slab_late, 1, 1)
    over = jnp.concatenate([part(x, 1 - side) for x in (first, second, third)], axis=0)
    over, made = between(over)
    over = passed(over, lambda row, core: (row, 1 - core))
    near = jnp.concatenate([half, part(beside, side), part(first, side), part(second, side)], axis=0)
    far = jnp.concatenate([part(third, side), over], axis=0)
    return near, far, [[0, 1, 5, 2], [0, 1, 4, 3]], [[6, 4, 3, 7], [7, 5, 2, 6]], made


def shards(pair_rep, slab_rep, length, weight_a, gate_a, weight_b, gate_b, weight_gate, weight_out):
    rows_dev, half_cols, width = pair_rep.shape
    hidden = weight_a.shape[1]
    count = lax.axis_size("row")
    side = lax.axis_index("col")
    half_rows = rows_dev // 2
    depth = divisor(half_cols, 144, rows_dev)
    blocks = half_cols // depth
    grid = () if blocks == 1 else (blocks,)
    near = count // 2
    smem = pl.BlockSpec(memory_space=pltpu.SMEM)
    vmem = pl.BlockSpec(memory_space=pltpu.VMEM)
    params = pltpu.CompilerParams(vmem_limit_bytes=40 << 20)

    def whole(*shape):
        return vmem if blocks == 1 else pl.BlockSpec(shape, lambda *_: (0,) * len(shape))

    def deep(rows):
        return vmem if blocks == 1 else pl.BlockSpec((rows, depth, width), lambda k: (0, k, 0))

    square = jax.ShapeDtypeStruct((2 * width, 2 * width), BF16)
    center, share = pl.pallas_call(
        centering_kernel,
        out_shape=(square, square),
        out_specs=(vmem, vmem),
        compiler_params=pltpu.CompilerParams(vmem_limit_bytes=8 << 20),
        cost_estimate=pl.CostEstimate(flops=4 * 10**9, bytes_accessed=8 * 10**6, transcendentals=0),
        name="centering",
    )()
    slab_late, center, share = lax.optimization_barrier((slab_rep, center, share))

    chunk = divisor(rows_dev, max(2, 2592 // half_cols), 2)
    right_call = pl.pallas_call(
        functools.partial(right_kernel, chunk=chunk),
        out_shape=jax.ShapeDtypeStruct((rows_dev, half_cols, hidden), BF16),
        in_specs=[vmem] * 5,
        out_specs=vmem,
        compiler_params=params,
        cost_estimate=pl.CostEstimate(
            flops=2 * rows_dev * half_cols * width * hidden * 6,
            bytes_accessed=4 * rows_dev * half_cols * width,
            transcendentals=2 * rows_dev * half_cols * width,
        ),
        name="right",
    )

    def between(held):
        made, held = lax.optimization_barrier((right_call(center, share, weight_b, gate_b, pair_rep), held))
        return held, made

    half = lax.dynamic_slice_in_dim(slab_late, side * half_cols, half_cols, 1)
    gather = functools.partial(direct, slab_rep, slab_late) if count == 8 else functools.partial(doubled, count=count)
    near_slabs, far_slabs, near_places, far_places, right = gather(half, between=between)

    sums = jax.ShapeDtypeStruct((near // QUAD, half_rows * QUAD, hidden), F32)
    gates = jax.ShapeDtypeStruct((near * GATE_ROWS, width), F32)
    swapped = jax.ShapeDtypeStruct((2, half_rows * count, hidden), F32)
    norm = pltpu.VMEM((QUAD, depth + GATE_ROWS, width), F32)
    cost = pl.CostEstimate(
        flops=2 * rows_dev * half_cols * near * hidden,
        bytes_accessed=2 * rows_dev * half_cols * width,
        transcendentals=near * half_cols * width,
    )
    squares = [whole(*square.shape)] * 2
    weights = [whole(width, hidden), whole(width, hidden), whole(width, width)]

    left_shape = jax.ShapeDtypeStruct((near, half_cols, hidden), F32 if blocks == 1 else BF16)
    near_sums, near_gates, near_left = pl.pallas_call(
        functools.partial(near_kernel, blocks=blocks),
        out_shape=(sums, gates, left_shape),
        grid=grid,
        in_specs=[smem] + squares + [deep(rows_dev), deep(near)] + weights,
        out_specs=(whole(*sums.shape), whole(*gates.shape), deep(near)),
        scratch_shapes=[norm],
        compiler_params=params,
        cost_estimate=cost,
        name="near",
    )(length, center, share, right, near_slabs, gate_a, weight_a, weight_gate)

    send, far_left, far_gates = pl.pallas_call(
        functools.partial(send_kernel, blocks=blocks, near_places=near_places, far_places=far_places),
        out_shape=(jax.ShapeDtypeStruct(swapped.shape, BF16), left_shape, gates),
        grid=grid,
        in_specs=[smem] + squares + [deep(rows_dev), deep(near)] + weights + [whole(*sums.shape), whole(*gates.shape)],
        out_specs=(whole(*swapped.shape), deep(near), whole(*gates.shape)),
        scratch_shapes=[pltpu.VMEM(swapped.shape, F32), pltpu.VMEM(sums.shape, F32), norm],
        compiler_params=params,
        name="send",
    )(length, center, share, right, far_slabs, gate_a, weight_a, weight_gate, near_sums, near_gates)

    swap = passed(send, lambda row, core: (row, 1 - core))

    keep = pl.pallas_call(
        functools.partial(keep_kernel, blocks=blocks, near_places=near_places, far_places=far_places),
        out_shape=swapped,
        grid=grid,
        in_specs=[smem, deep(rows_dev), deep(near), deep(near), whole(*gates.shape), whole(*gates.shape)],
        out_specs=whole(*swapped.shape),
        scratch_shapes=[pltpu.VMEM(sums.shape, F32), pltpu.VMEM(sums.shape, F32)],
        compiler_params=params,
        cost_estimate=cost,
        name="keep",
    )(length, right, near_left, far_left, near_gates, far_gates)

    update = pl.pallas_call(
        functools.partial(last_kernel, half_cols=half_cols),
        out_shape=jax.ShapeDtypeStruct((half_rows, count, width), BF16),
        in_specs=[vmem, vmem, vmem],
        out_specs=vmem,
        compiler_params=pltpu.CompilerParams(vmem_limit_bytes=32 << 20),
        name="last",
    )(keep, swap, weight_out)
    return jnp.transpose(update, (1, 0, 2))


def solution(mesh):
    placed = (
        P(("groups", "row"), "col", None),
        P(("groups", "row"), None, None),
        P("groups"),
        P(),
        P(),
        P(),
        P(),
        P(),
        P(),
    )
    return jax.shard_map(
        shards,
        mesh=mesh,
        in_specs=placed,
        out_specs=P("groups", ("row", "col"), None),
        check_vma=False,
    )
```
